32 devices in a mesh: shard: 4 (over z), ctx: 4 (over y, core), tp: 2 (over x).
Axes of the slice: x: 2, y: 2, z: 4, core: 2. Of those that a mesh axis runs over, the one named last changes fastest.
Arguments:
- tokens: bfloat16 [12, 1280, 1024], P('shard', 'ctx'), may hold values from -6 to 6
- cotangent: bfloat16 [12, 1280, 1024], P('shard', 'ctx'), may hold values from -6 to 6
- lengths: int32 [12], P('shard'), may hold values from 257 to 1025, as said below
- ln1_gain: float32 [1024], replicated, may hold values from 0.1 to 1.9
- qkv_weight: bfloat16 [3, 1024, 1024], P(None, 'shard', 'tp'), may hold values from -0.1875 to 0.1875
- attn_gain: float32 [1024], P('tp'), may hold values from 0.1 to 1.9
- proj_weight: bfloat16 [1024, 1024], P('tp', 'shard'), may hold values from -0.1875 to 0.1875
- ln2_gain: float32 [1024], replicated, may hold values from 0.1 to 1.9
- gate_up: bfloat16 [2, 1024, 2730], P(None, 'shard', 'tp'), may hold values from -0.1875 to 0.1875
- ffn_gain: float32 [2730], P('tp'), may hold values from 0.1 to 1.9
- down_weight: bfloat16 [2730, 1024], P('tp', 'shard'), may hold values from -0.109375 to 0.109375
Outputs:
- mixed: bfloat16 [12, 1280, 1024], P('shard', 'ctx')
- grad_tokens: bfloat16 [12, 1280, 1024], P('shard', 'ctx')
- grad_ln1_gain: float32 [1024], replicated
- grad_qkv_weight: float32 [3, 1024, 1024], P(None, 'shard', 'tp')
- grad_attn_gain: float32 [1024], P('tp')
- grad_proj_weight: float32 [1024, 1024], P('tp', 'shard')
- grad_ln2_gain: float32 [1024], replicated
- grad_gate_up: float32 [2, 1024, 2730], P(None, 'shard', 'tp')
- grad_ffn_gain: float32 [2730], P('tp')
- grad_down_weight: float32 [2730, 1024], P('tp', 'shard')
The draws below stay inside these ranges and needn't reach their ends.
Inputs may be any that keep to these rules, and one draw needn't show every extreme that they name: `lengths`: every image has 257 to 1025 valid tokens; in each aligned block of 3 images at least one has exactly 1025.
All inputs are finite; a program needn't handle non-finite values.
Results may differ from the reference program's by a relative error of at most 0.02.
Values may be sent and summed in bfloat16 or wider, within the bound.
No kernel may reach another device: no remote copies, remote signals or barrier semaphores. Data moves between devices by JAX's collectives and lax.ppermute only.
A program may use at most 320 MiB of HBM per device.

```python
import math
import jax
import jax.numpy as jnp
from jax import lax

D = 1024
HEADS = 16
HEAD = 64
FF = 2730
GRID = 32
SEQ = 1280
IMG_DEV = 1
MICRO = 3
IMAGES = 12


def draw_lengths(key, part):
    key = jax.random.fold_in(key, 7)
    longest = 1 + GRID * GRID
    shortest = 1 + GRID * GRID // 4
    block_size = IMG_DEV * MICRO
    first_key, second_key = jax.random.split(key)
    base_lengths = jax.random.randint(first_key, (IMAGES // block_size, block_size), shortest, longest + 1)
    chosen = jax.random.randint(second_key, (IMAGES // block_size, 1), 0, block_size)
    filled = jnp.where(jnp.arange(block_size)[None, :] == chosen, longest, base_lengths)
    return filled.reshape(IMAGES).astype(jnp.int32)


def block_scale(stream_key, extent, cuts, low, largest):
    level, own = 1.0, jax.random.fold_in(stream_key, 6)
    for axis_at, shards_of in cuts:
        draws = jnp.exp(jax.random.uniform(jax.random.fold_in(own, axis_at), (shards_of,), jnp.float32, low / len(cuts), largest / len(cuts)))
        level = level * jnp.repeat(draws, extent[axis_at] // shards_of).reshape([-1 if axis == axis_at else 1 for axis in range(len(extent))])
    return level


def noise(key, shape, spread, reach, cuts=(), held_as=jnp.bfloat16):
    values = jax.random.normal(key, shape, jnp.float32) * spread
    if len(cuts) > 0:
        values = block_scale(key, shape, cuts, -0.22, 0.18) * values
    return jnp.clip(values, min=-reach, max=reach).astype(held_as)


def setup_inputs(seed: int = 0) -> dict:
    seeds = jax.random.split(jax.random.key(seed), 12)
    tokens = noise(seeds[0], (IMAGES, SEQ, D), 1.0, 6.0, ((0, 4), (1, 4)))
    cotangent = noise(seeds[1], (IMAGES, SEQ, D), 1.0, 6.0, ((0, 4), (1, 4)))
    lengths = draw_lengths(jax.random.fold_in(seeds[11], 71), 0)
    ln1_gain = jnp.clip(1.0 + 0.18 * jax.random.normal(seeds[3], (D,), jnp.float32), 0.1, 1.9)
    qkv_weight = noise(seeds[4], (3, D, D), D ** -0.5, 0.1875, ((1, 4), (2, 2)))
    attn_gain = jnp.clip(1.0 + 0.18 * jax.random.normal(seeds[5], (D,), jnp.float32), 0.1, 1.9)
    proj_weight = noise(seeds[6], (D, D), D ** -0.5, 0.1875, ((0, 2), (1, 4)))
    ln2_gain = jnp.clip(1.0 + 0.18 * jax.random.normal(seeds[7], (D,), jnp.float32), 0.1, 1.9)
    gate_up = noise(seeds[8], (2, D, FF), D ** -0.5, 0.1875, ((1, 4), (2, 2)))
    ffn_gain = jnp.clip(1.0 + 0.18 * jax.random.normal(seeds[9], (FF,), jnp.float32), 0.1, 1.9)
    down_weight = noise(seeds[10], (FF, D), FF ** -0.5, 0.109375, ((0, 2), (1, 4)))
    return dict(tokens=tokens, cotangent=cotangent, lengths=lengths, ln1_gain=ln1_gain, qkv_weight=qkv_weight, attn_gain=attn_gain, proj_weight=proj_weight, ln2_gain=ln2_gain, gate_up=gate_up, ffn_gain=ffn_gain, down_weight=down_weight)


@jax.custom_vjp
def low(v):
    return lax.optimization_barrier(v.astype(jnp.bfloat16)).astype(jnp.float32)

@jax.custom_vjp
def low_back(v):
    return v

def low_keep(v):
    return (low(v), None)

def low_pass(kept, grad):
    return (grad,)

def back_keep(v):
    return (v, None)

def back_low(kept, grad):
    return (low(grad),)
low.defvjp(low_keep, low_pass)
low_back.defvjp(back_keep, back_low)
epsilon = 1e-06
HIGHEST = lax.Precision.HIGHEST

def layer_norm(values, gain_vec):
    row_mean = lax.optimization_barrier(jnp.mean(values, axis=-1, keepdims=True))
    centred = values - row_mean
    variance = lax.optimization_barrier(jnp.mean(centred * centred, axis=-1, keepdims=True))
    return centred * lax.rsqrt(variance + epsilon) * gain_vec

def rotary_tables(positions, quarter):
    patch_place = jnp.maximum(positions - 1, 0)
    row_pos = (patch_place // GRID).astype(jnp.float32)
    col_pos = (patch_place % GRID).astype(jnp.float32)
    frequency = jnp.exp(jnp.arange(quarter).astype(jnp.float32) * (-math.log(10000.0) / quarter))
    row_angle = row_pos[:, None] * frequency[None, :]
    col_angle = col_pos[:, None] * frequency[None, :]
    return (jnp.cos(row_angle), jnp.sin(row_angle), jnp.cos(col_angle), jnp.sin(col_angle))

def rotate(values, tables, turn_sign):
    cos_row, sin_row, cos_col, sin_col = tables
    quarter = values.shape[-1] // 4
    row_first = values[..., :quarter]
    row_second = values[..., quarter:2 * quarter]
    col_first = values[..., 2 * quarter:3 * quarter]
    col_second = values[..., 3 * quarter:]
    return jnp.concatenate([row_first * cos_row - turn_sign * row_second * sin_row, row_second * cos_row + turn_sign * row_first * sin_row, col_first * cos_col - turn_sign * col_second * sin_col, col_second * cos_col + turn_sign * col_first * sin_col], axis=-1)

def image_forward(image, length, params):
    ln1_gain, qkv_weight, attn_gain, proj_weight, ln2_gain, gate_up, ffn_gain, down_weight = params
    tables = tuple((table[:, None, :] for table in rotary_tables(jnp.arange(SEQ), HEAD // 4)))
    normed_one = low(layer_norm(image, ln1_gain))
    projected = [jnp.dot(normed_one, qkv_weight[slot_index], precision=HIGHEST).reshape(SEQ, HEADS, HEAD) for slot_index in range(3)]
    queries = low(rotate(low_back(projected[0]), tables, 1.0))
    key_rows = low(rotate(low_back(projected[1]), tables, 1.0))
    value_rows = low(low_back(projected[2]))
    scores = low_back(jnp.einsum('qhd,khd->hqk', queries, key_rows, precision=HIGHEST) * HEAD ** (-0.5))
    key_valid = jnp.arange(SEQ) < length
    scores = jnp.where(key_valid[None, None, :], scores, -1e+30)
    row_max = lax.optimization_barrier(jnp.max(scores, axis=-1, keepdims=True))
    exponent = jnp.exp(scores - row_max)
    attn_probs = low(exponent / lax.optimization_barrier(jnp.sum(exponent, axis=-1, keepdims=True)))
    mixed_heads = jnp.einsum('hqk,khd->qhd', attn_probs, value_rows, precision=HIGHEST).reshape(SEQ, HEADS * HEAD)
    mixed_heads = low_back(mixed_heads)
    normed_attn = low(layer_norm(mixed_heads, attn_gain))
    residual_one = image + low_back(jnp.dot(normed_attn, proj_weight, precision=HIGHEST))
    normed_two = low(layer_norm(residual_one, ln2_gain))
    gate_pre = low_back(jnp.dot(normed_two, gate_up[0], precision=HIGHEST))
    up_pre = low_back(jnp.dot(normed_two, gate_up[1], precision=HIGHEST))
    hidden = jax.nn.silu(gate_pre) * up_pre
    normed_ffn = low(layer_norm(hidden, ffn_gain))
    return residual_one + low_back(jnp.dot(normed_ffn, down_weight, precision=HIGHEST))

def reference(tokens, cotangent, lengths, ln1_gain, qkv_weight, attn_gain, proj_weight, ln2_gain, gate_up, ffn_gain, down_weight):
    params = tuple((table.astype(jnp.float32) for table in (ln1_gain, qkv_weight, attn_gain, proj_weight, ln2_gain, gate_up, ffn_gain, down_weight)))
    start_rows = tokens.astype(jnp.float32)

    def forward(inputs, weights_all):

        def one_image(operand):
            return image_forward(operand[0], operand[1], weights_all)
        return lax.map(jax.checkpoint(one_image), (inputs, lengths))
    result, pullback = jax.vjp(forward, start_rows, params)
    query_valid = (jnp.arange(SEQ)[None, :] < lengths[:, None]).astype(jnp.float32)
    grad_input, grad_params = pullback(cotangent.astype(jnp.float32) * query_valid[:, :, None])
    return (result.astype(jnp.bfloat16), grad_input.astype(jnp.bfloat16), grad_params[0], grad_params[1], grad_params[2], grad_params[3], grad_params[4], grad_params[5], grad_params[6], grad_params[7])
```

```python
import functools
import math

import jax
import jax.numpy as jnp
from jax import lax
from jax.experimental import pallas as pl
from jax.experimental.pallas import tpu as pltpu
from jax.sharding import PartitionSpec as P

HEAD = 64
GRID = 32
LANES = 128
EPS = 1e-06
BF = jnp.bfloat16
F32 = jnp.float32
TAIL = 80


def dot_nn(a, b):
    return lax.dot_general(a, b, (((1,), (0,)), ((), ())), preferred_element_type=F32)


def dot_nt(a, b):
    return lax.dot_general(a, b, (((1,), (1,)), ((), ())), preferred_element_type=F32)


def dot_tn(a, b):
    return lax.dot_general(a, b, (((0,), (0,)), ((), ())), preferred_element_type=F32)


def tiles(width, step=256):
    return [(at, min(step, width - at)) for at in range(0, width, step)]


def pair_perm(size, flip):
    return [(at, at ^ flip) for at in range(size)]


def rope_tables(positions):
    quarter = HEAD // 4
    place = jnp.maximum(positions - 1, 0)
    row_pos = (place // GRID).astype(F32)
    col_pos = (place % GRID).astype(F32)
    frequency = jnp.exp(jnp.arange(quarter).astype(F32) * (-math.log(10000.0) / quarter))
    row_angle = row_pos[:, None] * frequency[None, :]
    col_angle = col_pos[:, None] * frequency[None, :]
    cr, sr, cc, sc = jnp.cos(row_angle), jnp.sin(row_angle), jnp.cos(col_angle), jnp.sin(col_angle)
    zero = jnp.zeros_like(sr)
    cos = jnp.concatenate([cr, cr, cc, cc], axis=1)
    up = jnp.concatenate([-sr, zero, -sc, zero], axis=1)
    down = jnp.concatenate([zero, sr, zero, sc], axis=1)
    return jnp.stack([jnp.concatenate([t, t], axis=1) for t in (cos, up, down)])


def turn(values, tables_ref, sign):
    shift = HEAD // 4
    return values * tables_ref[0] + sign * (
        pltpu.roll(values, LANES - shift, 1) * tables_ref[1]
        + pltpu.roll(values, shift, 1) * tables_ref[2]
    )


def row_norm(values, width):
    mean = jnp.sum(values, axis=1, keepdims=True) * (1.0 / width)
    centred = values - mean
    inv = lax.rsqrt(jnp.sum(centred * centred, axis=1, keepdims=True) * (1.0 / width) + EPS)
    return centred * inv, inv


def row_norm_back(scaled, normed, inv, width):
    first = jnp.sum(scaled, axis=1, keepdims=True) * (1.0 / width)
    second = jnp.sum(scaled * normed, axis=1, keepdims=True) * (1.0 / width)
    return inv * (scaled - first - normed * second)


def valid_rows(values, count):
    rows = lax.broadcasted_iota(jnp.int32, values.shape, 0)
    return jnp.where(rows < count, values, jnp.zeros_like(values))


def qkv_kernel(x_ref, gain_ref, w_ref, rope_ref, h_ref, q_ref, kv_ref):
    x = x_ref[0].astype(F32)
    normed, _ = row_norm(x, x.shape[1])
    h_ref[...] = (normed * gain_ref[...]).astype(BF)
    width = w_ref.shape[2]
    h = h_ref[...]
    for at, size in tiles(width):
        q = dot_nn(h, w_ref[0, :, at : at + size])
        k = dot_nn(h, w_ref[1, :, at : at + size])
        v = dot_nn(h, w_ref[2, :, at : at + size])
        for off in range(0, size, LANES):
            cols = slice(off, off + LANES)
            q_ref[:, at + off : at + off + LANES] = (
                turn(q[:, cols], rope_ref, 1.0) * HEAD ** (-0.5)
            ).astype(BF)
            kv_ref[:, at + off : at + off + LANES] = turn(k[:, cols], rope_ref, 1.0).astype(BF)
        kv_ref[:, width + at : width + at + size] = v.astype(BF)


def split_pair(values):
    lane = lax.broadcasted_iota(jnp.int32, values.shape, 1)
    zero = jnp.zeros_like(values)
    return jnp.concatenate(
        [jnp.where(lane < HEAD, values, zero), jnp.where(lane >= HEAD, values, zero)], axis=0
    )


def join_pair(values):
    rows = values.shape[0] // 2
    lane = lax.broadcasted_iota(jnp.int32, (rows, values.shape[1]), 1)
    return jnp.where(lane < HEAD, values[:rows], values[rows:])


def attend_kernel(n_ref, q_ref, kv0, kv1, kv2, kv3, o_ref, lse_ref, m_s, l_s, acc_s):
    rows, width = q_ref.shape
    for pair in range(width // LANES):
        cols = slice(pair * LANES, (pair + 1) * LANES)
        vcols = slice(width + pair * LANES, width + (pair + 1) * LANES)
        qb = split_pair(q_ref[:, cols])
        m_s[...] = jnp.full(m_s.shape, -1e30, F32)
        l_s[...] = jnp.zeros(l_s.shape, F32)
        acc_s[...] = jnp.zeros(acc_s.shape, F32)

        def step(kv_ref, count, size):
            s = dot_nt(kv_ref[:size, cols], qb)
            key = lax.broadcasted_iota(jnp.int32, s.shape, 0)
            s = jnp.where(key < count, s, -1e30)
            m_old = m_s[...]
            m_new = jnp.maximum(m_old, jnp.max(s, axis=0, keepdims=True))
            scale = jnp.exp(m_old - m_new)
            e = jnp.exp(s - m_new)
            m_s[...] = m_new
            l_s[...] = l_s[...] * scale + jnp.sum(e, axis=0, keepdims=True)
            acc_s[...] = acc_s[...] * scale + dot_tn(kv_ref[:size, vcols], e.astype(BF))

        for at, kv_ref in enumerate((kv0, kv1, kv2, kv3)):
            count = n_ref[at]

            @pl.when(count > TAIL)
            def _():
                step(kv_ref, count, kv_ref.shape[0])

            @pl.when((count > 0) & (count <= TAIL))
            def _():
                step(kv_ref, count, TAIL)

        total = l_s[...]
        out = acc_s[...] * (1.0 / total)
        o_ref[:, cols] = join_pair(out.T).astype(BF)
        lse_ref[pair : pair + 1, :] = m_s[...] + jnp.log(total)


def attend_back_kernel(
    n_ref, q_ref, kv0, kv1, kv2, kv3, o_ref, do_ref, lse_ref, rope_ref, dq_ref, keep_ref, send_ref, dq_s
):
    rows, width = q_ref.shape
    for pair in range(width // LANES):
        cols = slice(pair * LANES, (pair + 1) * LANES)
        vcols = slice(width + pair * LANES, width + (pair + 1) * LANES)
        qb = split_pair(q_ref[:, cols])
        do = do_ref[:, cols]
        dob = split_pair(do)
        prod = split_pair(do.astype(F32) * o_ref[:, cols].astype(F32))
        delta = jnp.sum(prod.T, axis=0, keepdims=True)
        lse = lse_ref[pair : pair + 1, :]
        dq_s[...] = jnp.zeros(dq_s.shape, F32)

        def step(kv_ref, out_ref, slot, count, size):
            k = kv_ref[:size, cols]
            s = dot_nt(k, qb)
            key = lax.broadcasted_iota(jnp.int32, s.shape, 0)
            p = jnp.where(key < count, jnp.exp(s - lse), 0.0)
            dp = dot_nt(kv_ref[:size, vcols], dob)
            ds = (p * (dp - delta)).astype(BF)
            out_ref[slot, :size, vcols] = dot_nn(p.astype(BF), dob).astype(BF)
            out_ref[slot, :size, cols] = dot_nn(ds, qb).astype(BF)
            dq_s[...] += dot_tn(k, ds)
            if size < rows:
                out_ref[slot, size:, vcols] = jnp.zeros((rows - size, LANES), BF)
                out_ref[slot, size:, cols] = jnp.zeros((rows - size, LANES), BF)

        for at, kv_ref in enumerate((kv0, kv1, kv2, kv3)):
            count = n_ref[at]
            out_ref = (keep_ref, send_ref)[at % 2]
            slot = at // 2

            @pl.when(count > TAIL)
            def _():
                step(kv_ref, out_ref, slot, count, kv_ref.shape[0])

            @pl.when((count > 0) & (count <= TAIL))
            def _():
                step(kv_ref, out_ref, slot, count, TAIL)

            @pl.when(count <= 0)
            def _():
                out_ref[slot, :, vcols] = jnp.zeros((rows, LANES), BF)
                out_ref[slot, :, cols] = jnp.zeros((rows, LANES), BF)

        dq = join_pair(dq_s[...].T) * HEAD ** (-0.5)
        dq_ref[:, cols] = turn(dq, rope_ref, -1.0).astype(BF)


def merge_heads(dst, own_ref, other_ref, tp, half):
    dst[:, pl.ds(pl.multiple_of(tp * half, half), half)] = own_ref[...]
    dst[:, pl.ds(pl.multiple_of((1 - tp) * half, half), half)] = other_ref[...]


def middle_kernel(
    sc_ref, x_ref, cot_ref, own_ref, other_ref, again_ref, ln2_ref, fgain_ref, w_ref,
    x1_ref, h2_ref, g_ref, u_ref, dm_ref, a_ref, st_ref,
    pj_s, gw_s, uw_s, dw_s, o_s, a_s, st_s, sem,
):
    width = x_ref.shape[2]
    half = own_ref.shape[1]
    rows = own_ref.shape[0]
    ff = g_ref.shape[1]
    loads = []
    at = 0
    for slot, dst in enumerate((pj_s, gw_s, uw_s, dw_s)):
        loads.append(
            pltpu.make_async_copy(w_ref.at[:, pl.ds(at, dst.shape[1])], dst, sem.at[slot])
        )
        at += dst.shape[1]
    for load in loads:
        load.start()
    tp = sc_ref[1]
    merge_heads(o_s, own_ref, other_ref, tp, half)
    normed, _ = row_norm(o_s[...].astype(F32), width)
    a_s[...] = (normed * again_ref[...]).astype(BF)
    a_ref[...] = a_s[:, pl.ds(pl.multiple_of(tp * half, half), half)]
    loads[0].wait()
    a = a_s[...]
    for at, size in tiles(width):
        x1_ref[:, at : at + size] = x_ref[0, :, at : at + size].astype(F32) + dot_nt(
            a, pj_s[at : at + size, :]
        )
    normed, _ = row_norm(x1_ref[...], width)
    h2_ref[...] = (normed * ln2_ref[...]).astype(BF)
    h2 = h2_ref[...]
    dyb = valid_rows(cot_ref[0], sc_ref[0])
    for load in loads[1:]:
        load.wait()
    sums = [jnp.zeros((rows, LANES), F32) for _ in range(4)]
    for at, size in tiles(ff):
        span = slice(at, at + size)
        g = dot_nn(h2, gw_s[:, span]).astype(BF)
        u = dot_nn(h2, uw_s[:, span]).astype(BF)
        dm = dot_nn(dyb, dw_s[:, span]).astype(BF)
        g_ref[:, span] = g
        u_ref[:, span] = u
        dm_ref[:, span] = dm
        gf = g.astype(F32)
        z = gf * jax.nn.sigmoid(gf) * u.astype(F32)
        e = dm.astype(F32) * fgain_ref[:, span]
        for off in range(0, size, LANES):
            zo = z[:, off : off + LANES]
            eo = e[:, off : off + LANES]
            sums = [sums[0] + zo, sums[1] + zo * zo, sums[2] + eo, sums[3] + eo * zo]
    lane = lax.broadcasted_iota(jnp.int32, (rows, LANES), 1)
    packed = jnp.zeros((rows, LANES), F32)
    for slot, part in enumerate(sums):
        packed = jnp.where(lane == slot, jnp.sum(part, axis=1, keepdims=True), packed)
    st_s[...] = jnp.zeros(st_s.shape, F32)
    st_s[:rows, :] = packed
    st_ref[...] = st_s[...].T[:8, :]


def ffn_kernel(
    sa_ref, sb_ref, g_ref, u_ref, dm_ref, fgain_ref, w_ref,
    m_ref, dg_ref, du_ref, out_ref, dh_ref, dgain_ref,
    gw_s, uw_s, dw_s, st_s, sem, *, total,
):
    rows, ff = g_ref.shape
    width = w_ref.shape[0]
    loads = []
    at = width
    for slot, dst in enumerate((gw_s, uw_s, dw_s)):
        loads.append(
            pltpu.make_async_copy(w_ref.at[:, pl.ds(at, dst.shape[1])], dst, sem.at[slot])
        )
        at += dst.shape[1]
    for load in loads:
        load.start()
    st_s[...] = jnp.zeros(st_s.shape, F32)
    st_s[:8, :] = sa_ref[...] + sb_ref[...]
    st = st_s[...].T[:rows, :]
    lane = lax.broadcasted_iota(jnp.int32, st.shape, 1)

    def column(slot):
        return jnp.sum(jnp.where(lane == slot, st, 0.0), axis=1, keepdims=True) * (1.0 / total)

    mean = column(0)
    inv = lax.rsqrt(jnp.maximum(column(1) - mean * mean, 0.0) + EPS)
    first = column(2)
    second = inv * (column(3) - mean * first)
    for at, size in tiles(ff):
        span = slice(at, at + size)
        g = g_ref[:, span].astype(F32)
        u = u_ref[:, span].astype(F32)
        dm = dm_ref[:, span].astype(F32)
        gain = fgain_ref[:, span]
        sig = jax.nn.sigmoid(g)
        act = g * sig
        normed = (act * u - mean) * inv
        m_ref[:, span] = (normed * gain).astype(BF)
        dgain_ref[:, span] = jnp.sum(dm * normed, axis=0, keepdims=True)
        dz = inv * (dm * gain - first - normed * second)
        dg_ref[:, span] = (dz * u * sig * (1.0 + g * (1.0 - sig))).astype(BF)
        du_ref[:, span] = (dz * act).astype(BF)
    loads[0].wait()
    loads[1].wait()
    dg = dg_ref[...]
    du = du_ref[...]
    for at, size in tiles(width):
        dh_ref[:, at : at + size] = (
            dot_nt(dg, gw_s[at : at + size, :]) + dot_nt(du, uw_s[at : at + size, :])
        ).astype(BF)
    loads[2].wait()
    m = m_ref[...]
    for at, size in tiles(width):
        out_ref[:, at : at + size] = dot_nt(m, dw_s[at : at + size, :]).astype(BF)


def attn_norm_back_kernel(
    sc_ref, dha_ref, dhb_ref, x1_ref, cot_ref, ln2_ref, own_ref, other_ref, again_ref, w_ref,
    dx_ref, dab_ref, do_ref, dln2_ref, dgain_ref,
    pj_s, o_s, e_s, f_s, sem,
):
    width = x1_ref.shape[1]
    half = own_ref.shape[1]
    load = pltpu.make_async_copy(w_ref.at[:, pl.ds(0, width)], pj_s, sem.at[0])
    load.start()
    tp = sc_ref[1]
    dh = dha_ref[...].astype(F32) + dhb_ref[...].astype(F32)
    normed, inv = row_norm(x1_ref[...], width)
    dln2_ref[...] = jnp.sum(dh * normed, axis=0, keepdims=True)
    dy = valid_rows(cot_ref[0].astype(F32), sc_ref[0])
    dx = dy + row_norm_back(dh * ln2_ref[...], normed, inv, width)
    dx_ref[...] = dx
    dab_ref[...] = dx.astype(BF)
    merge_heads(o_s, own_ref, other_ref, tp, half)
    normed, inv = row_norm(o_s[...].astype(F32), width)
    load.wait()
    dab = dab_ref[...]
    for at, size in tiles(width):
        da = dot_nn(dab, pj_s[:, at : at + size])
        e_s[:, at : at + size] = da
    da = e_s[...]
    f_s[...] = jnp.broadcast_to(jnp.sum(da * normed, axis=0, keepdims=True), f_s.shape)
    dgain_ref[...] = f_s[0:1, pl.ds(pl.multiple_of(tp * half, half), half)]
    e_s[...] = row_norm_back(da * again_ref[...], normed, inv, width)
    do_ref[...] = e_s[:, pl.ds(pl.multiple_of(tp * half, half), half)].astype(BF)


def qkv_back_kernel(keep_ref, recv_ref, far_ref, dq_ref, rope_ref, w_ref, dkv_ref, dh_ref):
    rows, half = dq_ref.shape
    total = keep_ref[0].astype(F32) + recv_ref[0].astype(F32) + far_ref[...].astype(F32)
    for at in range(0, half, LANES):
        dkv_ref[:, at : at + LANES] = turn(total[:, at : at + LANES], rope_ref, -1.0).astype(BF)
    dkv_ref[:, half:] = total[:, half:].astype(BF)
    dq = dq_ref[...]
    dk = dkv_ref[:, :half]
    dv = dkv_ref[:, half:]
    for at, size in tiles(w_ref.shape[1]):
        span = slice(at, at + size)
        dh_ref[:, span] = (
            dot_nt(dq, w_ref[0, span, :]) + dot_nt(dk, w_ref[1, span, :]) + dot_nt(dv, w_ref[2, span, :])
        ).astype(BF)


def tokens_back_kernel(da_ref, db_ref, x_ref, gain_ref, dx_ref, *rest):
    out_ref, dgain_ref = rest[-2:]
    width = dx_ref.shape[1]
    dh = da_ref[...].astype(F32) + db_ref[...].astype(F32)
    normed, inv = row_norm(x_ref[0].astype(F32), width)
    dgain_ref[...] = jnp.sum(dh * normed, axis=0, keepdims=True)
    out_ref[0] = (dx_ref[...] + row_norm_back(dh * gain_ref[...], normed, inv, width)).astype(BF)


def mixed_kernel(x1_ref, pa_ref, pb_ref, *rest):
    out_ref = rest[-1]
    out_ref[0] = (x1_ref[...] + (pa_ref[...].astype(F32) + pb_ref[...].astype(F32))).astype(BF)


VMEM = pl.BlockSpec(memory_space=pltpu.VMEM)
SMEM = pl.BlockSpec(memory_space=pltpu.SMEM)
ANY = pl.BlockSpec(memory_space=pl.ANY)


def shape(*dims, dtype=BF):
    return jax.ShapeDtypeStruct(dims, dtype)


def call(kernel, out_shape, in_specs, out_specs, scratch=(), name=None, flops=0, moved=0, aliases=None, mib=48):
    return pl.pallas_call(
        kernel,
        out_shape=out_shape,
        in_specs=in_specs,
        out_specs=out_specs,
        grid=(1,),
        scratch_shapes=list(scratch),
        input_output_aliases=aliases or {},
        name=name,
        cost_estimate=pl.CostEstimate(flops=flops, bytes_accessed=moved, transcendentals=0),
        compiler_params=pltpu.CompilerParams(vmem_limit_bytes=mib << 20),
    )


def whole(*dims):
    return pl.BlockSpec(dims, lambda i: (0,) * len(dims))


def image_of(index, rows, width):
    return pl.BlockSpec((1, rows, width), lambda i: (index, 0, 0))


def local(
    tokens, cotangent, lengths, ln1_gain, qkv_weight, attn_gain, proj_weight, ln2_gain, gate_up, ffn_gain, down_weight
):
    images, rows, width = tokens.shape
    half = attn_gain.shape[0]
    ff = ffn_gain.shape[0]
    ffp = -(-ff // LANES) * LANES
    pad = ffp - ff
    ctx_size = lax.axis_size("ctx")
    tp_size = lax.axis_size("tp")
    ctx = lax.axis_index("ctx")
    tp = lax.axis_index("tp")
    ff_total = ff * tp_size
    both = ("shard", "ctx")
    swap_tp = pair_perm(tp_size, 1)
    swap_near = pair_perm(ctx_size, 1)
    swap_far = pair_perm(ctx_size, 2)

    def swap(value):
        return lax.ppermute(value, "tp", swap_tp)

    def near(value):
        return lax.ppermute(value, "ctx", swap_near)

    def far(value):
        return lax.ppermute(value, "ctx", swap_far)

    def ordered(own, axis):
        other = swap(own)
        low = jnp.where(tp == 0, own, other)
        high = jnp.where(tp == 0, other, own)
        return jnp.concatenate([low, high], axis=axis)

    depth = qkv_weight.shape[1]
    part = depth // ctx_size
    first = ctx * part
    qkv_part = lax.dynamic_slice_in_dim(qkv_weight, first, part, axis=1)
    full_qkv = lax.all_gather(qkv_part, both, axis=1, tiled=True)
    proj_part = lax.dynamic_slice_in_dim(proj_weight, first, part, axis=1).T
    pairs_part = lax.dynamic_slice_in_dim(gate_up, first, part, axis=1)
    down_part = lax.dynamic_slice_in_dim(down_weight, first, part, axis=1).T
    rest_part = jnp.concatenate(
        [
            ordered(proj_part, 1),
            jnp.pad(pairs_part[0], ((0, 0), (0, pad))),
            jnp.pad(pairs_part[1], ((0, 0), (0, pad))),
            jnp.pad(down_part, ((0, 0), (0, pad))),
        ],
        axis=1,
    )
    rest = lax.all_gather(rest_part, both, axis=0, tiled=True)
    rest_width = rest.shape[1]

    ln1 = ln1_gain[None, :]
    ln2 = ln2_gain[None, :]
    again = ordered(attn_gain[None, :], 1)
    fgain = jnp.pad(ffn_gain, (0, pad))[None, :]
    tables = rope_tables(ctx * rows + jnp.arange(rows, dtype=jnp.int32))
    order = ctx ^ jnp.arange(4, dtype=jnp.int32)
    counts = jnp.clip(lengths[:, None] - rows * order[None, :], 0, rows)

    act = whole(rows, width)
    act_half = whole(rows, half)
    act_ff = whole(rows, ffp)
    line = whole(1, width)
    line_ff = whole(1, ffp)
    rope_spec = whole(3, rows, LANES)
    qkv_spec = whole(3, width, half)
    block_mb = rows * width

    st = [dict() for _ in range(images)]
    for i in range(images):
        s = st[i]
        s["n"] = counts[i]
        s["sc"] = jnp.stack([counts[i, 0], tp.astype(jnp.int32)])
        s["h1"], s["q"], s["kv"] = call(
            qkv_kernel,
            (shape(rows, width), shape(rows, half), shape(rows, 2 * half)),
            [image_of(i, rows, width), line, qkv_spec, rope_spec],
            [act, act_half, whole(rows, 2 * half)],
            name="qkv",
            flops=2 * rows * width * 3 * half,
            moved=6 * width * half + 8 * block_mb,
        )(tokens, ln1, full_qkv, tables)
        s["kvc"] = near(s["kv"])
        s["kvf"] = far(s["kv"])
        s["kvx"] = near(s["kvf"])
    for i in range(images):
        s = st[i]
        s["o"], s["lse"] = call(
            attend_kernel,
            (shape(rows, half), shape(8, 2 * rows, dtype=F32)),
            [SMEM, act_half] + [whole(rows, 2 * half)] * 4,
            [act_half, whole(8, 2 * rows)],
            [
                pltpu.VMEM((1, 2 * rows), F32),
                pltpu.VMEM((1, 2 * rows), F32),
                pltpu.VMEM((LANES, 2 * rows), F32),
            ],
            name="attend",
            flops=16 * rows * 4 * rows * half,
            moved=12 * block_mb,
        )(s["n"], s["q"], s["kv"], s["kvc"], s["kvf"], s["kvx"])
        s["ox"] = swap(s["o"])
    for i in range(images):
        s = st[i]
        s["x1"], s["h2"], s["g"], s["u"], s["dm"], s["a"], s["st"] = call(
            middle_kernel,
            (
                shape(rows, width, dtype=F32),
                shape(rows, width),
                shape(rows, ffp),
                shape(rows, ffp),
                shape(rows, ffp),
                shape(rows, half),
                shape(8, 384, dtype=F32),
            ),
            [SMEM, image_of(i, rows, width), image_of(i, rows, width), act_half, act_half, line, line, line_ff, ANY],
            [act, act, act_ff, act_ff, act_ff, act_half, whole(8, 384)],
            [
                pltpu.VMEM((width, width), BF),
                pltpu.VMEM((width, ffp), BF),
                pltpu.VMEM((width, ffp), BF),
                pltpu.VMEM((width, ffp), BF),
                pltpu.VMEM((rows, width), BF),
                pltpu.VMEM((rows, width), BF),
                pltpu.VMEM((384, LANES), F32),
                pltpu.SemaphoreType.DMA((4,)),
            ],
            name="middle",
            flops=2 * rows * width * (width + 3 * ffp),
            moved=2 * width * rest_width + 12 * block_mb + 6 * rows * ffp,
        )(s["sc"], tokens, cotangent, s["o"], s["ox"], again, ln2, fgain, rest)
        s["stx"] = swap(s["st"])
    for i in range(images):
        s = st[i]
        s["m"], s["dg"], s["du"], s["out"], s["dh2"], s["dffn"] = call(
            functools.partial(ffn_kernel, total=ff_total),
            (
                shape(rows, ffp),
                shape(rows, ffp),
                shape(rows, ffp),
                shape(rows, width),
                shape(rows, width),
                shape(1, ffp, dtype=F32),
            ),
            [whole(8, 384), whole(8, 384), act_ff, act_ff, act_ff, line_ff, ANY],
            [act_ff, act_ff, act_ff, act, act, line_ff],
            [
                pltpu.VMEM((width, ffp), BF),
                pltpu.VMEM((width, ffp), BF),
                pltpu.VMEM((width, ffp), BF),
                pltpu.VMEM((LANES, 384), F32),
                pltpu.SemaphoreType.DMA((3,)),
            ],
            name="ffn",
            flops=2 * rows * width * 3 * ffp,
            moved=6 * width * ffp + 12 * rows * ffp + 4 * block_mb,
        )(s["st"], s["stx"], s["g"], s["u"], s["dm"], fgain, rest)
        s["dh2x"] = swap(s["dh2"])
        s["outx"] = swap(s["out"])
    for i in range(images):
        s = st[i]
        s["dx"], s["dab"], s["do"], s["dln2"], s["dattn"] = call(
            attn_norm_back_kernel,
            (
                shape(rows, width, dtype=F32),
                shape(rows, width),
                shape(rows, half),
                shape(1, width, dtype=F32),
                shape(1, half, dtype=F32),
            ),
            [SMEM, act, act, act, image_of(i, rows, width), line, act_half, act_half, line, ANY],
            [act, act, act_half, line, whole(1, half)],
            [
                pltpu.VMEM((width, width), BF),
                pltpu.VMEM((rows, width), BF),
                pltpu.VMEM((rows, width), F32),
                pltpu.VMEM((8, width), F32),
                pltpu.SemaphoreType.DMA((1,)),
            ],
            name="attn_norm_back",
            flops=2 * rows * width * width,
            moved=2 * width * width + 16 * block_mb,
        )(s["sc"], s["dh2"], s["dh2x"], s["x1"], cotangent, ln2, s["o"], s["ox"], again, rest)
        s["dq"], s["keep"], s["send"] = call(
            attend_back_kernel,
            (shape(rows, half), shape(2, rows, 2 * half), shape(2, rows, 2 * half)),
            [SMEM, act_half] + [whole(rows, 2 * half)] * 4 + [act_half, act_half, whole(8, 2 * rows), rope_spec],
            [act_half, whole(2, rows, 2 * half), whole(2, rows, 2 * half)],
            [pltpu.VMEM((LANES, 2 * rows), F32)],
            name="attend_back",
            flops=40 * rows * 4 * rows * half,
            moved=20 * block_mb,
        )(s["n"], s["q"], s["kv"], s["kvc"], s["kvf"], s["kvx"], s["o"], s["do"], s["lse"], tables)
        s["recv"] = near(s["send"])
        s["far"] = far((s["keep"][1].astype(F32) + s["recv"][1].astype(F32)).astype(BF))
    grad_tokens = None
    for i in range(images):
        s = st[i]
        s["dkv"], s["dh1"] = call(
            qkv_back_kernel,
            (shape(rows, 2 * half), shape(rows, width)),
            [
                pl.BlockSpec((1, rows, 2 * half), lambda i: (0, 0, 0)),
                pl.BlockSpec((1, rows, 2 * half), lambda i: (0, 0, 0)),
                whole(rows, 2 * half),
                act_half,
                rope_spec,
                qkv_spec,
            ],
            [whole(rows, 2 * half), act],
            name="qkv_back",
            flops=2 * rows * width * 3 * half,
            moved=6 * width * half + 10 * block_mb,
        )(s["keep"], s["recv"], s["far"], s["dq"], tables, full_qkv)
        s["dh1x"] = swap(s["dh1"])
    for i in range(images):
        s = st[i]
        again_buf = [] if grad_tokens is None else [grad_tokens]
        grad_tokens, s["dln1"] = call(
            tokens_back_kernel,
            (shape(images, rows, width), shape(1, width, dtype=F32)),
            [act, act, image_of(i, rows, width), line, act] + [ANY] * len(again_buf),
            [image_of(i, rows, width), line],
            name="tokens_back",
            moved=12 * block_mb,
            aliases={5: 0} if again_buf else None,
        )(s["dh1"], s["dh1x"], tokens, ln1, s["dx"], *again_buf)
    mixed = None
    for i in range(images):
        s = st[i]
        again_buf = [] if mixed is None else [mixed]
        mixed = call(
            mixed_kernel,
            shape(images, rows, width),
            [act, act, act] + [ANY] * len(again_buf),
            image_of(i, rows, width),
            name="mixed",
            moved=10 * block_mb,
            aliases={3: 0} if again_buf else None,
        )(s["x1"], s["out"], s["outx"], *again_buf)

    def stacked(name):
        return jnp.concatenate([s[name] for s in st], axis=0)

    def weight_grad(lhs, rhs):
        return dot_tn(lhs, rhs).astype(BF)

    query_pos = ctx * rows + jnp.arange(rows, dtype=jnp.int32)
    query_valid = query_pos[None, :] < lengths[:, None]
    dyb = jnp.where(query_valid[:, :, None], cotangent, jnp.zeros_like(cotangent)).reshape(images * rows, width)
    h2 = stacked("h2")
    grads_rest = jnp.concatenate(
        [
            weight_grad(stacked("dab"), stacked("a")),
            weight_grad(h2, stacked("dg")),
            weight_grad(h2, stacked("du")),
            weight_grad(dyb, stacked("m")),
        ],
        axis=1,
    )
    h1 = stacked("h1")
    grads_qkv = jnp.concatenate([weight_grad(h1, stacked("dq")), weight_grad(h1, stacked("dkv"))], axis=1)

    def reduce(value):
        own = lax.psum_scatter(value, both, scatter_dimension=0, tiled=True)
        return lax.all_gather(own, "ctx", axis=0, tiled=True).astype(F32)

    sum_rest = reduce(grads_rest)
    sum_qkv = reduce(grads_qkv)
    grad_proj = sum_rest[:, :half].T
    grad_pairs = jnp.stack(
        [sum_rest[:, half : half + ff], sum_rest[:, half + ffp : half + ffp + ff]]
    )
    grad_down = sum_rest[:, half + 2 * ffp : half + 2 * ffp + ff].T
    grad_qkv = jnp.stack([sum_qkv[:, j * half : (j + 1) * half] for j in range(3)])

    def gain(name):
        return sum(s[name] for s in st)[0]

    gain_ln1, gain_attn, gain_ln2, gain_ffn = lax.psum(
        (gain("dln1"), gain("dattn"), gain("dln2"), gain("dffn")), both
    )
    return (
        mixed,
        grad_tokens,
        gain_ln1,
        grad_qkv,
        gain_attn,
        grad_proj,
        gain_ln2,
        grad_pairs,
        gain_ffn[:ff],
        grad_down,
    )


def solution(mesh):
    tokens = P("shard", "ctx", None)
    matrix = P(None, "shard", "tp")
    flipped = P("tp", "shard")
    return jax.shard_map(
        local,
        mesh=mesh,
        in_specs=(
            tokens, tokens, P("shard"), P(), matrix, P("tp"), flipped, P(), matrix, P("tp"), flipped,
        ),
        out_specs=(tokens, tokens, P(), matrix, P("tp"), flipped, P(), matrix, P("tp"), flipped),
        check_vma=False,
    )
```

```python
import functools
import math

import jax
import jax.numpy as jnp
from jax import lax
from jax.experimental import pallas as pl
from jax.experimental.pallas import tpu as pltpu
from jax.sharding import PartitionSpec as P

HEAD = 64
GRID = 32
LANES = 128
EPS = 1e-06
BF = jnp.bfloat16
F32 = jnp.float32
TAIL = 80


def dot_nn(a, b):
    return lax.dot_general(a, b, (((1,), (0,)), ((), ())), preferred_element_type=F32)


def dot_nt(a, b):
    return lax.dot_general(a, b, (((1,), (1,)), ((), ())), preferred_element_type=F32)


def dot_tn(a, b):
    return lax.dot_general(a, b, (((0,), (0,)), ((), ())), preferred_element_type=F32)


def tiles(width, step=256):
    return [(at, min(step, width - at)) for at in range(0, width, step)]


def pair_perm(size, flip):
    return [(at, at ^ flip) for at in range(size)]


def rope_tables(positions):
    quarter = HEAD // 4
    place = jnp.maximum(positions - 1, 0)
    row_pos = (place // GRID).astype(F32)
    col_pos = (place % GRID).astype(F32)
    frequency = jnp.exp(jnp.arange(quarter).astype(F32) * (-math.log(10000.0) / quarter))
    row_angle = row_pos[:, None] * frequency[None, :]
    col_angle = col_pos[:, None] * frequency[None, :]
    cr, sr, cc, sc = jnp.cos(row_angle), jnp.sin(row_angle), jnp.cos(col_angle), jnp.sin(col_angle)
    zero = jnp.zeros_like(sr)
    cos = jnp.concatenate([cr, cr, cc, cc], axis=1)
    up = jnp.concatenate([-sr, zero, -sc, zero], axis=1)
    down = jnp.concatenate([zero, sr, zero, sc], axis=1)
    return jnp.stack([jnp.concatenate([t, t], axis=1) for t in (cos, up, down)])


def turn(values, tables_ref, sign):
    shift = HEAD // 4
    return values * tables_ref[0] + sign * (
        pltpu.roll(values, LANES - shift, 1) * tables_ref[1]
        + pltpu.roll(values, shift, 1) * tables_ref[2]
    )


def row_norm(values, width):
    mean = jnp.sum(values, axis=1, keepdims=True) * (1.0 / width)
    centred = values - mean
    inv = lax.rsqrt(jnp.sum(centred * centred, axis=1, keepdims=True) * (1.0 / width) + EPS)
    return centred * inv, inv


def row_norm_back(scaled, normed, inv, width):
    first = jnp.sum(scaled, axis=1, keepdims=True) * (1.0 / width)
    second = jnp.sum(scaled * normed, axis=1, keepdims=True) * (1.0 / width)
    return inv * (scaled - first - normed * second)


def valid_rows(values, count):
    rows = lax.broadcasted_iota(jnp.int32, values.shape, 0)
    return jnp.where(rows < count, values, jnp.zeros_like(values))


def qkv_kernel(x_ref, gain_ref, w_ref, rope_ref, h_ref, q_ref, kv_ref):
    x = x_ref[0].astype(F32)
    normed, _ = row_norm(x, x.shape[1])
    h_ref[...] = (normed * gain_ref[...]).astype(BF)
    width = w_ref.shape[2]
    h = h_ref[...]
    for at, size in tiles(width):
        q = dot_nn(h, w_ref[0, :, at : at + size])
        k = dot_nn(h, w_ref[1, :, at : at + size])
        v = dot_nn(h, w_ref[2, :, at : at + size])
        for off in range(0, size, LANES):
            cols = slice(off, off + LANES)
            q_ref[:, at + off : at + off + LANES] = (
                turn(q[:, cols], rope_ref, 1.0) * HEAD ** (-0.5)
            ).astype(BF)
            kv_ref[:, at + off : at + off + LANES] = turn(k[:, cols], rope_ref, 1.0).astype(BF)
        kv_ref[:, width + at : width + at + size] = v.astype(BF)


def split_pair(values):
    lane = lax.broadcasted_iota(jnp.int32, values.shape, 1)
    zero = jnp.zeros_like(values)
    return jnp.concatenate(
        [jnp.where(lane < HEAD, values, zero), jnp.where(lane >= HEAD, values, zero)], axis=0
    )


def join_pair(values):
    rows = values.shape[0] // 2
    lane = lax.broadcasted_iota(jnp.int32, (rows, values.shape[1]), 1)
    return jnp.where(lane < HEAD, values[:rows], values[rows:])


def attend_kernel(n_ref, q_ref, kv0, kv1, kv2, kv3, o_ref, lse_ref, m_s, l_s, acc_s):
    rows, width = q_ref.shape
    for pair in range(width // LANES):
        cols = slice(pair * LANES, (pair + 1) * LANES)
        vcols = slice(width + pair * LANES, width + (pair + 1) * LANES)
        qb = split_pair(q_ref[:, cols])
        m_s[...] = jnp.full(m_s.shape, -1e30, F32)
        l_s[...] = jnp.zeros(l_s.shape, F32)
        acc_s[...] = jnp.zeros(acc_s.shape, F32)

        def step(kv_ref, count, size):
            s = dot_nt(kv_ref[:size, cols], qb)
            key = lax.broadcasted_iota(jnp.int32, s.shape, 0)
            s = jnp.where(key < count, s, -1e30)
            m_old = m_s[...]
            m_new = jnp.maximum(m_old, jnp.max(s, axis=0, keepdims=True))
            scale = jnp.exp(m_old - m_new)
            e = jnp.exp(s - m_new)
            m_s[...] = m_new
            l_s[...] = l_s[...] * scale + jnp.sum(e, axis=0, keepdims=True)
            acc_s[...] = acc_s[...] * scale + dot_tn(kv_ref[:size, vcols], e.astype(BF))

        for at, kv_ref in enumerate((kv0, kv1, kv2, kv3)):
            count = n_ref[at]

            @pl.when(count > TAIL)
            def _():
                step(kv_ref, count, kv_ref.shape[0])

            @pl.when((count > 0) & (count <= TAIL))
            def _():
                step(kv_ref, count, TAIL)

        total = l_s[...]
        out = acc_s[...] * (1.0 / total)
        o_ref[:, cols] = join_pair(out.T).astype(BF)
        lse_ref[pair : pair + 1, :] = m_s[...] + jnp.log(total)


def attend_back_kernel(
    n_ref, q_ref, kv0, kv1, kv2, kv3, o_ref, do_ref, lse_ref, rope_ref, dq_ref, keep_ref, send_ref, dq_s
):
    rows, width = q_ref.shape
    for pair in range(width // LANES):
        cols = slice(pair * LANES, (pair + 1) * LANES)
        vcols = slice(width + pair * LANES, width + (pair + 1) * LANES)
        qb = split_pair(q_ref[:, cols])
        do = do_ref[:, cols]
        dob = split_pair(do)
        prod = split_pair(do.astype(F32) * o_ref[:, cols].astype(F32))
        delta = jnp.sum(prod.T, axis=0, keepdims=True)
        lse = lse_ref[pair : pair + 1, :]
        dq_s[...] = jnp.zeros(dq_s.shape, F32)

        def step(kv_ref, out_ref, slot, count, size):
            k = kv_ref[:size, cols]
            s = dot_nt(k, qb)
            key = lax.broadcasted_iota(jnp.int32, s.shape, 0)
            p = jnp.where(key < count, jnp.exp(s - lse), 0.0)
            dp = dot_nt(kv_ref[:size, vcols], dob)
            ds = (p * (dp - delta)).astype(BF)
            out_ref[slot, :size, vcols] = dot_nn(p.astype(BF), dob).astype(BF)
            out_ref[slot, :size, cols] = dot_nn(ds, qb).astype(BF)
            dq_s[...] += dot_tn(k, ds)
            if size < rows:
                out_ref[slot, size:, vcols] = jnp.zeros((rows - size, LANES), BF)
                out_ref[slot, size:, cols] = jnp.zeros((rows - size, LANES), BF)

        for at, kv_ref in enumerate((kv0, kv1, kv2, kv3)):
            count = n_ref[at]
            out_ref = (keep_ref, send_ref)[at % 2]
            slot = at // 2

            @pl.when(count > TAIL)
            def _():
                step(kv_ref, out_ref, slot, count, kv_ref.shape[0])

            @pl.when((count > 0) & (count <= TAIL))
            def _():
                step(kv_ref, out_ref, slot, count, TAIL)

            @pl.when(count <= 0)
            def _():
                out_ref[slot, :, vcols] = jnp.zeros((rows, LANES), BF)
                out_ref[slot, :, cols] = jnp.zeros((rows, LANES), BF)

        dq = join_pair(dq_s[...].T) * HEAD ** (-0.5)
        dq_ref[:, cols] = turn(dq, rope_ref, -1.0).astype(BF)


def merge_heads(dst, own_ref, other_ref, tp, half):
    dst[:, pl.ds(pl.multiple_of(tp * half, half), half)] = own_ref[...]
    dst[:, pl.ds(pl.multiple_of((1 - tp) * half, half), half)] = other_ref[...]


def middle_kernel(
    sc_ref, x_ref, cot_ref, own_ref0, own_ref1, own_ref2, other_ref0, other_ref1, other_ref2,
    again_ref, ln2_ref, fgain_ref, wp_ref, ws_ref,
    x1_ref, h2_ref, g_ref, u_ref, dm_ref, a_ref, st_ref,
    pj_s, gw_s, uw_s, dw_s, o_s, a_s, st_s, sem,
):
    image = pl.program_id(0)
    width = x_ref.shape[2]
    half = own_ref0.shape[1]
    rows = own_ref0.shape[0]
    ff = g_ref.shape[2]
    loads = [
        pltpu.make_async_copy(ws_ref.at[:, pl.ds(0, width)], pj_s, sem.at[0]),
        pltpu.make_async_copy(wp_ref.at[:, pl.ds(0, ff)], gw_s, sem.at[1]),
        pltpu.make_async_copy(wp_ref.at[:, pl.ds(ff, ff)], uw_s, sem.at[2]),
        pltpu.make_async_copy(ws_ref.at[:, pl.ds(width, ff)], dw_s, sem.at[3]),
    ]

    @pl.when(image == 0)
    def _():
        for load in loads:
            load.start()

    tp = sc_ref[3]
    for at, (own_ref, other_ref) in enumerate(
        ((own_ref0, other_ref0), (own_ref1, other_ref1), (own_ref2, other_ref2))
    ):

        @pl.when(image == at)
        def _():
            merge_heads(o_s, own_ref, other_ref, tp, half)

    normed, _ = row_norm(o_s[...].astype(F32), width)
    a_s[...] = (normed * again_ref[...]).astype(BF)
    a_ref[0] = a_s[:, pl.ds(pl.multiple_of(tp * half, half), half)]

    @pl.when(image == 0)
    def _():
        loads[0].wait()

    a = a_s[...]
    for at, size in tiles(width):
        x1_ref[0, :, at : at + size] = x_ref[0, :, at : at + size].astype(F32) + dot_nt(
            a, pj_s[at : at + size, :]
        )
    normed, _ = row_norm(x1_ref[0], width)
    h2_ref[0] = (normed * ln2_ref[...]).astype(BF)
    h2 = h2_ref[0]
    dyb = valid_rows(cot_ref[0], sc_ref[image])

    @pl.when(image == 0)
    def _():
        for load in loads[1:]:
            load.wait()

    sums = [jnp.zeros((rows, LANES), F32) for _ in range(4)]
    for at, size in tiles(ff):
        span = slice(at, at + size)
        g = dot_nn(h2, gw_s[:, span]).astype(BF)
        u = dot_nn(h2, uw_s[:, span]).astype(BF)
        dm = dot_nn(dyb, dw_s[:, span]).astype(BF)
        g_ref[0, :, span] = g
        u_ref[0, :, span] = u
        dm_ref[0, :, span] = dm
        gf = g.astype(F32)
        z = gf * jax.nn.sigmoid(gf) * u.astype(F32)
        e = dm.astype(F32) * fgain_ref[:, span]
        for off in range(0, size, LANES):
            zo = z[:, off : off + LANES]
            eo = e[:, off : off + LANES]
            sums = [sums[0] + zo, sums[1] + zo * zo, sums[2] + eo, sums[3] + eo * zo]
    lane = lax.broadcasted_iota(jnp.int32, (rows, LANES), 1)
    packed = jnp.zeros((rows, LANES), F32)
    for slot, part in enumerate(sums):
        packed = jnp.where(lane == slot, jnp.sum(part, axis=1, keepdims=True), packed)
    st_s[...] = jnp.zeros(st_s.shape, F32)
    st_s[:rows, :] = packed
    st_ref[0] = st_s[...].T[:8, :]


def ffn_kernel(
    sa_ref, sb_ref, g_ref, u_ref, dm_ref, fgain_ref, wp_ref, ws_ref,
    m_ref, dg_ref, du_ref, out_ref, dh_ref, dgain_ref,
    gw_s, uw_s, dw_s, st_s, sem, *, total,
):
    _, rows, ff = g_ref.shape
    width = wp_ref.shape[0]
    loads = [
        pltpu.make_async_copy(wp_ref.at[:, pl.ds(0, ff)], gw_s, sem.at[0]),
        pltpu.make_async_copy(wp_ref.at[:, pl.ds(ff, ff)], uw_s, sem.at[1]),
        pltpu.make_async_copy(ws_ref.at[:, pl.ds(width, ff)], dw_s, sem.at[2]),
    ]
    for load in loads:
        load.start()
    st_s[...] = jnp.zeros(st_s.shape, F32)
    st_s[:8, :] = sa_ref[0] + sb_ref[0]
    st = st_s[...].T[:rows, :]
    lane = lax.broadcasted_iota(jnp.int32, st.shape, 1)

    def column(slot):
        return jnp.sum(jnp.where(lane == slot, st, 0.0), axis=1, keepdims=True) * (1.0 / total)

    mean = column(0)
    inv = lax.rsqrt(jnp.maximum(column(1) - mean * mean, 0.0) + EPS)
    first = column(2)
    second = inv * (column(3) - mean * first)
    for at, size in tiles(ff):
        span = slice(at, at + size)
        g = g_ref[0, :, span].astype(F32)
        u = u_ref[0, :, span].astype(F32)
        dm = dm_ref[0, :, span].astype(F32)
        gain = fgain_ref[:, span]
        sig = jax.nn.sigmoid(g)
        act = g * sig
        normed = (act * u - mean) * inv
        m_ref[:, span] = (normed * gain).astype(BF)
        dgain_ref[:, span] = jnp.sum(dm * normed, axis=0, keepdims=True)
        dz = inv * (dm * gain - first - normed * second)
        dg_ref[:, span] = (dz * u * sig * (1.0 + g * (1.0 - sig))).astype(BF)
        du_ref[:, span] = (dz * act).astype(BF)
    loads[0].wait()
    loads[1].wait()
    dg = dg_ref[...]
    du = du_ref[...]
    for at, size in tiles(width):
        dh_ref[:, at : at + size] = (
            dot_nt(dg, gw_s[at : at + size, :]) + dot_nt(du, uw_s[at : at + size, :])
        ).astype(BF)
    loads[2].wait()
    m = m_ref[...]
    for at, size in tiles(width):
        out_ref[:, at : at + size] = dot_nt(m, dw_s[at : at + size, :]).astype(BF)


def attn_norm_back_kernel(
    sc_ref, dha_ref, dhb_ref, x1_ref, cot_ref, ln2_ref, own_ref, other_ref, again_ref, w_ref,
    dx_ref, dab_ref, do_ref, dln2_ref, dgain_ref,
    pj_s, o_s, e_s, f_s, sem,
):
    width = x1_ref.shape[2]
    half = own_ref.shape[1]
    load = pltpu.make_async_copy(w_ref.at[:, pl.ds(0, width)], pj_s, sem.at[0])
    load.start()
    tp = sc_ref[1]
    dh = dha_ref[...].astype(F32) + dhb_ref[...].astype(F32)
    normed, inv = row_norm(x1_ref[0], width)
    dln2_ref[...] = jnp.sum(dh * normed, axis=0, keepdims=True)
    dy = valid_rows(cot_ref[0].astype(F32), sc_ref[0])
    dx = dy + row_norm_back(dh * ln2_ref[...], normed, inv, width)
    dx_ref[...] = dx
    dab_ref[...] = dx.astype(BF)
    merge_heads(o_s, own_ref, other_ref, tp, half)
    normed, inv = row_norm(o_s[...].astype(F32), width)
    load.wait()
    dab = dab_ref[...]
    for at, size in tiles(width):
        da = dot_nn(dab, pj_s[:, at : at + size])
        e_s[:, at : at + size] = da
    da = e_s[...]
    f_s[...] = jnp.broadcast_to(jnp.sum(da * normed, axis=0, keepdims=True), f_s.shape)
    dgain_ref[...] = f_s[0:1, pl.ds(pl.multiple_of(tp * half, half), half)]
    e_s[...] = row_norm_back(da * again_ref[...], normed, inv, width)
    do_ref[...] = e_s[:, pl.ds(pl.multiple_of(tp * half, half), half)].astype(BF)


def qkv_back_kernel(keep_ref, recv_ref, far_ref, dq_ref, rope_ref, w_ref, dkv_ref, dh_ref):
    rows, half = dq_ref.shape
    total = keep_ref[0].astype(F32) + recv_ref[0].astype(F32) + far_ref[...].astype(F32)
    for at in range(0, half, LANES):
        dkv_ref[:, at : at + LANES] = turn(total[:, at : at + LANES], rope_ref, -1.0).astype(BF)
    dkv_ref[:, half:] = total[:, half:].astype(BF)
    dq = dq_ref[...]
    dk = dkv_ref[:, :half]
    dv = dkv_ref[:, half:]
    for at, size in tiles(w_ref.shape[1]):
        span = slice(at, at + size)
        dh_ref[:, span] = (
            dot_nt(dq, w_ref[0, span, :]) + dot_nt(dk, w_ref[1, span, :]) + dot_nt(dv, w_ref[2, span, :])
        ).astype(BF)


def tokens_back_kernel(da_ref, db_ref, x_ref, gain_ref, dx_ref, *rest):
    out_ref, dgain_ref = rest[-2:]
    width = dx_ref.shape[1]
    dh = da_ref[...].astype(F32) + db_ref[...].astype(F32)
    normed, inv = row_norm(x_ref[0].astype(F32), width)
    dgain_ref[...] = jnp.sum(dh * normed, axis=0, keepdims=True)
    out_ref[0] = (dx_ref[...] + row_norm_back(dh * gain_ref[...], normed, inv, width)).astype(BF)


def mixed_kernel(x1_ref, pa_ref, pb_ref, *rest):
    out_ref = rest[-1]
    out_ref[0] = (x1_ref[0] + (pa_ref[...].astype(F32) + pb_ref[...].astype(F32))).astype(BF)


def place_kernel(at_ref, *refs, part):
    *pieces, out_ref, sem = refs
    copies = []
    for slot, piece in enumerate(pieces):
        row = pl.multiple_of(at_ref[slot], part)
        copies.append(
            pltpu.make_async_copy(piece, out_ref.at[pl.ds(row, piece.shape[0]), :], sem.at[slot])
        )
    for copy in copies:
        copy.start()
    for copy in copies:
        copy.wait()


def grads_kernel(n_ref, *refs, plan):
    out_ref, flip_s, out_s, sem = refs[-4:]
    refs = list(refs[:-4])

    def take(count):
        mine = refs[:count]
        del refs[:count]
        return mine

    def joined(mine, cols):
        if len(mine) == 1:
            block = mine[0][:, :, cols]
            return block.reshape(block.shape[0] * block.shape[1], block.shape[2])
        return jnp.concatenate([ref[:, cols] for ref in mine], axis=0)

    copies = []
    column = 0
    for group, (masked, left, rights) in enumerate(plan):
        mine = take(left)
        if masked:
            parts = [valid_rows(mine[0][i], n_ref[i]) for i in range(mine[0].shape[0])]
            flip_s[...] = jnp.concatenate(parts, axis=0).T
        else:
            flip_s[...] = joined(mine, slice(None)).T
        flipped = flip_s[...]
        start = column
        for right in rights:
            mine = take(right)
            span = mine[0].shape[-1]
            for at, size in tiles(span):
                out_s[:, column + at : column + at + size] = dot_nn(
                    flipped, joined(mine, slice(at, at + size))
                ).astype(BF)
            column += span
        copies.append(
            pltpu.make_async_copy(
                out_s.at[:, pl.ds(start, column - start)],
                out_ref.at[:, pl.ds(start, column - start)],
                sem.at[group],
            )
        )
        copies[-1].start()
    for copy in copies:
        copy.wait()


VMEM = pl.BlockSpec(memory_space=pltpu.VMEM)
SMEM = pl.BlockSpec(memory_space=pltpu.SMEM)
ANY = pl.BlockSpec(memory_space=pl.ANY)


def shape(*dims, dtype=BF):
    return jax.ShapeDtypeStruct(dims, dtype)


def call(kernel, out_shape, in_specs, out_specs, scratch=(), name=None, flops=0, moved=0, aliases=None, mib=48, grid=1):
    return pl.pallas_call(
        kernel,
        out_shape=out_shape,
        in_specs=in_specs,
        out_specs=out_specs,
        grid=(grid,),
        scratch_shapes=list(scratch),
        input_output_aliases=aliases or {},
        name=name,
        cost_estimate=pl.CostEstimate(flops=flops, bytes_accessed=moved, transcendentals=0),
        compiler_params=pltpu.CompilerParams(vmem_limit_bytes=mib << 20),
    )


def whole(*dims):
    return pl.BlockSpec(dims, lambda i: (0,) * len(dims))


def image_of(index, rows, width):
    return pl.BlockSpec((1, rows, width), lambda i: (index, 0, 0))


def local(
    tokens, cotangent, lengths, ln1_gain, qkv_weight, attn_gain, proj_weight, ln2_gain, gate_up, ffn_gain, down_weight
):
    images, rows, width = tokens.shape
    half = attn_gain.shape[0]
    ff = ffn_gain.shape[0]
    ffp = -(-ff // LANES) * LANES
    pad = ffp - ff
    ctx_size = lax.axis_size("ctx")
    tp_size = lax.axis_size("tp")
    ctx = lax.axis_index("ctx")
    tp = lax.axis_index("tp")
    ff_total = ff * tp_size
    both = ("shard", "ctx")
    swap_tp = pair_perm(tp_size, 1)
    swap_near = pair_perm(ctx_size, 1)
    swap_far = pair_perm(ctx_size, 2)

    def swap(value):
        return lax.ppermute(value, "tp", swap_tp)

    def near(value):
        return lax.ppermute(value, "ctx", swap_near)

    def far(value):
        return lax.ppermute(value, "ctx", swap_far)

    def ordered(own, axis):
        other = swap(own)
        low = jnp.where(tp == 0, own, other)
        high = jnp.where(tp == 0, other, own)
        return jnp.concatenate([low, high], axis=axis)

    depth = qkv_weight.shape[1]
    part = depth // ctx_size
    first = ctx * part
    qkv_part = lax.dynamic_slice_in_dim(qkv_weight, first, part, axis=1)
    full_qkv = lax.all_gather(qkv_part, both, axis=1, tiled=True)
    pairs_part = lax.dynamic_slice_in_dim(gate_up, first, part, axis=1)
    shards = lax.axis_size("shard")
    shard = lax.axis_index("shard")

    def shift(value, by):
        return lax.ppermute(value, "shard", [(at, (at + by) % shards) for at in range(shards)])

    low_half = ctx % 2
    half_part = 2 * part
    side_part = jnp.concatenate(
        [
            ordered(lax.dynamic_slice_in_dim(proj_weight, low_half * half_part, half_part, axis=1).T, 1),
            jnp.pad(
                lax.dynamic_slice_in_dim(down_weight, low_half * half_part, half_part, axis=1).T,
                ((0, 0), (0, pad)),
            ),
        ],
        axis=1,
    )
    pieces, rows_at = [], []
    for by in range(shards):
        own = side_part if by == 0 else shift(side_part, by)
        base = (shard + shards - by) % shards * depth
        for flip, piece in enumerate((own, near(own))):
            pieces.append(piece)
            rows_at.append(base + (low_half ^ flip) * half_part)
    side = call(
        functools.partial(place_kernel, part=half_part),
        shape(width, width + ffp),
        [SMEM] + [ANY] * len(pieces),
        ANY,
        [pltpu.SemaphoreType.DMA((len(pieces),))],
        name="place",
        moved=4 * width * (width + ffp),
        mib=8,
    )(jnp.stack(rows_at).astype(jnp.int32), *pieces)
    pairs_part = jnp.concatenate(
        [jnp.pad(pairs_part[at], ((0, 0), (0, pad))) for at in range(2)], axis=1
    )
    pairs = lax.all_gather(pairs_part, both, axis=0, tiled=True)

    ln1 = ln1_gain[None, :]
    ln2 = ln2_gain[None, :]
    again = ordered(attn_gain[None, :], 1)
    fgain = jnp.pad(ffn_gain, (0, pad))[None, :]
    tables = rope_tables(ctx * rows + jnp.arange(rows, dtype=jnp.int32))
    order = ctx ^ jnp.arange(4, dtype=jnp.int32)
    counts = jnp.clip(lengths[:, None] - rows * order[None, :], 0, rows)

    act = whole(rows, width)
    act_half = whole(rows, half)
    act_ff = whole(rows, ffp)
    line = whole(1, width)
    line_ff = whole(1, ffp)
    rope_spec = whole(3, rows, LANES)
    qkv_spec = whole(3, width, half)
    block_mb = rows * width

    st = [dict() for _ in range(images)]
    for i in range(images):
        s = st[i]
        s["n"] = counts[i]
        s["sc"] = jnp.stack([counts[i, 0], tp.astype(jnp.int32)])
        s["h1"], s["q"], s["kv"] = call(
            qkv_kernel,
            (shape(rows, width), shape(rows, half), shape(rows, 2 * half)),
            [image_of(i, rows, width), line, qkv_spec, rope_spec],
            [act, act_half, whole(rows, 2 * half)],
            name="qkv",
            mib=24,
            flops=2 * rows * width * 3 * half,
            moved=6 * width * half + 8 * block_mb,
        )(tokens, ln1, full_qkv, tables)
        s["kvc"] = near(s["kv"])
        s["kvf"] = far(s["kv"])
        s["kvx"] = near(s["kvf"])
    for i in range(images):
        s = st[i]
        s["o"], s["lse"] = call(
            attend_kernel,
            (shape(rows, half), shape(8, 2 * rows, dtype=F32)),
            [SMEM, act_half] + [whole(rows, 2 * half)] * 4,
            [act_half, whole(8, 2 * rows)],
            [
                pltpu.VMEM((1, 2 * rows), F32),
                pltpu.VMEM((1, 2 * rows), F32),
                pltpu.VMEM((LANES, 2 * rows), F32),
            ],
            name="attend",
            mib=24,
            flops=16 * rows * 4 * rows * half,
            moved=12 * block_mb,
        )(s["n"], s["q"], s["kv"], s["kvc"], s["kvf"], s["kvx"])
        s["ox"] = swap(s["o"])
    valid = jnp.concatenate([counts[:, 0], tp.astype(jnp.int32)[None]])

    def each(*dims):
        return pl.BlockSpec((1,) + dims, lambda i: (i,) + (0,) * len(dims))

    x1, h2, gate, up, dm, attn_in, stats = call(
        middle_kernel,
        (
            shape(images, rows, width, dtype=F32),
            shape(images, rows, width),
            shape(images, rows, ffp),
            shape(images, rows, ffp),
            shape(images, rows, ffp),
            shape(images, rows, half),
            shape(images, 8, 384, dtype=F32),
        ),
        [SMEM, each(rows, width), each(rows, width)] + [act_half] * 6 + [line, line, line_ff, ANY, ANY],
        [
            each(rows, width), each(rows, width), each(rows, ffp), each(rows, ffp), each(rows, ffp),
            each(rows, half), each(8, 384),
        ],
        [
            pltpu.VMEM((width, width), BF),
            pltpu.VMEM((width, ffp), BF),
            pltpu.VMEM((width, ffp), BF),
            pltpu.VMEM((width, ffp), BF),
            pltpu.VMEM((rows, width), BF),
            pltpu.VMEM((rows, width), BF),
            pltpu.VMEM((384, LANES), F32),
            pltpu.SemaphoreType.DMA((4,)),
        ],
        name="middle",
        mib=48,
        grid=images,
        flops=2 * images * rows * width * (width + 3 * ffp),
        moved=2 * width * (width + 3 * ffp) + images * (12 * block_mb + 6 * rows * ffp),
    )(valid, tokens, cotangent, *[s["o"] for s in st], *[s["ox"] for s in st], again, ln2, fgain, pairs, side)
    stats_x = swap(stats)
    for i in range(images):
        s = st[i]
        s["m"], s["dg"], s["du"], s["out"], s["dh2"], s["dffn"] = call(
            functools.partial(ffn_kernel, total=ff_total),
            (
                shape(rows, ffp),
                shape(rows, ffp),
                shape(rows, ffp),
                shape(rows, width),
                shape(rows, width),
                shape(1, ffp, dtype=F32),
            ),
            [image_of(i, 8, 384)] * 2 + [image_of(i, rows, ffp)] * 3 + [line_ff, ANY, ANY],
            [act_ff, act_ff, act_ff, act, act, line_ff],
            [
                pltpu.VMEM((width, ffp), BF),
                pltpu.VMEM((width, ffp), BF),
                pltpu.VMEM((width, ffp), BF),
                pltpu.VMEM((LANES, 384), F32),
                pltpu.SemaphoreType.DMA((3,)),
            ],
            name="ffn",
            mib=36,
            flops=2 * rows * width * 3 * ffp,
            moved=6 * width * ffp + 12 * rows * ffp + 4 * block_mb,
        )(stats, stats_x, gate, up, dm, fgain, pairs, side)
        s["dh2x"] = swap(s["dh2"])
        s["outx"] = swap(s["out"])
    def weight_grads(groups, tag):
        plan = [(masked, len(left), [len(right) for right in rights]) for masked, left, rights in groups]
        flat = [v for _, left, rights in groups for v in left + [w for right in rights for w in right]]
        columns = sum(right[0].shape[-1] for _, _, rights in groups for right in rights)
        return call(
            functools.partial(grads_kernel, plan=plan),
            shape(width, columns),
            [SMEM] + [whole(*v.shape) for v in flat],
            ANY,
            [
                pltpu.VMEM((width, images * rows), BF),
                pltpu.VMEM((width, columns), BF),
                pltpu.SemaphoreType.DMA((len(groups),)),
            ],
            name=tag,
            flops=2 * images * rows * width * columns,
            moved=4 * width * columns,
            mib=50 if columns > 2 * width else 36,
        )(counts[:, 0], *flat)

    def of(key):
        return [s[key] for s in st]

    grads_ffn = weight_grads(
        [(False, [h2], [of("dg"), of("du")]), (True, [cotangent], [of("m")])], "grads_ffn"
    )
    for i in range(images):
        s = st[i]
        s["dx"], s["dab"], s["do"], s["dln2"], s["dattn"] = call(
            attn_norm_back_kernel,
            (
                shape(rows, width, dtype=F32),
                shape(rows, width),
                shape(rows, half),
                shape(1, width, dtype=F32),
                shape(1, half, dtype=F32),
            ),
            [SMEM, act, act, image_of(i, rows, width), image_of(i, rows, width), line, act_half, act_half, line, ANY],
            [act, act, act_half, line, whole(1, half)],
            [
                pltpu.VMEM((width, width), BF),
                pltpu.VMEM((rows, width), BF),
                pltpu.VMEM((rows, width), F32),
                pltpu.VMEM((8, width), F32),
                pltpu.SemaphoreType.DMA((1,)),
            ],
            name="attn_norm_back",
            mib=28,
            flops=2 * rows * width * width,
            moved=2 * width * width + 16 * block_mb,
        )(s["sc"], s["dh2"], s["dh2x"], x1, cotangent, ln2, s["o"], s["ox"], again, side)
        if i == 0:
            s["do"], grads_ffn = lax.optimization_barrier((s["do"], grads_ffn))
        else:
            s["do"], st[i - 1]["outx"] = lax.optimization_barrier((s["do"], st[i - 1]["outx"]))
        s["dq"], s["keep"], s["send"] = call(
            attend_back_kernel,
            (shape(rows, half), shape(2, rows, 2 * half), shape(2, rows, 2 * half)),
            [SMEM, act_half] + [whole(rows, 2 * half)] * 4 + [act_half, act_half, whole(8, 2 * rows), rope_spec],
            [act_half, whole(2, rows, 2 * half), whole(2, rows, 2 * half)],
            [pltpu.VMEM((LANES, 2 * rows), F32)],
            name="attend_back",
            mib=28,
            flops=40 * rows * 4 * rows * half,
            moved=20 * block_mb,
        )(s["n"], s["q"], s["kv"], s["kvc"], s["kvf"], s["kvx"], s["o"], s["do"], s["lse"], tables)
        s["recv"] = near(s["send"])
        s["far"] = far((s["keep"][1].astype(F32) + s["recv"][1].astype(F32)).astype(BF))
    mixed = None
    for i in range(images):
        s = st[i]
        again_buf = [] if mixed is None else [mixed]
        mixed = call(
            mixed_kernel,
            shape(images, rows, width),
            [image_of(i, rows, width), act, act] + [ANY] * len(again_buf),
            image_of(i, rows, width),
            name="mixed",
            mib=12,
            moved=10 * block_mb,
            aliases={3: 0} if again_buf else None,
        )(x1, s["out"], s["outx"], *again_buf)
    st[0]["dq"], mixed = lax.optimization_barrier((st[0]["dq"], mixed))
    grad_tokens = None
    for i in range(images):
        s = st[i]
        s["dkv"], s["dh1"] = call(
            qkv_back_kernel,
            (shape(rows, 2 * half), shape(rows, width)),
            [
                pl.BlockSpec((1, rows, 2 * half), lambda i: (0, 0, 0)),
                pl.BlockSpec((1, rows, 2 * half), lambda i: (0, 0, 0)),
                whole(rows, 2 * half),
                act_half,
                rope_spec,
                qkv_spec,
            ],
            [whole(rows, 2 * half), act],
            name="qkv_back",
            mib=24,
            flops=2 * rows * width * 3 * half,
            moved=6 * width * half + 10 * block_mb,
        )(s["keep"], s["recv"], s["far"], s["dq"], tables, full_qkv)
        s["dh1x"] = swap(s["dh1"])
    for i in range(images):
        s = st[i]
        again_buf = [] if grad_tokens is None else [grad_tokens]
        grad_tokens, s["dln1"] = call(
            tokens_back_kernel,
            (shape(images, rows, width), shape(1, width, dtype=F32)),
            [act, act, image_of(i, rows, width), line, act] + [ANY] * len(again_buf),
            [image_of(i, rows, width), line],
            name="tokens_back",
            mib=16,
            moved=12 * block_mb,
            aliases={5: 0} if again_buf else None,
        )(s["dh1"], s["dh1x"], tokens, ln1, s["dx"], *again_buf)
    own_ffn = lax.psum_scatter(grads_ffn, both, scatter_dimension=0, tiled=True)

    def around(own):
        beyond = far(own)
        held = [own, near(own), beyond, near(beyond)]
        return jnp.concatenate([lax.select_n(ctx ^ at, *held) for at in range(4)], axis=0)

    grads_qkv = weight_grads(
        [(False, of("h1"), [of("dq"), of("dkv")]), (False, of("dab"), [[attn_in]])], "grads_qkv"
    )
    grads_qkv, own_ffn = lax.optimization_barrier((grads_qkv, own_ffn))
    own_qkv = lax.psum_scatter(grads_qkv, both, scatter_dimension=0, tiled=True)
    sum_ffn = around(own_ffn).astype(F32)
    own_qkv, grad_tokens, st[0]["dln1"] = lax.optimization_barrier((own_qkv, grad_tokens, st[0]["dln1"]))
    sum_qkv = lax.all_gather(own_qkv, "ctx", axis=0, tiled=True).astype(F32)
    grad_proj = sum_qkv[:, 3 * half :].T
    grad_pairs = jnp.stack([sum_ffn[:, :ff], sum_ffn[:, ffp : ffp + ff]])
    grad_down = sum_ffn[:, 2 * ffp : 2 * ffp + ff].T
    grad_qkv = jnp.stack([sum_qkv[:, j * half : (j + 1) * half] for j in range(3)])

    def everywhere(value):
        step = 1
        while step < ctx_size:
            value = value + lax.ppermute(value, "ctx", pair_perm(ctx_size, step))
            step *= 2
        step = 1
        while step < shards:
            value = value + lax.ppermute(value, "shard", pair_perm(shards, step))
            step *= 2
        return value

    def gain(name):
        return sum(s[name] for s in st)[0]

    packed = everywhere(jnp.concatenate([gain("dffn"), gain("dln2"), gain("dattn")]))
    gain_ffn = packed[:ff]
    gain_ln2 = packed[ffp : ffp + width]
    gain_attn = packed[ffp + width :]
    gain_ln1 = everywhere(gain("dln1"))
    return (
        mixed,
        grad_tokens,
        gain_ln1,
        grad_qkv,
        gain_attn,
        grad_proj,
        gain_ln2,
        grad_pairs,
        gain_ffn,
        grad_down,
    )


def solution(mesh):
    tokens = P("shard", "ctx", None)
    matrix = P(None, "shard", "tp")
    flipped = P("tp", "shard")
    return jax.shard_map(
        local,
        mesh=mesh,
        in_specs=(
            tokens, tokens, P("shard"), P(), matrix, P("tp"), flipped, P(), matrix, P("tp"), flipped,
        ),
        out_specs=(tokens, tokens, P(), matrix, P("tp"), flipped, P(), matrix, P("tp"), flipped),
        check_vma=False,
    )
```

```python
import functools
import math

import jax
import jax.numpy as jnp
from jax import lax
from jax.experimental import pallas as pl
from jax.experimental.pallas import tpu as pltpu
from jax.sharding import PartitionSpec as P

HEAD = 64
GRID = 32
LANES = 128
EPS = 1e-06
BF = jnp.bfloat16
F32 = jnp.float32
TAIL = 80


def dot_nn(a, b):
    return lax.dot_general(a, b, (((1,), (0,)), ((), ())), preferred_element_type=F32)


def dot_nt(a, b):
    return lax.dot_general(a, b, (((1,), (1,)), ((), ())), preferred_element_type=F32)


def dot_tn(a, b):
    return lax.dot_general(a, b, (((0,), (0,)), ((), ())), preferred_element_type=F32)


def tiles(width, step=256):
    return [(at, min(step, width - at)) for at in range(0, width, step)]


def pair_perm(size, flip):
    return [(at, at ^ flip) for at in range(size)]


def rope_tables(positions):
    quarter = HEAD // 4
    place = jnp.maximum(positions - 1, 0)
    row_pos = (place // GRID).astype(F32)
    col_pos = (place % GRID).astype(F32)
    frequency = jnp.exp(jnp.arange(quarter).astype(F32) * (-math.log(10000.0) / quarter))
    row_angle = row_pos[:, None] * frequency[None, :]
    col_angle = col_pos[:, None] * frequency[None, :]
    cr, sr, cc, sc = jnp.cos(row_angle), jnp.sin(row_angle), jnp.cos(col_angle), jnp.sin(col_angle)
    zero = jnp.zeros_like(sr)
    cos = jnp.concatenate([cr, cr, cc, cc], axis=1)
    up = jnp.concatenate([-sr, zero, -sc, zero], axis=1)
    down = jnp.concatenate([zero, sr, zero, sc], axis=1)
    return jnp.stack([jnp.concatenate([t, t], axis=1) for t in (cos, up, down)])


def turn(values, tables_ref, sign):
    shift = HEAD // 4
    return values * tables_ref[0] + sign * (
        pltpu.roll(values, LANES - shift, 1) * tables_ref[1]
        + pltpu.roll(values, shift, 1) * tables_ref[2]
    )


def row_norm(values, width):
    mean = jnp.sum(values, axis=1, keepdims=True) * (1.0 / width)
    centred = values - mean
    inv = lax.rsqrt(jnp.sum(centred * centred, axis=1, keepdims=True) * (1.0 / width) + EPS)
    return centred * inv, inv


def row_norm_back(scaled, normed, inv, width):
    first = jnp.sum(scaled, axis=1, keepdims=True) * (1.0 / width)
    second = jnp.sum(scaled * normed, axis=1, keepdims=True) * (1.0 / width)
    return inv * (scaled - first - normed * second)


def valid_rows(values, count):
    rows = lax.broadcasted_iota(jnp.int32, values.shape, 0)
    return jnp.where(rows < count, values, jnp.zeros_like(values))


def qkv_kernel(x_ref, gain_ref, w_ref, rope_ref, h_ref, q_ref, kv_ref):
    x = x_ref[0].astype(F32)
    normed, _ = row_norm(x, x.shape[1])
    h_ref[...] = (normed * gain_ref[...]).astype(BF)
    width = w_ref.shape[2]
    h = h_ref[...]
    for at, size in tiles(width):
        q = dot_nn(h, w_ref[0, :, at : at + size])
        k = dot_nn(h, w_ref[1, :, at : at + size])
        v = dot_nn(h, w_ref[2, :, at : at + size])
        for off in range(0, size, LANES):
            cols = slice(off, off + LANES)
            q_ref[:, at + off : at + off + LANES] = (
                turn(q[:, cols], rope_ref, 1.0) * HEAD ** (-0.5)
            ).astype(BF)
            pair = 2 * (at + off)
            kv_ref[:, pair : pair + LANES] = turn(k[:, cols], rope_ref, 1.0).astype(BF)
            kv_ref[:, pair + LANES : pair + 2 * LANES] = v[:, cols].astype(BF)


def split_pair(values):
    lane = lax.broadcasted_iota(jnp.int32, values.shape, 1)
    zero = jnp.zeros_like(values)
    return jnp.concatenate(
        [jnp.where(lane < HEAD, values, zero), jnp.where(lane >= HEAD, values, zero)], axis=0
    )


def join_pair(values):
    rows = values.shape[0] // 2
    lane = lax.broadcasted_iota(jnp.int32, (rows, values.shape[1]), 1)
    return jnp.where(lane < HEAD, values[:rows], values[rows:])


def attend_kernel(n_ref, q_ref, kv0, kv1, kv2, kv3, o_ref, lse_ref, m_s, l_s, acc_s):
    qb = split_pair(q_ref[...])
    m_s[...] = jnp.full(m_s.shape, -1e30, F32)
    l_s[...] = jnp.zeros(l_s.shape, F32)
    acc_s[...] = jnp.zeros(acc_s.shape, F32)

    def step(kv_ref, count, size):
        s = dot_nt(kv_ref[:size, :LANES], qb)
        key = lax.broadcasted_iota(jnp.int32, s.shape, 0)
        s = jnp.where(key < count, s, -1e30)
        m_old = m_s[...]
        m_new = jnp.maximum(m_old, jnp.max(s, axis=0, keepdims=True))
        scale = jnp.exp(m_old - m_new)
        e = jnp.exp(s - m_new)
        m_s[...] = m_new
        l_s[...] = l_s[...] * scale + jnp.sum(e, axis=0, keepdims=True)
        acc_s[...] = acc_s[...] * scale + dot_tn(kv_ref[:size, LANES:], e.astype(BF))

    for at, kv_ref in enumerate((kv0, kv1, kv2, kv3)):
        count = n_ref[at]

        @pl.when(count > TAIL)
        def _():
            step(kv_ref, count, kv_ref.shape[0])

        @pl.when((count > 0) & (count <= TAIL))
        def _():
            step(kv_ref, count, TAIL)

    total = l_s[...]
    out = acc_s[...] * (1.0 / total)
    o_ref[...] = join_pair(out.T).astype(BF)
    lse_ref[0] = m_s[...] + jnp.log(total)


def attend_back_kernel(
    n_ref, q_ref, kv0, kv1, kv2, kv3, o_ref, do_ref, lse_ref, rope_ref, dq_ref, keep_ref, send_ref, dq_s
):
    rows = q_ref.shape[0]
    qb = split_pair(q_ref[...])
    do = do_ref[...]
    dob = split_pair(do)
    prod = split_pair(do.astype(F32) * o_ref[...].astype(F32))
    delta = jnp.sum(prod.T, axis=0, keepdims=True)
    lse = lse_ref[0]
    dq_s[...] = jnp.zeros(dq_s.shape, F32)

    def step(kv_ref, out_ref, slot, count, size):
        k = kv_ref[:size, :LANES]
        s = dot_nt(k, qb)
        key = lax.broadcasted_iota(jnp.int32, s.shape, 0)
        p = jnp.where(key < count, jnp.exp(s - lse), 0.0)
        dp = dot_nt(kv_ref[:size, LANES:], dob)
        ds = (p * (dp - delta)).astype(BF)
        out_ref[slot, :size, LANES:] = dot_nn(p.astype(BF), dob).astype(BF)
        out_ref[slot, :size, :LANES] = dot_nn(ds, qb).astype(BF)
        dq_s[...] += dot_tn(k, ds)
        if size < rows:
            out_ref[slot, size:, :] = jnp.zeros((rows - size, 2 * LANES), BF)

    for at, kv_ref in enumerate((kv0, kv1, kv2, kv3)):
        count = n_ref[at]
        out_ref = (keep_ref, send_ref)[at % 2]
        slot = at // 2

        @pl.when(count > TAIL)
        def _():
            step(kv_ref, out_ref, slot, count, kv_ref.shape[0])

        @pl.when((count > 0) & (count <= TAIL))
        def _():
            step(kv_ref, out_ref, slot, count, TAIL)

        @pl.when(count <= 0)
        def _():
            out_ref[slot] = jnp.zeros((rows, 2 * LANES), BF)

    dq = join_pair(dq_s[...].T) * HEAD ** (-0.5)
    dq_ref[...] = turn(dq, rope_ref, -1.0).astype(BF)


def merge_heads(dst, own_ref, other_ref, tp, half):
    dst[:, pl.ds(pl.multiple_of(tp * half, half), half)] = own_ref[...]
    dst[:, pl.ds(pl.multiple_of((1 - tp) * half, half), half)] = other_ref[...]


def middle_kernel(
    sc_ref, x_ref, cot_ref, own_ref0, own_ref1, own_ref2, other_ref0, other_ref1, other_ref2,
    again_ref, ln2_ref, fgain_ref, w_ref,
    x1_ref, h2_ref, g_ref, u_ref, dm_ref, a_ref, st_ref,
    pj_s, gw_s, uw_s, dw_s, o_s, a_s, st_s, sem,
):
    image = pl.program_id(0)
    width = x_ref.shape[2]
    half = own_ref0.shape[1]
    rows = own_ref0.shape[0]
    ff = g_ref.shape[2]
    loads = [
        pltpu.make_async_copy(w_ref.at[:, pl.ds(0, width)], pj_s, sem.at[0]),
        pltpu.make_async_copy(w_ref.at[:, pl.ds(width + ff, ff)], gw_s, sem.at[1]),
        pltpu.make_async_copy(w_ref.at[:, pl.ds(width + 2 * ff, ff)], uw_s, sem.at[2]),
        pltpu.make_async_copy(w_ref.at[:, pl.ds(width, ff)], dw_s, sem.at[3]),
    ]

    @pl.when(image == 0)
    def _():
        for load in loads:
            load.start()

    tp = sc_ref[3]
    for at, (own_ref, other_ref) in enumerate(
        ((own_ref0, other_ref0), (own_ref1, other_ref1), (own_ref2, other_ref2))
    ):

        @pl.when(image == at)
        def _():
            merge_heads(o_s, own_ref, other_ref, tp, half)

    normed, _ = row_norm(o_s[...].astype(F32), width)
    a_s[...] = (normed * again_ref[...]).astype(BF)
    a_ref[0] = a_s[:, pl.ds(pl.multiple_of(tp * half, half), half)]

    @pl.when(image == 0)
    def _():
        loads[0].wait()

    a = a_s[...]
    for at, size in tiles(width):
        x1_ref[0, :, at : at + size] = x_ref[0, :, at : at + size].astype(F32) + dot_nt(
            a, pj_s[at : at + size, :]
        )
    normed, _ = row_norm(x1_ref[0], width)
    h2_ref[0] = (normed * ln2_ref[...]).astype(BF)
    h2 = h2_ref[0]
    dyb = valid_rows(cot_ref[0], sc_ref[image])

    @pl.when(image == 0)
    def _():
        for load in loads[1:]:
            load.wait()

    sums = [jnp.zeros((rows, LANES), F32) for _ in range(4)]
    for at, size in tiles(ff):
        span = slice(at, at + size)
        g = dot_nn(h2, gw_s[:, span]).astype(BF)
        u = dot_nn(h2, uw_s[:, span]).astype(BF)
        dm = dot_nn(dyb, dw_s[:, span]).astype(BF)
        g_ref[0, :, span] = g
        u_ref[0, :, span] = u
        dm_ref[0, :, span] = dm
        gf = g.astype(F32)
        z = gf * jax.nn.sigmoid(gf) * u.astype(F32)
        e = dm.astype(F32) * fgain_ref[:, span]
        for off in range(0, size, LANES):
            zo = z[:, off : off + LANES]
            eo = e[:, off : off + LANES]
            sums = [sums[0] + zo, sums[1] + zo * zo, sums[2] + eo, sums[3] + eo * zo]
    lane = lax.broadcasted_iota(jnp.int32, (rows, LANES), 1)
    packed = jnp.zeros((rows, LANES), F32)
    for slot, part in enumerate(sums):
        packed = jnp.where(lane == slot, jnp.sum(part, axis=1, keepdims=True), packed)
    st_s[...] = jnp.zeros(st_s.shape, F32)
    st_s[:rows, :] = packed
    st_ref[0] = st_s[...].T[:8, :]


def ffn_kernel(
    sa_ref, sb_ref, g_ref, u_ref, dm_ref, fgain_ref, w_ref,
    m_ref, dg_ref, du_ref, out_ref, dh_ref, dgain_ref,
    gw_s, uw_s, dw_s, st_s, sem, *, total,
):
    _, rows, ff = g_ref.shape
    width = w_ref.shape[0]
    loads = [
        pltpu.make_async_copy(w_ref.at[:, pl.ds(width + ff, ff)], gw_s, sem.at[0]),
        pltpu.make_async_copy(w_ref.at[:, pl.ds(width + 2 * ff, ff)], uw_s, sem.at[1]),
        pltpu.make_async_copy(w_ref.at[:, pl.ds(width, ff)], dw_s, sem.at[2]),
    ]
    for load in loads:
        load.start()
    st_s[...] = jnp.zeros(st_s.shape, F32)
    st_s[:8, :] = sa_ref[0] + sb_ref[0]
    st = st_s[...].T[:rows, :]
    lane = lax.broadcasted_iota(jnp.int32, st.shape, 1)

    def column(slot):
        return jnp.sum(jnp.where(lane == slot, st, 0.0), axis=1, keepdims=True) * (1.0 / total)

    mean = column(0)
    inv = lax.rsqrt(jnp.maximum(column(1) - mean * mean, 0.0) + EPS)
    first = column(2)
    second = inv * (column(3) - mean * first)
    for at, size in tiles(ff):
        span = slice(at, at + size)
        g = g_ref[0, :, span].astype(F32)
        u = u_ref[0, :, span].astype(F32)
        dm = dm_ref[0, :, span].astype(F32)
        gain = fgain_ref[:, span]
        sig = jax.nn.sigmoid(g)
        act = g * sig
        normed = (act * u - mean) * inv
        m_ref[:, span] = (normed * gain).astype(BF)
        dgain_ref[:, span] = jnp.sum(dm * normed, axis=0, keepdims=True)
        dz = inv * (dm * gain - first - normed * second)
        dg_ref[:, span] = (dz * u * sig * (1.0 + g * (1.0 - sig))).astype(BF)
        du_ref[:, span] = (dz * act).astype(BF)
    loads[0].wait()
    loads[1].wait()
    dg = dg_ref[...]
    du = du_ref[...]
    for at, size in tiles(width):
        dh_ref[:, at : at + size] = (
            dot_nt(dg, gw_s[at : at + size, :]) + dot_nt(du, uw_s[at : at + size, :])
        ).astype(BF)
    loads[2].wait()
    m = m_ref[...]
    for at, size in tiles(width):
        out_ref[:, at : at + size] = dot_nt(m, dw_s[at : at + size, :]).astype(BF)


def attn_norm_back_kernel(
    sc_ref, dha_ref, dhb_ref, x1_ref, cot_ref, ln2_ref, own_ref, other_ref, again_ref, w_ref,
    dx_ref, dab_ref, do_ref, dln2_ref, dgain_ref,
    pj_s, o_s, e_s, f_s, sem,
):
    width = x1_ref.shape[2]
    half = own_ref.shape[1]
    load = pltpu.make_async_copy(w_ref.at[:, pl.ds(0, width)], pj_s, sem.at[0])
    load.start()
    tp = sc_ref[1]
    dh = dha_ref[...].astype(F32) + dhb_ref[...].astype(F32)
    normed, inv = row_norm(x1_ref[0], width)
    dln2_ref[...] = jnp.sum(dh * normed, axis=0, keepdims=True)
    dy = valid_rows(cot_ref[0].astype(F32), sc_ref[0])
    dx = dy + row_norm_back(dh * ln2_ref[...], normed, inv, width)
    dx_ref[...] = dx
    dab_ref[...] = dx.astype(BF)
    merge_heads(o_s, own_ref, other_ref, tp, half)
    normed, inv = row_norm(o_s[...].astype(F32), width)
    load.wait()
    dab = dab_ref[...]
    for at, size in tiles(width):
        da = dot_nn(dab, pj_s[:, at : at + size])
        e_s[:, at : at + size] = da
    da = e_s[...]
    f_s[...] = jnp.broadcast_to(jnp.sum(da * normed, axis=0, keepdims=True), f_s.shape)
    dgain_ref[...] = f_s[0:1, pl.ds(pl.multiple_of(tp * half, half), half)]
    e_s[...] = row_norm_back(da * again_ref[...], normed, inv, width)
    do_ref[...] = e_s[:, pl.ds(pl.multiple_of(tp * half, half), half)].astype(BF)


def qkv_back_kernel(keep_ref, recv_ref, far_ref, dq_ref, rope_ref, w_ref, dkv_ref, dh_ref):
    rows, half = dq_ref.shape
    total = keep_ref[0].astype(F32) + recv_ref[0].astype(F32) + far_ref[...].astype(F32)
    for at in range(0, half, LANES):
        pair = total[:, 2 * at : 2 * at + 2 * LANES]
        dkv_ref[:, at : at + LANES] = turn(pair[:, :LANES], rope_ref, -1.0).astype(BF)
        dkv_ref[:, half + at : half + at + LANES] = pair[:, LANES:].astype(BF)
    dq = dq_ref[...]
    dk = dkv_ref[:, :half]
    dv = dkv_ref[:, half:]
    for at, size in tiles(w_ref.shape[1]):
        span = slice(at, at + size)
        dh_ref[:, span] = (
            dot_nt(dq, w_ref[0, span, :]) + dot_nt(dk, w_ref[1, span, :]) + dot_nt(dv, w_ref[2, span, :])
        ).astype(BF)


def tokens_back_kernel(da_ref, db_ref, x_ref, gain_ref, dx_ref, *rest):
    out_ref, dgain_ref = rest[-2:]
    width = dx_ref.shape[1]
    dh = da_ref[...].astype(F32) + db_ref[...].astype(F32)
    normed, inv = row_norm(x_ref[0].astype(F32), width)
    dgain_ref[...] = jnp.sum(dh * normed, axis=0, keepdims=True)
    out_ref[0] = (dx_ref[...] + row_norm_back(dh * gain_ref[...], normed, inv, width)).astype(BF)


def mixed_kernel(x1_ref, pa_ref, pb_ref, *rest):
    out_ref = rest[-1]
    out_ref[0] = (x1_ref[0] + (pa_ref[...].astype(F32) + pb_ref[...].astype(F32))).astype(BF)


def finish_kernel(sum_ref, pairs_ref, down_ref):
    ff = down_ref.shape[0]
    ffp = sum_ref.shape[1] // 3
    for at in range(0, ff, LANES):
        size = min(LANES, ff - at)
        for slot in range(3):
            cols = slice(slot * ffp + at, slot * ffp + at + LANES)
            flipped = sum_ref[:, cols].astype(F32).T[:size]
            if slot < 2:
                pairs_ref[at : at + size, slot, :] = flipped
            else:
                down_ref[at : at + size, :] = flipped


def grads_kernel(n_ref, *refs, plan):
    out_ref, flip_s, out_s, sem = refs[-4:]
    refs = list(refs[:-4])

    def take(count):
        mine = refs[:count]
        del refs[:count]
        return mine

    def joined(mine, cols):
        if len(mine) == 1:
            block = mine[0][:, :, cols]
            return block.reshape(block.shape[0] * block.shape[1], block.shape[2])
        return jnp.concatenate([ref[:, cols] for ref in mine], axis=0)

    copies = []
    column = 0
    for group, (masked, left, rights) in enumerate(plan):
        mine = take(left)
        if masked:
            parts = [valid_rows(mine[0][i], n_ref[i]) for i in range(mine[0].shape[0])]
            flip_s[...] = jnp.concatenate(parts, axis=0).T
        else:
            flip_s[...] = joined(mine, slice(None)).T
        flipped = flip_s[...]
        start = column
        for right in rights:
            mine = take(right)
            span = mine[0].shape[-1]
            for at, size in tiles(span):
                out_s[:, column + at : column + at + size] = dot_nn(
                    flipped, joined(mine, slice(at, at + size))
                ).astype(BF)
            column += span
        copies.append(
            pltpu.make_async_copy(
                out_s.at[:, pl.ds(start, column - start)],
                out_ref.at[:, pl.ds(start, column - start)],
                sem.at[group],
            )
        )
        copies[-1].start()
    for copy in copies:
        copy.wait()


VMEM = pl.BlockSpec(memory_space=pltpu.VMEM)
SMEM = pl.BlockSpec(memory_space=pltpu.SMEM)
ANY = pl.BlockSpec(memory_space=pl.ANY)
HBM = pl.BlockSpec(memory_space=pltpu.HBM)


def shape(*dims, dtype=BF):
    return jax.ShapeDtypeStruct(dims, dtype)


def call(kernel, out_shape, in_specs, out_specs, scratch=(), name=None, flops=0, moved=0, aliases=None, mib=48, grid=1):
    return pl.pallas_call(
        kernel,
        out_shape=out_shape,
        in_specs=in_specs,
        out_specs=out_specs,
        grid=(grid,),
        scratch_shapes=list(scratch),
        input_output_aliases=aliases or {},
        name=name,
        cost_estimate=pl.CostEstimate(flops=flops // 16, bytes_accessed=moved // 16, transcendentals=0),
        compiler_params=pltpu.CompilerParams(vmem_limit_bytes=mib << 20),
    )


def whole(*dims):
    return pl.BlockSpec(dims, lambda i: (0,) * len(dims))


def image_of(index, rows, width):
    return pl.BlockSpec((1, rows, width), lambda i: (index, 0, 0))


def in_hbm(value):
    return pltpu.with_memory_space_constraint(value, pltpu.HBM)


def local(
    tokens, cotangent, lengths, ln1_gain, qkv_weight, attn_gain, proj_weight, ln2_gain, gate_up, ffn_gain, down_weight
):
    images, rows, width = tokens.shape
    half = attn_gain.shape[0]
    ff = ffn_gain.shape[0]
    ffp = -(-ff // LANES) * LANES
    pad = ffp - ff
    ctx_size = lax.axis_size("ctx")
    tp_size = lax.axis_size("tp")
    ctx = lax.axis_index("ctx")
    tp = lax.axis_index("tp")
    ff_total = ff * tp_size
    both = ("shard", "ctx")
    swap_tp = pair_perm(tp_size, 1)
    swap_near = pair_perm(ctx_size, 1)
    swap_far = pair_perm(ctx_size, 2)

    def swap(value):
        return lax.ppermute(value, "tp", swap_tp)

    def near(value):
        return lax.ppermute(value, "ctx", swap_near)

    def far(value):
        return lax.ppermute(value, "ctx", swap_far)

    def ordered(own, axis):
        other = swap(own)
        low = jnp.where(tp == 0, own, other)
        high = jnp.where(tp == 0, other, own)
        return jnp.concatenate([low, high], axis=axis)

    depth = qkv_weight.shape[1]
    part = depth // ctx_size
    first = ctx * part
    qkv_part = lax.dynamic_slice_in_dim(qkv_weight, first, part, axis=1)
    full_qkv = lax.all_gather(qkv_part, both, axis=1, tiled=True)
    proj_part = lax.dynamic_slice_in_dim(proj_weight, first, part, axis=1).T
    down_part = lax.dynamic_slice_in_dim(down_weight, first, part, axis=1).T
    pairs_part = lax.dynamic_slice_in_dim(gate_up, first, part, axis=1)
    shards = lax.axis_size("shard")
    rest_part = jnp.concatenate(
        [
            ordered(proj_part, 1),
            jnp.pad(down_part, ((0, 0), (0, pad))),
            jnp.pad(pairs_part[0], ((0, 0), (0, pad))),
            jnp.pad(pairs_part[1], ((0, 0), (0, pad))),
        ],
        axis=1,
    )
    rest = lax.all_gather(rest_part, both, axis=0, tiled=True)
    rest = pltpu.with_memory_space_constraint(rest, pltpu.HBM)

    ln1 = ln1_gain[None, :]
    ln2 = ln2_gain[None, :]
    again = ordered(attn_gain[None, :], 1)
    fgain = jnp.pad(ffn_gain, (0, pad))[None, :]
    tables = rope_tables(ctx * rows + jnp.arange(rows, dtype=jnp.int32))
    order = ctx ^ jnp.arange(4, dtype=jnp.int32)
    counts = jnp.clip(lengths[:, None] - rows * order[None, :], 0, rows)

    act = whole(rows, width)
    act_half = whole(rows, half)
    act_ff = whole(rows, ffp)
    line = whole(1, width)
    line_ff = whole(1, ffp)
    rope_spec = whole(3, rows, LANES)
    qkv_spec = whole(3, width, half)
    pair_half = pl.BlockSpec((rows, LANES), lambda i: (0, i))
    pair_kv = pl.BlockSpec((rows, 2 * LANES), lambda i: (0, i))
    pair_kv2 = pl.BlockSpec((2, rows, 2 * LANES), lambda i: (0, 0, i))
    pair_line = pl.BlockSpec((1, 1, 2 * rows), lambda i: (i, 0, 0))
    block_mb = rows * width

    st = [dict() for _ in range(images)]
    for i in range(images):
        s = st[i]
        s["n"] = counts[i]
        s["sc"] = jnp.stack([counts[i, 0], tp.astype(jnp.int32)])
        s["h1"], s["q"], s["kv"] = call(
            qkv_kernel,
            (shape(rows, width), shape(rows, half), shape(rows, 2 * half)),
            [image_of(i, rows, width), line, qkv_spec, rope_spec],
            [act, act_half, whole(rows, 2 * half)],
            name="qkv",
            mib=24,
            flops=2 * rows * width * 3 * half,
            moved=6 * width * half + 8 * block_mb,
        )(tokens, ln1, full_qkv, tables)
        s["kvc"] = in_hbm(near(s["kv"]))
        s["kvf"] = far(s["kv"])
        s["q"] = in_hbm(s["q"])
    for i in range(images):
        s = st[i]
        if i == images - 1:
            s["kvf"], st[0]["o"] = lax.optimization_barrier((s["kvf"], st[0]["o"]))
        s["kvx"] = in_hbm(near(s["kvf"]))
        s["kvf"], s["kv"] = in_hbm(s["kvf"]), in_hbm(s["kv"])
        s["o"], s["lse"] = call(
            attend_kernel,
            (shape(rows, half), shape(half // LANES, 1, 2 * rows, dtype=F32)),
            [SMEM, pair_half] + [pair_kv] * 4,
            [pair_half, pair_line],
            [
                pltpu.VMEM((1, 2 * rows), F32),
                pltpu.VMEM((1, 2 * rows), F32),
                pltpu.VMEM((LANES, 2 * rows), F32),
            ],
            name="attend",
            mib=20,
            grid=half // LANES,
            flops=16 * rows * 4 * rows * half,
            moved=12 * block_mb,
        )(s["n"], s["q"], s["kv"], s["kvc"], s["kvf"], s["kvx"])
        s["ox"] = swap(s["o"])
    valid = jnp.concatenate([counts[:, 0], tp.astype(jnp.int32)[None]])

    def each(*dims):
        return pl.BlockSpec((1,) + dims, lambda i: (i,) + (0,) * len(dims))

    x1, h2, gate, up, dm, attn_in, stats = call(
        middle_kernel,
        (
            shape(images, rows, width, dtype=F32),
            shape(images, rows, width),
            shape(images, rows, ffp),
            shape(images, rows, ffp),
            shape(images, rows, ffp),
            shape(images, rows, half),
            shape(images, 8, 384, dtype=F32),
        ),
        [SMEM, each(rows, width), each(rows, width)] + [act_half] * 6 + [line, line, line_ff, HBM],
        [
            each(rows, width), each(rows, width), each(rows, ffp), each(rows, ffp), each(rows, ffp),
            each(rows, half), each(8, 384),
        ],
        [
            pltpu.VMEM((width, width), BF),
            pltpu.VMEM((width, ffp), BF),
            pltpu.VMEM((width, ffp), BF),
            pltpu.VMEM((width, ffp), BF),
            pltpu.VMEM((rows, width), BF),
            pltpu.VMEM((rows, width), BF),
            pltpu.VMEM((384, LANES), F32),
            pltpu.SemaphoreType.DMA((4,)),
        ],
        name="middle",
        mib=48,
        grid=images,
        flops=2 * images * rows * width * (width + 3 * ffp),
        moved=2 * width * (width + 3 * ffp) + images * (12 * block_mb + 6 * rows * ffp),
    )(valid, tokens, cotangent, *[s["o"] for s in st], *[s["ox"] for s in st], again, ln2, fgain, rest)
    stats_x = swap(stats)
    for i in range(images):
        s = st[i]
        s["m"], s["dg"], s["du"], s["out"], s["dh2"], s["dffn"] = call(
            functools.partial(ffn_kernel, total=ff_total),
            (
                shape(rows, ffp),
                shape(rows, ffp),
                shape(rows, ffp),
                shape(rows, width),
                shape(rows, width),
                shape(1, ffp, dtype=F32),
            ),
            [image_of(i, 8, 384)] * 2 + [image_of(i, rows, ffp)] * 3 + [line_ff, HBM],
            [act_ff, act_ff, act_ff, act, act, line_ff],
            [
                pltpu.VMEM((width, ffp), BF),
                pltpu.VMEM((width, ffp), BF),
                pltpu.VMEM((width, ffp), BF),
                pltpu.VMEM((LANES, 384), F32),
                pltpu.SemaphoreType.DMA((3,)),
            ],
            name="ffn",
            mib=36,
            flops=2 * rows * width * 3 * ffp,
            moved=6 * width * ffp + 12 * rows * ffp + 4 * block_mb,
        )(stats, stats_x, gate, up, dm, fgain, rest)
        s["dh2x"] = swap(s["dh2"])
    def weight_grads(groups, tag):
        plan = [(masked, len(left), [len(right) for right in rights]) for masked, left, rights in groups]
        flat = [v for _, left, rights in groups for v in left + [w for right in rights for w in right]]
        columns = sum(right[0].shape[-1] for _, _, rights in groups for right in rights)
        return call(
            functools.partial(grads_kernel, plan=plan),
            shape(width, columns),
            [SMEM] + [whole(*v.shape) for v in flat],
            ANY,
            [
                pltpu.VMEM((width, images * rows), BF),
                pltpu.VMEM((width, columns), BF),
                pltpu.SemaphoreType.DMA((len(groups),)),
            ],
            name=tag,
            flops=2 * images * rows * width * columns,
            moved=4 * width * columns,
            mib=50 if columns > 2 * width else 36,
        )(counts[:, 0], *flat)

    def of(key):
        return [s[key] for s in st]

    grads_ffn = weight_grads(
        [(False, [h2], [of("dg"), of("du")]), (True, [cotangent], [of("m")])], "grads_ffn"
    )
    def norm_back(i):
        s = st[i]
        s["dx"], s["dab"], s["do"], s["dln2"], s["dattn"] = call(
            attn_norm_back_kernel,
            (
                shape(rows, width, dtype=F32),
                shape(rows, width),
                shape(rows, half),
                shape(1, width, dtype=F32),
                shape(1, half, dtype=F32),
            ),
            [SMEM, act, act, image_of(i, rows, width), image_of(i, rows, width), line, act_half, act_half, line, HBM],
            [act, act, act_half, line, whole(1, half)],
            [
                pltpu.VMEM((width, width), BF),
                pltpu.VMEM((rows, width), BF),
                pltpu.VMEM((rows, width), F32),
                pltpu.VMEM((8, width), F32),
                pltpu.SemaphoreType.DMA((1,)),
            ],
            name="attn_norm_back",
            mib=28,
            flops=2 * rows * width * width,
            moved=2 * width * width + 16 * block_mb,
        )(s["sc"], s["dh2"], s["dh2x"], x1, cotangent, ln2, s["o"], s["ox"], again, rest)

    def attention_back(i):
        s = st[i]
        s["dq"], s["keep"], s["send"] = call(
            attend_back_kernel,
            (shape(rows, half), shape(2, rows, 2 * half), shape(2, rows, 2 * half)),
            [SMEM, pair_half] + [pair_kv] * 4 + [pair_half, pair_half, pair_line, rope_spec],
            [pair_half, pair_kv2, pair_kv2],
            [pltpu.VMEM((LANES, 2 * rows), F32)],
            grid=half // LANES,
            name="attend_back",
            mib=20,
            flops=40 * rows * 4 * rows * half,
            moved=20 * block_mb,
        )(s["n"], s["q"], s["kv"], s["kvc"], s["kvf"], s["kvx"], s["o"], s["do"], s["lse"], tables)
        s["recv"] = near(s["send"])
        s["mid"] = (s["keep"][1].astype(F32) + s["recv"][1].astype(F32)).astype(BF)

    def qkv_back(i):
        s = st[i]
        s["dkv"], s["dh1"] = call(
            qkv_back_kernel,
            (shape(rows, 2 * half), shape(rows, width)),
            [
                pl.BlockSpec((1, rows, 2 * half), lambda i: (0, 0, 0)),
                pl.BlockSpec((1, rows, 2 * half), lambda i: (0, 0, 0)),
                whole(rows, 2 * half),
                act_half,
                rope_spec,
                qkv_spec,
            ],
            [whole(rows, 2 * half), act],
            name="qkv_back",
            mib=24,
            flops=2 * rows * width * 3 * half,
            moved=6 * width * half + 10 * block_mb,
        )(s["keep"], s["recv"], s["far"], s["dq"], tables, full_qkv)
        s["dh1x"] = swap(s["dh1"])

    def mixed_part(i, mixed):
        s = st[i]
        again_buf = [] if mixed is None else [mixed]
        mixed = call(
            mixed_kernel,
            shape(images, rows, width),
            [image_of(i, rows, width), act, act] + [ANY] * len(again_buf),
            image_of(i, rows, width),
            name="mixed",
            mib=12,
            moved=10 * block_mb,
            aliases={3: 0} if again_buf else None,
        )(x1, s["out"], s["outx"], *again_buf)
        return mixed

    def tokens_part(i, grad_tokens):
        s = st[i]
        again_buf = [] if grad_tokens is None else [grad_tokens]
        grad_tokens, s["dln1"] = call(
            tokens_back_kernel,
            (shape(images, rows, width), shape(1, width, dtype=F32)),
            [act, act, image_of(i, rows, width), line, act] + [ANY] * len(again_buf),
            [image_of(i, rows, width), line],
            name="tokens_back",
            mib=16,
            moved=12 * block_mb,
            aliases={5: 0} if again_buf else None,
        )(s["dh1"], s["dh1x"], tokens, ln1, s["dx"], *again_buf)
        return grad_tokens

    def tie(*values):
        return lax.optimization_barrier(values)

    mixed = grad_tokens = None
    norm_back(0)
    late = [st[1], st[2]]
    tied = tie(st[0]["do"], *[s["out"] for s in st], *[s["dh2x"] for s in late], grads_ffn)
    st[0]["do"], grads_ffn = tied[0], tied[-1]
    for i, s in enumerate(st):
        s["out"] = tied[1 + i]
        s["outx"] = swap(s["out"])
    for i, s in enumerate(late):
        s["dh2x"] = tied[1 + images + i]
    attention_back(0)
    norm_back(1)
    st[1]["do"], st[0]["mid"] = tie(st[1]["do"], st[0]["mid"])
    st[0]["far"] = far(st[0]["mid"])
    attention_back(1)
    norm_back(2)
    st[2]["do"], st[0]["far"] = tie(st[2]["do"], st[0]["far"])
    st[1]["far"] = far(st[1]["mid"])
    qkv_back(0)
    attention_back(2)
    st[2]["far"] = far(st[2]["mid"])
    qkv_back(1)
    st[2]["far"], st[1]["dkv"], st[0]["outx"], st[0]["dh1x"] = tie(
        st[2]["far"], st[1]["dkv"], st[0]["outx"], st[0]["dh1x"]
    )
    qkv_back(2)
    for i in range(images):
        mixed = mixed_part(i, mixed)
    for i in range(images):
        grad_tokens = tokens_part(i, grad_tokens)
    own_ffn = lax.psum_scatter(grads_ffn, both, scatter_dimension=0, tiled=True)

    def around(own):
        beyond = far(own)
        held = [own, near(own), beyond, near(beyond)]
        return jnp.concatenate([lax.select_n(ctx ^ at, *held) for at in range(4)], axis=0)

    grads_qkv = weight_grads(
        [(False, of("h1"), [of("dq"), of("dkv")]), (False, of("dab"), [[attn_in]])], "grads_qkv"
    )
    grads_qkv, own_ffn = lax.optimization_barrier((grads_qkv, own_ffn))
    own_qkv = lax.psum_scatter(grads_qkv, both, scatter_dimension=0, tiled=True)
    grad_pairs, grad_down = call(
        finish_kernel,
        (shape(ff, 2, depth, dtype=F32), shape(ff, depth, dtype=F32)),
        [whole(depth, 3 * ffp)],
        [whole(ff, 2, depth), whole(ff, depth)],
        name="finish",
        mib=20,
        moved=18 * ff * depth,
    )(around(own_ffn))

    def everywhere(value):
        step = 1
        while step < ctx_size:
            value = value + lax.ppermute(value, "ctx", pair_perm(ctx_size, step))
            step *= 2
        step = 1
        while step < shards:
            value = value + lax.ppermute(value, "shard", pair_perm(shards, step))
            step *= 2
        return value

    def gain(name):
        return sum(s[name] for s in st)[0]

    packed = everywhere(jnp.concatenate([gain("dffn"), gain("dln2"), gain("dattn")]))
    gain_ffn = packed[:ff]
    gain_ln2 = packed[ffp : ffp + width]
    gain_attn = packed[ffp + width :]
    gain_ln1 = everywhere(gain("dln1"))
    own_qkv, grad_tokens, mixed, gain_ln1, gain_ffn, grad_pairs, grad_down = tie(
        own_qkv, grad_tokens, mixed, gain_ln1, gain_ffn, grad_pairs, grad_down
    )
    grad_pairs = jnp.transpose(grad_pairs, (1, 2, 0))
    sum_qkv = lax.all_gather(own_qkv[:, : 3 * half], "ctx", axis=0, tiled=True).astype(F32)
    grad_proj = around(own_qkv[:, 3 * half :]).astype(F32).T
    grad_qkv = jnp.stack([sum_qkv[:, j * half : (j + 1) * half] for j in range(3)])

    return (
        mixed,
        grad_tokens,
        gain_ln1,
        grad_qkv,
        gain_attn,
        grad_proj,
        gain_ln2,
        grad_pairs,
        gain_ffn,
        grad_down,
    )


def solution(mesh):
    tokens = P("shard", "ctx", None)
    matrix = P(None, "shard", "tp")
    flipped = P("tp", "shard")
    return jax.shard_map(
        local,
        mesh=mesh,
        in_specs=(
            tokens, tokens, P("shard"), P(), matrix, P("tp"), flipped, P(), matrix, P("tp"), flipped,
        ),
        out_specs=(tokens, tokens, P(), matrix, P("tp"), flipped, P(), matrix, P("tp"), flipped),
        check_vma=False,
    )
```

```python
import functools
import math

import jax
import jax.numpy as jnp
from jax import lax
from jax.experimental import pallas as pl
from jax.experimental.pallas import tpu as pltpu
from jax.sharding import Mesh, PartitionSpec as P

HEAD = 64
GRID = 32
LANES = 128
EPS = 1e-06
BF = jnp.bfloat16
F32 = jnp.float32
TAIL = 80


def dot_nn(a, b):
    return lax.dot_general(a, b, (((1,), (0,)), ((), ())), preferred_element_type=F32)


def dot_nt(a, b):
    return lax.dot_general(a, b, (((1,), (1,)), ((), ())), preferred_element_type=F32)


def dot_tn(a, b):
    return lax.dot_general(a, b, (((0,), (0,)), ((), ())), preferred_element_type=F32)


def tiles(width, step=256):
    return [(at, min(step, width - at)) for at in range(0, width, step)]


def pair_perm(size, flip):
    return [(at, at ^ flip) for at in range(size)]


def rope_tables(positions):
    quarter = HEAD // 4
    place = jnp.maximum(positions - 1, 0)
    row_pos = (place // GRID).astype(F32)
    col_pos = (place % GRID).astype(F32)
    frequency = jnp.exp(jnp.arange(quarter).astype(F32) * (-math.log(10000.0) / quarter))
    row_angle = row_pos[:, None] * frequency[None, :]
    col_angle = col_pos[:, None] * frequency[None, :]
    cr, sr, cc, sc = jnp.cos(row_angle), jnp.sin(row_angle), jnp.cos(col_angle), jnp.sin(col_angle)
    zero = jnp.zeros_like(sr)
    cos = jnp.concatenate([cr, cr, cc, cc], axis=1)
    up = jnp.concatenate([-sr, zero, -sc, zero], axis=1)
    down = jnp.concatenate([zero, sr, zero, sc], axis=1)
    return jnp.stack([jnp.concatenate([t, t], axis=1) for t in (cos, up, down)])


def turn(values, tables_ref, sign):
    shift = HEAD // 4
    return values * tables_ref[0] + sign * (
        pltpu.roll(values, LANES - shift, 1) * tables_ref[1]
        + pltpu.roll(values, shift, 1) * tables_ref[2]
    )


def row_norm(values, width):
    mean = jnp.sum(values, axis=1, keepdims=True) * (1.0 / width)
    centred = values - mean
    inv = lax.rsqrt(jnp.sum(centred * centred, axis=1, keepdims=True) * (1.0 / width) + EPS)
    return centred * inv, inv


def row_norm_back(scaled, normed, inv, width):
    first = jnp.sum(scaled, axis=1, keepdims=True) * (1.0 / width)
    second = jnp.sum(scaled * normed, axis=1, keepdims=True) * (1.0 / width)
    return inv * (scaled - first - normed * second)


def valid_rows(values, count):
    rows = lax.broadcasted_iota(jnp.int32, values.shape, 0)
    return jnp.where(rows < count, values, jnp.zeros_like(values))


def qkv_kernel(x_ref, gain_ref, w_ref, rope_ref, h_ref, q_ref, kv_ref):
    x = x_ref[0].astype(F32)
    normed, _ = row_norm(x, x.shape[1])
    h_ref[...] = (normed * gain_ref[...]).astype(BF)
    width = w_ref.shape[2]
    h = h_ref[...]
    for at, size in tiles(width):
        q = dot_nn(h, w_ref[0, :, at : at + size])
        k = dot_nn(h, w_ref[1, :, at : at + size])
        v = dot_nn(h, w_ref[2, :, at : at + size])
        for off in range(0, size, LANES):
            cols = slice(off, off + LANES)
            q_ref[:, at + off : at + off + LANES] = (
                turn(q[:, cols], rope_ref, 1.0) * HEAD ** (-0.5)
            ).astype(BF)
            pair = 2 * (at + off)
            kv_ref[:, pair : pair + LANES] = turn(k[:, cols], rope_ref, 1.0).astype(BF)
            kv_ref[:, pair + LANES : pair + 2 * LANES] = v[:, cols].astype(BF)


def split_pair(values):
    lane = lax.broadcasted_iota(jnp.int32, values.shape, 1)
    zero = jnp.zeros_like(values)
    return jnp.concatenate(
        [jnp.where(lane < HEAD, values, zero), jnp.where(lane >= HEAD, values, zero)], axis=0
    )


def join_pair(values):
    rows = values.shape[0] // 2
    lane = lax.broadcasted_iota(jnp.int32, (rows, values.shape[1]), 1)
    return jnp.where(lane < HEAD, values[:rows], values[rows:])


def attend_kernel(n_ref, q_ref, kv0, kv1, kv2, kv3, o_ref, lse_ref, m_s, l_s, acc_s):
    qb = split_pair(q_ref[...])
    m_s[...] = jnp.full(m_s.shape, -1e30, F32)
    l_s[...] = jnp.zeros(l_s.shape, F32)
    acc_s[...] = jnp.zeros(acc_s.shape, F32)

    def step(kv_ref, count, size):
        s = dot_nt(kv_ref[:size, :LANES], qb)
        key = lax.broadcasted_iota(jnp.int32, s.shape, 0)
        s = jnp.where(key < count, s, -1e30)
        m_old = m_s[...]
        m_new = jnp.maximum(m_old, jnp.max(s, axis=0, keepdims=True))
        scale = jnp.exp(m_old - m_new)
        e = jnp.exp(s - m_new)
        m_s[...] = m_new
        l_s[...] = l_s[...] * scale + jnp.sum(e, axis=0, keepdims=True)
        acc_s[...] = acc_s[...] * scale + dot_tn(kv_ref[:size, LANES:], e.astype(BF))

    for at, kv_ref in enumerate((kv0, kv1, kv2, kv3)):
        count = n_ref[at]

        @pl.when(count > TAIL)
        def _():
            step(kv_ref, count, kv_ref.shape[0])

        @pl.when((count > 0) & (count <= TAIL))
        def _():
            step(kv_ref, count, TAIL)

    total = l_s[...]
    out = acc_s[...] * (1.0 / total)
    o_ref[...] = join_pair(out.T).astype(BF)
    lse_ref[0] = m_s[...] + jnp.log(total)


def attend_back_kernel(
    n_ref, q_ref, kv0, kv1, kv2, kv3, o_ref, do_ref, lse_ref, rope_ref, dq_ref, keep_ref, send_ref, dq_s
):
    rows = q_ref.shape[0]
    qb = split_pair(q_ref[...])
    do = do_ref[...]
    dob = split_pair(do)
    prod = split_pair(do.astype(F32) * o_ref[...].astype(F32))
    delta = jnp.sum(prod.T, axis=0, keepdims=True)
    lse = lse_ref[0]
    dq_s[...] = jnp.zeros(dq_s.shape, F32)

    def step(kv_ref, out_ref, slot, count, size):
        k = kv_ref[:size, :LANES]
        s = dot_nt(k, qb)
        key = lax.broadcasted_iota(jnp.int32, s.shape, 0)
        p = jnp.where(key < count, jnp.exp(s - lse), 0.0)
        dp = dot_nt(kv_ref[:size, LANES:], dob)
        ds = (p * (dp - delta)).astype(BF)
        out_ref[slot, :size, LANES:] = dot_nn(p.astype(BF), dob).astype(BF)
        out_ref[slot, :size, :LANES] = dot_nn(ds, qb).astype(BF)
        dq_s[...] += dot_tn(k, ds)
        if size < rows:
            out_ref[slot, size:, :] = jnp.zeros((rows - size, 2 * LANES), BF)

    for at, kv_ref in enumerate((kv0, kv1, kv2, kv3)):
        count = n_ref[at]
        out_ref = (keep_ref, send_ref)[at % 2]
        slot = at // 2

        @pl.when(count > TAIL)
        def _():
            step(kv_ref, out_ref, slot, count, kv_ref.shape[0])

        @pl.when((count > 0) & (count <= TAIL))
        def _():
            step(kv_ref, out_ref, slot, count, TAIL)

        @pl.when(count <= 0)
        def _():
            out_ref[slot] = jnp.zeros((rows, 2 * LANES), BF)

    dq = join_pair(dq_s[...].T) * HEAD ** (-0.5)
    dq_ref[...] = turn(dq, rope_ref, -1.0).astype(BF)


def merge_heads(dst, own_ref, other_ref, tp, half):
    dst[:, pl.ds(pl.multiple_of(tp * half, half), half)] = own_ref[...]
    dst[:, pl.ds(pl.multiple_of((1 - tp) * half, half), half)] = other_ref[...]


def middle_kernel(
    sc_ref, x_ref, cot_ref, own_ref0, own_ref1, own_ref2, other_ref0, other_ref1, other_ref2,
    again_ref, ln2_ref, fgain_ref, w_ref,
    x1_ref, h2_ref, g_ref, u_ref, dm_ref, a_ref, st_ref,
    pj_s, gw_s, uw_s, dw_s, o_s, a_s, st_s, sem,
):
    image = pl.program_id(0)
    width = x_ref.shape[2]
    half = own_ref0.shape[1]
    rows = own_ref0.shape[0]
    ff = g_ref.shape[2]
    loads = [
        pltpu.make_async_copy(w_ref.at[:, pl.ds(0, width)], pj_s, sem.at[0]),
        pltpu.make_async_copy(w_ref.at[:, pl.ds(width + ff, ff)], gw_s, sem.at[1]),
        pltpu.make_async_copy(w_ref.at[:, pl.ds(width + 2 * ff, ff)], uw_s, sem.at[2]),
        pltpu.make_async_copy(w_ref.at[:, pl.ds(width, ff)], dw_s, sem.at[3]),
    ]

    @pl.when(image == 0)
    def _():
        for load in loads:
            load.start()

    tp = sc_ref[3]
    for at, (own_ref, other_ref) in enumerate(
        ((own_ref0, other_ref0), (own_ref1, other_ref1), (own_ref2, other_ref2))
    ):

        @pl.when(image == at)
        def _():
            merge_heads(o_s, own_ref, other_ref, tp, half)

    normed, _ = row_norm(o_s[...].astype(F32), width)
    a_s[...] = (normed * again_ref[...]).astype(BF)
    a_ref[0] = a_s[:, pl.ds(pl.multiple_of(tp * half, half), half)]

    @pl.when(image == 0)
    def _():
        loads[0].wait()

    a = a_s[...]
    for at, size in tiles(width):
        x1_ref[0, :, at : at + size] = x_ref[0, :, at : at + size].astype(F32) + dot_nt(
            a, pj_s[at : at + size, :]
        )
    normed, _ = row_norm(x1_ref[0], width)
    h2_ref[0] = (normed * ln2_ref[...]).astype(BF)
    h2 = h2_ref[0]
    dyb = valid_rows(cot_ref[0], sc_ref[image])

    @pl.when(image == 0)
    def _():
        for load in loads[1:]:
            load.wait()

    sums = [jnp.zeros((rows, LANES), F32) for _ in range(4)]
    for at, size in tiles(ff):
        span = slice(at, at + size)
        g = dot_nn(h2, gw_s[:, span]).astype(BF)
        u = dot_nn(h2, uw_s[:, span]).astype(BF)
        dm = dot_nn(dyb, dw_s[:, span]).astype(BF)
        g_ref[0, :, span] = g
        u_ref[0, :, span] = u
        dm_ref[0, :, span] = dm
        gf = g.astype(F32)
        z = gf * jax.nn.sigmoid(gf) * u.astype(F32)
        e = dm.astype(F32) * fgain_ref[:, span]
        for off in range(0, size, LANES):
            zo = z[:, off : off + LANES]
            eo = e[:, off : off + LANES]
            sums = [sums[0] + zo, sums[1] + zo * zo, sums[2] + eo, sums[3] + eo * zo]
    lane = lax.broadcasted_iota(jnp.int32, (rows, LANES), 1)
    packed = jnp.zeros((rows, LANES), F32)
    for slot, part in enumerate(sums):
        packed = jnp.where(lane == slot, jnp.sum(part, axis=1, keepdims=True), packed)
    st_s[...] = jnp.zeros(st_s.shape, F32)
    st_s[:rows, :] = packed
    st_ref[0] = st_s[...].T[:8, :]


def ffn_kernel(
    sa_ref, sb_ref, g_ref, u_ref, dm_ref, fgain_ref, w_ref,
    m_ref, dg_ref, du_ref, out_ref, dh_ref, dgain_ref,
    gw_s, uw_s, dw_s, st_s, sem, *, total,
):
    _, rows, ff = g_ref.shape
    width = w_ref.shape[0]
    loads = [
        pltpu.make_async_copy(w_ref.at[:, pl.ds(width + ff, ff)], gw_s, sem.at[0]),
        pltpu.make_async_copy(w_ref.at[:, pl.ds(width + 2 * ff, ff)], uw_s, sem.at[1]),
        pltpu.make_async_copy(w_ref.at[:, pl.ds(width, ff)], dw_s, sem.at[2]),
    ]
    for load in loads:
        load.start()
    st_s[...] = jnp.zeros(st_s.shape, F32)
    st_s[:8, :] = sa_ref[0] + sb_ref[0]
    st = st_s[...].T[:rows, :]
    lane = lax.broadcasted_iota(jnp.int32, st.shape, 1)

    def column(slot):
        return jnp.sum(jnp.where(lane == slot, st, 0.0), axis=1, keepdims=True) * (1.0 / total)

    mean = column(0)
    inv = lax.rsqrt(jnp.maximum(column(1) - mean * mean, 0.0) + EPS)
    first = column(2)
    second = inv * (column(3) - mean * first)
    for at, size in tiles(ff):
        span = slice(at, at + size)
        g = g_ref[0, :, span].astype(F32)
        u = u_ref[0, :, span].astype(F32)
        dm = dm_ref[0, :, span].astype(F32)
        gain = fgain_ref[:, span]
        sig = jax.nn.sigmoid(g)
        act = g * sig
        normed = (act * u - mean) * inv
        m_ref[:, span] = (normed * gain).astype(BF)
        dgain_ref[:, span] = jnp.sum(dm * normed, axis=0, keepdims=True)
        dz = inv * (dm * gain - first - normed * second)
        dg_ref[:, span] = (dz * u * sig * (1.0 + g * (1.0 - sig))).astype(BF)
        du_ref[:, span] = (dz * act).astype(BF)
    loads[0].wait()
    loads[1].wait()
    dg = dg_ref[...]
    du = du_ref[...]
    for at, size in tiles(width):
        dh_ref[:, at : at + size] = (
            dot_nt(dg, gw_s[at : at + size, :]) + dot_nt(du, uw_s[at : at + size, :])
        ).astype(BF)
    loads[2].wait()
    m = m_ref[...]
    for at, size in tiles(width):
        out_ref[:, at : at + size] = dot_nt(m, dw_s[at : at + size, :]).astype(BF)


def attn_norm_back_kernel(
    sc_ref, dha_ref, dhb_ref, x1_ref, cot_ref, ln2_ref, own_ref, other_ref, again_ref, w_ref,
    dx_ref, dab_ref, do_ref, dln2_ref, dgain_ref,
    pj_s, o_s, e_s, f_s, sem,
):
    width = x1_ref.shape[2]
    half = own_ref.shape[1]
    load = pltpu.make_async_copy(w_ref.at[:, pl.ds(0, width)], pj_s, sem.at[0])
    load.start()
    tp = sc_ref[1]
    dh = dha_ref[...].astype(F32) + dhb_ref[...].astype(F32)
    normed, inv = row_norm(x1_ref[0], width)
    dln2_ref[...] = jnp.sum(dh * normed, axis=0, keepdims=True)
    dy = valid_rows(cot_ref[0].astype(F32), sc_ref[0])
    dx = dy + row_norm_back(dh * ln2_ref[...], normed, inv, width)
    dx_ref[...] = dx
    dab_ref[...] = dx.astype(BF)
    merge_heads(o_s, own_ref, other_ref, tp, half)
    normed, inv = row_norm(o_s[...].astype(F32), width)
    load.wait()
    dab = dab_ref[...]
    for at, size in tiles(width):
        da = dot_nn(dab, pj_s[:, at : at + size])
        e_s[:, at : at + size] = da
    da = e_s[...]
    f_s[...] = jnp.broadcast_to(jnp.sum(da * normed, axis=0, keepdims=True), f_s.shape)
    dgain_ref[...] = f_s[0:1, pl.ds(pl.multiple_of(tp * half, half), half)]
    e_s[...] = row_norm_back(da * again_ref[...], normed, inv, width)
    do_ref[...] = e_s[:, pl.ds(pl.multiple_of(tp * half, half), half)].astype(BF)


def qkv_back_kernel(keep_ref, recv_ref, far_ref, dq_ref, rope_ref, w_ref, dkv_ref, dh_ref):
    rows, half = dq_ref.shape
    total = keep_ref[0].astype(F32) + recv_ref[0].astype(F32) + far_ref[...].astype(F32)
    for at in range(0, half, LANES):
        pair = total[:, 2 * at : 2 * at + 2 * LANES]
        dkv_ref[:, at : at + LANES] = turn(pair[:, :LANES], rope_ref, -1.0).astype(BF)
        dkv_ref[:, half + at : half + at + LANES] = pair[:, LANES:].astype(BF)
    dq = dq_ref[...]
    dk = dkv_ref[:, :half]
    dv = dkv_ref[:, half:]
    for at, size in tiles(w_ref.shape[1]):
        span = slice(at, at + size)
        dh_ref[:, span] = (
            dot_nt(dq, w_ref[0, span, :]) + dot_nt(dk, w_ref[1, span, :]) + dot_nt(dv, w_ref[2, span, :])
        ).astype(BF)


def tokens_back_kernel(da_ref, db_ref, x_ref, gain_ref, dx_ref, *rest):
    out_ref, dgain_ref = rest[-2:]
    width = dx_ref.shape[1]
    dh = da_ref[...].astype(F32) + db_ref[...].astype(F32)
    normed, inv = row_norm(x_ref[0].astype(F32), width)
    dgain_ref[...] = jnp.sum(dh * normed, axis=0, keepdims=True)
    out_ref[0] = (dx_ref[...] + row_norm_back(dh * gain_ref[...], normed, inv, width)).astype(BF)


def mixed_kernel(x1_ref, pa_ref, pb_ref, *rest):
    out_ref = rest[-1]
    out_ref[0] = (x1_ref[0] + (pa_ref[...].astype(F32) + pb_ref[...].astype(F32))).astype(BF)


def finish_kernel(sum_ref, pairs_ref, down_ref):
    ff = down_ref.shape[0]
    ffp = sum_ref.shape[1] // 3
    for at in range(0, ff, LANES):
        size = min(LANES, ff - at)
        for slot in range(3):
            cols = slice(slot * ffp + at, slot * ffp + at + LANES)
            flipped = sum_ref[:, cols].astype(F32).T[:size]
            if slot < 2:
                pairs_ref[at : at + size, slot, :] = flipped
            else:
                down_ref[at : at + size, :] = flipped


def grads_kernel(n_ref, *refs, plan, split=None):
    outs = 1 if split is None else 2
    refs = list(refs)
    *out_refs, flip_s, out_s, sem = refs[-outs - 3 :]
    refs = refs[: -outs - 3]

    def take(count):
        mine = refs[:count]
        del refs[:count]
        return mine

    def joined(mine, cols):
        if len(mine) == 1:
            block = mine[0][:, :, cols]
            return block.reshape(block.shape[0] * block.shape[1], block.shape[2])
        return jnp.concatenate([ref[:, cols] for ref in mine], axis=0)

    copies = []
    column = 0
    for group, (masked, left, rights) in enumerate(plan):
        mine = take(left)
        if masked:
            parts = [valid_rows(mine[0][i], n_ref[i]) for i in range(mine[0].shape[0])]
            flip_s[...] = jnp.concatenate(parts, axis=0).T
        else:
            flip_s[...] = joined(mine, slice(None)).T
        flipped = flip_s[...]
        start = column
        for right in rights:
            mine = take(right)
            span = mine[0].shape[-1]
            for at, size in tiles(span):
                out_s[:, column + at : column + at + size] = dot_nn(
                    flipped, joined(mine, slice(at, at + size))
                ).astype(BF)
            column += span
        if split is None:
            copies.append(
                pltpu.make_async_copy(
                    out_s.at[:, pl.ds(start, column - start)],
                    out_refs[0].at[:, pl.ds(start, column - start)],
                    sem.at[group],
                )
            )
            copies[-1].start()
    if split is not None:
        shards, part = split
        low = n_ref[n_ref.shape[0] - 1]
        for block in range(2 * shards):
            for slot, parity in enumerate((1 - low, low)):
                row = pl.multiple_of((2 * block + parity) * part, part)
                copies.append(
                    pltpu.make_async_copy(
                        out_s.at[pl.ds(row, part), :],
                        out_refs[slot].at[pl.ds(block * part, part), :],
                        sem.at[2 * block + slot],
                    )
                )
                copies[-1].start()
    for copy in copies:
        copy.wait()


VMEM = pl.BlockSpec(memory_space=pltpu.VMEM)
SMEM = pl.BlockSpec(memory_space=pltpu.SMEM)
ANY = pl.BlockSpec(memory_space=pl.ANY)
HBM = pl.BlockSpec(memory_space=pltpu.HBM)


def shape(*dims, dtype=BF):
    return jax.ShapeDtypeStruct(dims, dtype)


def call(kernel, out_shape, in_specs, out_specs, scratch=(), name=None, flops=0, moved=0, aliases=None, mib=48, grid=1):
    return pl.pallas_call(
        kernel,
        out_shape=out_shape,
        in_specs=in_specs,
        out_specs=out_specs,
        grid=(grid,),
        scratch_shapes=list(scratch),
        input_output_aliases=aliases or {},
        name=name,
        cost_estimate=pl.CostEstimate(flops=flops // 16, bytes_accessed=moved // 16, transcendentals=0),
        compiler_params=pltpu.CompilerParams(vmem_limit_bytes=mib << 20),
    )


def whole(*dims):
    return pl.BlockSpec(dims, lambda i: (0,) * len(dims))


def image_of(index, rows, width):
    return pl.BlockSpec((1, rows, width), lambda i: (index, 0, 0))


def in_hbm(value):
    return pltpu.with_memory_space_constraint(value, pltpu.HBM)


def local(
    tokens, cotangent, lengths, ln1_gain, qkv_weight, attn_gain, proj_weight, ln2_gain, gate_up, ffn_gain, down_weight
):
    images, rows, width = tokens.shape
    half = attn_gain.shape[0]
    ff = ffn_gain.shape[0]
    ffp = -(-ff // LANES) * LANES
    pad = ffp - ff
    tp_size = lax.axis_size("tp")
    pairs_of = ("far", "near")
    ctx_size = lax.axis_size(pairs_of)
    ctx = lax.axis_index(pairs_of)
    tp = lax.axis_index("tp")
    ff_total = ff * tp_size
    both = ("shard", *pairs_of)
    swap_tp = pair_perm(tp_size, 1)
    swap_pair = pair_perm(2, 1)

    def swap(value):
        return lax.ppermute(value, "tp", swap_tp)

    def near(value):
        return lax.ppermute(value, "near", swap_pair)

    def far(value):
        return lax.ppermute(value, "far", swap_pair)

    def ordered(own, axis):
        other = swap(own)
        low = jnp.where(tp == 0, own, other)
        high = jnp.where(tp == 0, other, own)
        return jnp.concatenate([low, high], axis=axis)

    depth = qkv_weight.shape[1]
    part = depth // ctx_size
    first = ctx * part
    qkv_part = lax.dynamic_slice_in_dim(qkv_weight, first, part, axis=1)
    full_qkv = lax.all_gather(qkv_part, both, axis=1, tiled=True)
    proj_part = lax.dynamic_slice_in_dim(proj_weight, first, part, axis=1).T
    down_part = lax.dynamic_slice_in_dim(down_weight, first, part, axis=1).T
    pairs_part = lax.dynamic_slice_in_dim(gate_up, first, part, axis=1)
    shards = lax.axis_size("shard")
    rest_part = jnp.concatenate(
        [
            ordered(proj_part, 1),
            jnp.pad(down_part, ((0, 0), (0, pad))),
            jnp.pad(pairs_part[0], ((0, 0), (0, pad))),
            jnp.pad(pairs_part[1], ((0, 0), (0, pad))),
        ],
        axis=1,
    )
    rest = lax.all_gather(rest_part, both, axis=0, tiled=True)
    rest = pltpu.with_memory_space_constraint(rest, pltpu.HBM)

    ln1 = ln1_gain[None, :]
    ln2 = ln2_gain[None, :]
    again = ordered(attn_gain[None, :], 1)
    fgain = jnp.pad(ffn_gain, (0, pad))[None, :]
    tables = rope_tables(ctx * rows + jnp.arange(rows, dtype=jnp.int32))
    order = ctx ^ jnp.arange(4, dtype=jnp.int32)
    counts = jnp.clip(lengths[:, None] - rows * order[None, :], 0, rows)

    act = whole(rows, width)
    act_half = whole(rows, half)
    act_ff = whole(rows, ffp)
    line = whole(1, width)
    line_ff = whole(1, ffp)
    rope_spec = whole(3, rows, LANES)
    qkv_spec = whole(3, width, half)
    pair_half = pl.BlockSpec((rows, LANES), lambda i: (0, i))
    pair_kv = pl.BlockSpec((rows, 2 * LANES), lambda i: (0, i))
    pair_kv2 = pl.BlockSpec((2, rows, 2 * LANES), lambda i: (0, 0, i))
    pair_line = pl.BlockSpec((1, 1, 2 * rows), lambda i: (i, 0, 0))
    block_mb = rows * width

    st = [dict() for _ in range(images)]
    for i in range(images):
        s = st[i]
        s["n"] = counts[i]
        s["sc"] = jnp.stack([counts[i, 0], tp.astype(jnp.int32)])
        s["h1"], s["q"], s["kv"] = call(
            qkv_kernel,
            (shape(rows, width), shape(rows, half), shape(rows, 2 * half)),
            [image_of(i, rows, width), line, qkv_spec, rope_spec],
            [act, act_half, whole(rows, 2 * half)],
            name="qkv",
            mib=14,
            flops=2 * rows * width * 3 * half,
            moved=6 * width * half + 8 * block_mb,
        )(tokens, ln1, full_qkv, tables)
        s["kvc"] = in_hbm(near(s["kv"]))
        s["kvf"] = far(s["kv"])
        s["q"] = in_hbm(s["q"])
    for i in range(images):
        s = st[i]
        if i == images - 1:
            s["kvf"], st[0]["o"] = lax.optimization_barrier((s["kvf"], st[0]["o"]))
        s["kvx"] = in_hbm(near(s["kvf"]))
        s["kvf"], s["kv"] = in_hbm(s["kvf"]), in_hbm(s["kv"])
        s["o"], s["lse"] = call(
            attend_kernel,
            (shape(rows, half), shape(half // LANES, 1, 2 * rows, dtype=F32)),
            [SMEM, pair_half] + [pair_kv] * 4,
            [pair_half, pair_line],
            [
                pltpu.VMEM((1, 2 * rows), F32),
                pltpu.VMEM((1, 2 * rows), F32),
                pltpu.VMEM((LANES, 2 * rows), F32),
            ],
            name="attend",
            mib=8,
            grid=half // LANES,
            flops=16 * rows * 4 * rows * half,
            moved=12 * block_mb,
        )(s["n"], s["q"], s["kv"], s["kvc"], s["kvf"], s["kvx"])
        s["ox"] = swap(s["o"])
    valid = jnp.concatenate([counts[:, 0], tp.astype(jnp.int32)[None]])

    def each(*dims):
        return pl.BlockSpec((1,) + dims, lambda i: (i,) + (0,) * len(dims))

    x1, h2, gate, up, dm, attn_in, stats = call(
        middle_kernel,
        (
            shape(images, rows, width, dtype=F32),
            shape(images, rows, width),
            shape(images, rows, ffp),
            shape(images, rows, ffp),
            shape(images, rows, ffp),
            shape(images, rows, half),
            shape(images, 8, 384, dtype=F32),
        ),
        [SMEM, each(rows, width), each(rows, width)] + [act_half] * 6 + [line, line, line_ff, HBM],
        [
            each(rows, width), each(rows, width), each(rows, ffp), each(rows, ffp), each(rows, ffp),
            each(rows, half), each(8, 384),
        ],
        [
            pltpu.VMEM((width, width), BF),
            pltpu.VMEM((width, ffp), BF),
            pltpu.VMEM((width, ffp), BF),
            pltpu.VMEM((width, ffp), BF),
            pltpu.VMEM((rows, width), BF),
            pltpu.VMEM((rows, width), BF),
            pltpu.VMEM((384, LANES), F32),
            pltpu.SemaphoreType.DMA((4,)),
        ],
        name="middle",
        mib=36,
        grid=images,
        flops=2 * images * rows * width * (width + 3 * ffp),
        moved=2 * width * (width + 3 * ffp) + images * (12 * block_mb + 6 * rows * ffp),
    )(valid, tokens, cotangent, *[s["o"] for s in st], *[s["ox"] for s in st], again, ln2, fgain, rest)
    stats_x = swap(stats)
    for i in range(images):
        s = st[i]
        s["m"], s["dg"], s["du"], s["out"], s["dh2"], s["dffn"] = call(
            functools.partial(ffn_kernel, total=ff_total),
            (
                shape(rows, ffp),
                shape(rows, ffp),
                shape(rows, ffp),
                shape(rows, width),
                shape(rows, width),
                shape(1, ffp, dtype=F32),
            ),
            [image_of(i, 8, 384)] * 2 + [image_of(i, rows, ffp)] * 3 + [line_ff, HBM],
            [act_ff, act_ff, act_ff, act, act, line_ff],
            [
                pltpu.VMEM((width, ffp), BF),
                pltpu.VMEM((width, ffp), BF),
                pltpu.VMEM((width, ffp), BF),
                pltpu.VMEM((LANES, 384), F32),
                pltpu.SemaphoreType.DMA((3,)),
            ],
            name="ffn",
            mib=26,
            flops=2 * rows * width * 3 * ffp,
            moved=6 * width * ffp + 12 * rows * ffp + 4 * block_mb,
        )(stats, stats_x, gate, up, dm, fgain, rest)
        s["dh2x"] = swap(s["dh2"])
    def weight_grads(groups, tag, split=None):
        plan = [(masked, len(left), [len(right) for right in rights]) for masked, left, rights in groups]
        flat = [v for _, left, rights in groups for v in left + [w for right in rights for w in right]]
        columns = sum(right[0].shape[-1] for _, _, rights in groups for right in rights)
        return call(
            functools.partial(grads_kernel, plan=plan, split=split),
            shape(width, columns) if split is None else (shape(width // 2, columns),) * 2,
            [SMEM] + [whole(*v.shape) for v in flat],
            ANY if split is None else (ANY, ANY),
            [
                pltpu.VMEM((width, images * rows), BF),
                pltpu.VMEM((width, columns), BF),
                pltpu.SemaphoreType.DMA((len(groups) if split is None else 4 * split[0],)),
            ],
            name=tag,
            flops=2 * images * rows * width * columns,
            moved=4 * width * columns,
            mib=40 if columns > 2 * width else 26,
        )(jnp.concatenate([counts[:, 0], (ctx % 2).astype(jnp.int32)[None]]), *flat)

    def of(key):
        return [s[key] for s in st]

    grads_ffn = weight_grads(
        [(False, [h2], [of("dg"), of("du")]), (True, [cotangent], [of("m")])], "grads_ffn"
    )
    def norm_back(i):
        s = st[i]
        s["dx"], s["dab"], s["do"], s["dln2"], s["dattn"] = call(
            attn_norm_back_kernel,
            (
                shape(rows, width, dtype=F32),
                shape(rows, width),
                shape(rows, half),
                shape(1, width, dtype=F32),
                shape(1, half, dtype=F32),
            ),
            [SMEM, act, act, image_of(i, rows, width), image_of(i, rows, width), line, act_half, act_half, line, HBM],
            [act, act, act_half, line, whole(1, half)],
            [
                pltpu.VMEM((width, width), BF),
                pltpu.VMEM((rows, width), BF),
                pltpu.VMEM((rows, width), F32),
                pltpu.VMEM((8, width), F32),
                pltpu.SemaphoreType.DMA((1,)),
            ],
            name="attn_norm_back",
            mib=18,
            flops=2 * rows * width * width,
            moved=2 * width * width + 16 * block_mb,
        )(s["sc"], s["dh2"], s["dh2x"], x1, cotangent, ln2, s["o"], s["ox"], again, rest)

    def attention_back(i):
        s = st[i]
        s["dq"], s["keep"], s["send"] = call(
            attend_back_kernel,
            (shape(rows, half), shape(2, rows, 2 * half), shape(2, rows, 2 * half)),
            [SMEM, pair_half] + [pair_kv] * 4 + [pair_half, pair_half, pair_line, rope_spec],
            [pair_half, pair_kv2, pair_kv2],
            [pltpu.VMEM((LANES, 2 * rows), F32)],
            grid=half // LANES,
            name="attend_back",
            mib=12,
            flops=40 * rows * 4 * rows * half,
            moved=20 * block_mb,
        )(s["n"], s["q"], s["kv"], s["kvc"], s["kvf"], s["kvx"], s["o"], s["do"], s["lse"], tables)
        s["recv"] = near(s["send"])
        s["mid"] = (s["keep"][1].astype(F32) + s["recv"][1].astype(F32)).astype(BF)

    def qkv_back(i):
        s = st[i]
        s["dkv"], s["dh1"] = call(
            qkv_back_kernel,
            (shape(rows, 2 * half), shape(rows, width)),
            [
                pl.BlockSpec((1, rows, 2 * half), lambda i: (0, 0, 0)),
                pl.BlockSpec((1, rows, 2 * half), lambda i: (0, 0, 0)),
                whole(rows, 2 * half),
                act_half,
                rope_spec,
                qkv_spec,
            ],
            [whole(rows, 2 * half), act],
            name="qkv_back",
            mib=14,
            flops=2 * rows * width * 3 * half,
            moved=6 * width * half + 10 * block_mb,
        )(s["keep"], s["recv"], s["far"], s["dq"], tables, full_qkv)
        s["dh1x"] = swap(s["dh1"])

    def mixed_part(i, mixed):
        s = st[i]
        again_buf = [] if mixed is None else [mixed]
        mixed = call(
            mixed_kernel,
            shape(images, rows, width),
            [image_of(i, rows, width), act, act] + [ANY] * len(again_buf),
            image_of(i, rows, width),
            name="mixed",
            mib=12,
            moved=10 * block_mb,
            aliases={3: 0} if again_buf else None,
        )(x1, s["out"], s["outx"], *again_buf)
        return mixed

    def tokens_part(i, grad_tokens):
        s = st[i]
        again_buf = [] if grad_tokens is None else [grad_tokens]
        grad_tokens, s["dln1"] = call(
            tokens_back_kernel,
            (shape(images, rows, width), shape(1, width, dtype=F32)),
            [act, act, image_of(i, rows, width), line, act] + [ANY] * len(again_buf),
            [image_of(i, rows, width), line],
            name="tokens_back",
            mib=16,
            moved=12 * block_mb,
            aliases={5: 0} if again_buf else None,
        )(s["dh1"], s["dh1x"], tokens, ln1, s["dx"], *again_buf)
        return grad_tokens

    def tie(*values):
        return lax.optimization_barrier(values)

    mixed = grad_tokens = None
    norm_back(0)
    late = [st[1], st[2]]
    tied = tie(st[0]["do"], *[s["out"] for s in st], *[s["dh2x"] for s in late], grads_ffn)
    st[0]["do"], grads_ffn = tied[0], tied[-1]
    for i, s in enumerate(st):
        s["out"] = tied[1 + i]
        s["outx"] = swap(s["out"])
    for i, s in enumerate(late):
        s["dh2x"] = tied[1 + images + i]
    attention_back(0)
    norm_back(1)
    st[1]["do"], st[0]["mid"] = tie(st[1]["do"], st[0]["mid"])
    st[0]["far"] = far(st[0]["mid"])
    attention_back(1)
    norm_back(2)
    st[2]["do"], st[0]["far"] = tie(st[2]["do"], st[0]["far"])
    st[1]["far"] = far(st[1]["mid"])
    qkv_back(0)
    attention_back(2)
    st[2]["far"] = far(st[2]["mid"])
    qkv_back(1)
    st[2]["far"], st[1]["dkv"], st[0]["outx"], st[0]["dh1x"] = tie(
        st[2]["far"], st[1]["dkv"], st[0]["outx"], st[0]["dh1x"]
    )
    qkv_back(2)
    for i in range(images):
        mixed = mixed_part(i, mixed)
    for i in range(images):
        grad_tokens = tokens_part(i, grad_tokens)
    own_ffn = lax.psum_scatter(grads_ffn, both, scatter_dimension=0, tiled=True)

    def around(own):
        beyond = far(own)
        held = [own, near(own), beyond, near(beyond)]
        return jnp.concatenate([lax.select_n(ctx ^ at, *held) for at in range(4)], axis=0)

    send, keep = weight_grads(
        [(False, of("h1"), [of("dq"), of("dkv")]), (False, of("dab"), [[attn_in]])], "grads_qkv", split=(shards, part)
    )
    grads_qkv = (keep.astype(F32) + near(send).astype(F32)).astype(BF)
    grads_qkv, own_ffn = tie(grads_qkv, own_ffn)
    own_qkv = lax.psum_scatter(grads_qkv, ("shard", "far"), scatter_dimension=0, tiled=True)
    grad_pairs, grad_down = call(
        finish_kernel,
        (shape(ff, 2, depth, dtype=F32), shape(ff, depth, dtype=F32)),
        [whole(depth, 3 * ffp)],
        [whole(ff, 2, depth), whole(ff, depth)],
        name="finish",
        mib=20,
        moved=18 * ff * depth,
    )(around(own_ffn))

    def everywhere(value):
        value = value + near(value)
        value = value + far(value)
        step = 1
        while step < shards:
            value = value + lax.ppermute(value, "shard", pair_perm(shards, step))
            step *= 2
        return value

    def gain(name):
        return sum(s[name] for s in st)[0]

    packed = everywhere(jnp.concatenate([gain("dffn"), gain("dln2"), gain("dattn")]))
    gain_ffn = packed[:ff]
    gain_ln2 = packed[ffp : ffp + width]
    gain_attn = packed[ffp + width :]
    gain_ln1 = everywhere(gain("dln1"))
    own_qkv, grad_tokens, mixed, gain_ln1, gain_ffn, grad_pairs, grad_down = tie(
        own_qkv, grad_tokens, mixed, gain_ln1, gain_ffn, grad_pairs, grad_down
    )
    grad_pairs = jnp.transpose(grad_pairs, (1, 2, 0))
    sum_qkv = lax.all_gather(own_qkv[:, : 3 * half], pairs_of, axis=0, tiled=True).astype(F32)
    grad_proj = around(own_qkv[:, 3 * half :]).astype(F32).T
    grad_qkv = jnp.stack([sum_qkv[:, j * half : (j + 1) * half] for j in range(3)])

    return (
        mixed,
        grad_tokens,
        gain_ln1,
        grad_qkv,
        gain_attn,
        grad_proj,
        gain_ln2,
        grad_pairs,
        gain_ffn,
        grad_down,
    )


def solution(mesh):
    size = dict(mesh.shape)
    mesh = Mesh(
        mesh.devices.reshape(size["shard"], size["ctx"] // 2, 2, size["tp"]), ("shard", "far", "near", "tp")
    )
    tokens = P("shard", ("far", "near"), None)
    matrix = P(None, "shard", "tp")
    flipped = P("tp", "shard")
    return jax.shard_map(
        local,
        mesh=mesh,
        in_specs=(
            tokens, tokens, P("shard"), P(), matrix, P("tp"), flipped, P(), matrix, P("tp"), flipped,
        ),
        out_specs=(tokens, tokens, P(), matrix, P("tp"), flipped, P(), matrix, P("tp"), flipped),
        check_vma=False,
    )
```

```python
import functools
import math

import jax
import jax.numpy as jnp
from jax import lax
from jax.experimental import pallas as pl
from jax.experimental.pallas import tpu as pltpu
from jax.sharding import Mesh, PartitionSpec as P

HEAD = 64
GRID = 32
LANES = 128
EPS = 1e-06
BF = jnp.bfloat16
F32 = jnp.float32
TAIL = 80


def dot_nn(a, b):
    return lax.dot_general(a, b, (((1,), (0,)), ((), ())), preferred_element_type=F32)


def dot_nt(a, b):
    return lax.dot_general(a, b, (((1,), (1,)), ((), ())), preferred_element_type=F32)


def dot_tn(a, b):
    return lax.dot_general(a, b, (((0,), (0,)), ((), ())), preferred_element_type=F32)


def tiles(width, step=256):
    return [(at, min(step, width - at)) for at in range(0, width, step)]


def pair_perm(size, flip):
    return [(at, at ^ flip) for at in range(size)]


def rope_tables(positions):
    quarter = HEAD // 4
    place = jnp.maximum(positions - 1, 0)
    row_pos = (place // GRID).astype(F32)
    col_pos = (place % GRID).astype(F32)
    frequency = jnp.exp(jnp.arange(quarter).astype(F32) * (-math.log(10000.0) / quarter))
    row_angle = row_pos[:, None] * frequency[None, :]
    col_angle = col_pos[:, None] * frequency[None, :]
    cr, sr, cc, sc = jnp.cos(row_angle), jnp.sin(row_angle), jnp.cos(col_angle), jnp.sin(col_angle)
    zero = jnp.zeros_like(sr)
    cos = jnp.concatenate([cr, cr, cc, cc], axis=1)
    up = jnp.concatenate([-sr, zero, -sc, zero], axis=1)
    down = jnp.concatenate([zero, sr, zero, sc], axis=1)
    return jnp.stack([jnp.concatenate([t, t], axis=1) for t in (cos, up, down)])


def turn(values, tables_ref, sign):
    shift = HEAD // 4
    return values * tables_ref[0] + sign * (
        pltpu.roll(values, LANES - shift, 1) * tables_ref[1]
        + pltpu.roll(values, shift, 1) * tables_ref[2]
    )


def row_norm(values, width):
    mean = jnp.sum(values, axis=1, keepdims=True) * (1.0 / width)
    centred = values - mean
    inv = lax.rsqrt(jnp.sum(centred * centred, axis=1, keepdims=True) * (1.0 / width) + EPS)
    return centred * inv, inv


def row_norm_back(scaled, normed, inv, width):
    first = jnp.sum(scaled, axis=1, keepdims=True) * (1.0 / width)
    second = jnp.sum(scaled * normed, axis=1, keepdims=True) * (1.0 / width)
    return inv * (scaled - first - normed * second)


def valid_rows(values, count):
    rows = lax.broadcasted_iota(jnp.int32, values.shape, 0)
    return jnp.where(rows < count, values, jnp.zeros_like(values))


def qkv_kernel(x_ref, gain_ref, w_ref, rope_ref, h_ref, q_ref, kv_ref):
    x = x_ref[0].astype(F32)
    normed, _ = row_norm(x, x.shape[1])
    h_ref[...] = (normed * gain_ref[...]).astype(BF)
    width = w_ref.shape[2]
    h = h_ref[...]
    for at, size in tiles(width):
        q = dot_nn(h, w_ref[0, :, at : at + size])
        k = dot_nn(h, w_ref[1, :, at : at + size])
        v = dot_nn(h, w_ref[2, :, at : at + size])
        for off in range(0, size, LANES):
            cols = slice(off, off + LANES)
            q_ref[:, at + off : at + off + LANES] = (
                turn(q[:, cols], rope_ref, 1.0) * HEAD ** (-0.5)
            ).astype(BF)
            pair = 2 * (at + off)
            kv_ref[:, pair : pair + LANES] = turn(k[:, cols], rope_ref, 1.0).astype(BF)
            kv_ref[:, pair + LANES : pair + 2 * LANES] = v[:, cols].astype(BF)


def split_pair(values):
    lane = lax.broadcasted_iota(jnp.int32, values.shape, 1)
    zero = jnp.zeros_like(values)
    return jnp.concatenate(
        [jnp.where(lane < HEAD, values, zero), jnp.where(lane >= HEAD, values, zero)], axis=0
    )


def join_pair(values):
    rows = values.shape[0] // 2
    lane = lax.broadcasted_iota(jnp.int32, (rows, values.shape[1]), 1)
    return jnp.where(lane < HEAD, values[:rows], values[rows:])


def attend_kernel(n_ref, q_ref, kv0, kv1, kv2, kv3, o_ref, lse_ref, m_s, l_s, acc_s, *, image):
    qb = split_pair(q_ref[...])
    m_s[...] = jnp.full(m_s.shape, -1e30, F32)
    l_s[...] = jnp.zeros(l_s.shape, F32)
    acc_s[...] = jnp.zeros(acc_s.shape, F32)

    def step(kv_ref, count, size):
        s = dot_nt(kv_ref[:size, :LANES], qb)
        key = lax.broadcasted_iota(jnp.int32, s.shape, 0)
        s = jnp.where(key < count, s, -1e30)
        m_old = m_s[...]
        m_new = jnp.maximum(m_old, jnp.max(s, axis=0, keepdims=True))
        scale = jnp.exp(m_old - m_new)
        e = jnp.exp(s - m_new)
        m_s[...] = m_new
        l_s[...] = l_s[...] * scale + jnp.sum(e, axis=0, keepdims=True)
        acc_s[...] = acc_s[...] * scale + dot_tn(kv_ref[:size, LANES:], e.astype(BF))

    for at, kv_ref in enumerate((kv0, kv1, kv2, kv3)):
        count = n_ref[4 * image + at]

        @pl.when(count > TAIL)
        def _():
            step(kv_ref, count, kv_ref.shape[0])

        @pl.when((count > 0) & (count <= TAIL))
        def _():
            step(kv_ref, count, TAIL)

    total = l_s[...]
    out = acc_s[...] * (1.0 / total)
    o_ref[...] = join_pair(out.T).astype(BF)
    lse_ref[0] = m_s[...] + jnp.log(total)


def attend_back_kernel(
    n_ref, q_ref, kv0, kv1, kv2, kv3, o_ref, do_ref, lse_ref, rope_ref, dq_ref, keep_ref, send_ref, dq_s, *, image
):
    rows = q_ref.shape[0]
    qb = split_pair(q_ref[...])
    do = do_ref[...]
    dob = split_pair(do)
    prod = split_pair(do.astype(F32) * o_ref[...].astype(F32))
    delta = jnp.sum(prod.T, axis=0, keepdims=True)
    lse = lse_ref[0]
    dq_s[...] = jnp.zeros(dq_s.shape, F32)

    def step(kv_ref, out_ref, slot, count, size):
        k = kv_ref[:size, :LANES]
        s = dot_nt(k, qb)
        key = lax.broadcasted_iota(jnp.int32, s.shape, 0)
        p = jnp.where(key < count, jnp.exp(s - lse), 0.0)
        dp = dot_nt(kv_ref[:size, LANES:], dob)
        ds = (p * (dp - delta)).astype(BF)
        out_ref[slot, :size, LANES:] = dot_nn(p.astype(BF), dob).astype(BF)
        out_ref[slot, :size, :LANES] = dot_nn(ds, qb).astype(BF)
        dq_s[...] += dot_tn(k, ds)
        if size < rows:
            out_ref[slot, size:, :] = jnp.zeros((rows - size, 2 * LANES), BF)

    for at, kv_ref in enumerate((kv0, kv1, kv2, kv3)):
        count = n_ref[4 * image + at]
        out_ref = (keep_ref, send_ref)[at % 2]
        slot = at // 2

        @pl.when(count > TAIL)
        def _():
            step(kv_ref, out_ref, slot, count, kv_ref.shape[0])

        @pl.when((count > 0) & (count <= TAIL))
        def _():
            step(kv_ref, out_ref, slot, count, TAIL)

        @pl.when(count <= 0)
        def _():
            out_ref[slot] = jnp.zeros((rows, 2 * LANES), BF)

    dq = join_pair(dq_s[...].T) * HEAD ** (-0.5)
    dq_ref[...] = turn(dq, rope_ref, -1.0).astype(BF)


def merge_heads(dst, own_ref, other_ref, tp, half):
    dst[:, pl.ds(pl.multiple_of(tp * half, half), half)] = own_ref[...]
    dst[:, pl.ds(pl.multiple_of((1 - tp) * half, half), half)] = other_ref[...]


def middle_kernel(
    sc_ref, x_ref, cot_ref, own_ref0, own_ref1, own_ref2, other_ref0, other_ref1, other_ref2,
    again_ref, ln2_ref, fgain_ref, w_ref,
    x1_ref, h2_ref, g_ref, u_ref, dm_ref, a_ref, st_ref,
    pj_s, gw_s, uw_s, dw_s, o_s, a_s, st_s, sem,
):
    image = pl.program_id(0)
    width = x_ref.shape[2]
    half = own_ref0.shape[1]
    rows = own_ref0.shape[0]
    ff = g_ref.shape[2]
    loads = [
        pltpu.make_async_copy(w_ref.at[:, pl.ds(0, width)], pj_s, sem.at[0]),
        pltpu.make_async_copy(w_ref.at[:, pl.ds(width + ff, ff)], gw_s, sem.at[1]),
        pltpu.make_async_copy(w_ref.at[:, pl.ds(width + 2 * ff, ff)], uw_s, sem.at[2]),
        pltpu.make_async_copy(w_ref.at[:, pl.ds(width, ff)], dw_s, sem.at[3]),
    ]

    @pl.when(image == 0)
    def _():
        for load in loads:
            load.start()

    tp = sc_ref[3]
    for at, (own_ref, other_ref) in enumerate(
        ((own_ref0, other_ref0), (own_ref1, other_ref1), (own_ref2, other_ref2))
    ):

        @pl.when(image == at)
        def _():
            merge_heads(o_s, own_ref, other_ref, tp, half)

    normed, _ = row_norm(o_s[...].astype(F32), width)
    a_s[...] = (normed * again_ref[...]).astype(BF)
    a_ref[0] = a_s[:, pl.ds(pl.multiple_of(tp * half, half), half)]

    @pl.when(image == 0)
    def _():
        loads[0].wait()

    a = a_s[...]
    for at, size in tiles(width):
        x1_ref[0, :, at : at + size] = x_ref[0, :, at : at + size].astype(F32) + dot_nt(
            a, pj_s[at : at + size, :]
        )
    normed, _ = row_norm(x1_ref[0], width)
    h2_ref[0] = (normed * ln2_ref[...]).astype(BF)
    h2 = h2_ref[0]
    dyb = valid_rows(cot_ref[0], sc_ref[image])

    @pl.when(image == 0)
    def _():
        for load in loads[1:]:
            load.wait()

    sums = [jnp.zeros((rows, LANES), F32) for _ in range(4)]
    for at, size in tiles(ff):
        span = slice(at, at + size)
        g = dot_nn(h2, gw_s[:, span]).astype(BF)
        u = dot_nn(h2, uw_s[:, span]).astype(BF)
        dm = dot_nn(dyb, dw_s[:, span]).astype(BF)
        g_ref[0, :, span] = g
        u_ref[0, :, span] = u
        dm_ref[0, :, span] = dm
        gf = g.astype(F32)
        z = gf * jax.nn.sigmoid(gf) * u.astype(F32)
        e = dm.astype(F32) * fgain_ref[:, span]
        for off in range(0, size, LANES):
            zo = z[:, off : off + LANES]
            eo = e[:, off : off + LANES]
            sums = [sums[0] + zo, sums[1] + zo * zo, sums[2] + eo, sums[3] + eo * zo]
    lane = lax.broadcasted_iota(jnp.int32, (rows, LANES), 1)
    packed = jnp.zeros((rows, LANES), F32)
    for slot, part in enumerate(sums):
        packed = jnp.where(lane == slot, jnp.sum(part, axis=1, keepdims=True), packed)
    st_s[...] = jnp.zeros(st_s.shape, F32)
    st_s[:rows, :] = packed
    st_ref[0] = st_s[...].T[:8, :]


def ffn_kernel(
    sa_ref, sb_ref, g_ref, u_ref, dm_ref, fgain_ref, w_ref,
    m_ref, dg_ref, du_ref, out_ref, dh_ref, dgain_ref,
    gw_s, uw_s, dw_s, st_s, sem, *, total,
):
    _, rows, ff = g_ref.shape
    width = w_ref.shape[0]
    loads = [
        pltpu.make_async_copy(w_ref.at[:, pl.ds(width + ff, ff)], gw_s, sem.at[0]),
        pltpu.make_async_copy(w_ref.at[:, pl.ds(width + 2 * ff, ff)], uw_s, sem.at[1]),
        pltpu.make_async_copy(w_ref.at[:, pl.ds(width, ff)], dw_s, sem.at[2]),
    ]
    for load in loads:
        load.start()
    st_s[...] = jnp.zeros(st_s.shape, F32)
    st_s[:8, :] = sa_ref[0] + sb_ref[0]
    st = st_s[...].T[:rows, :]
    lane = lax.broadcasted_iota(jnp.int32, st.shape, 1)

    def column(slot):
        return jnp.sum(jnp.where(lane == slot, st, 0.0), axis=1, keepdims=True) * (1.0 / total)

    mean = column(0)
    inv = lax.rsqrt(jnp.maximum(column(1) - mean * mean, 0.0) + EPS)
    first = column(2)
    second = inv * (column(3) - mean * first)
    for at, size in tiles(ff):
        span = slice(at, at + size)
        g = g_ref[0, :, span].astype(F32)
        u = u_ref[0, :, span].astype(F32)
        dm = dm_ref[0, :, span].astype(F32)
        gain = fgain_ref[:, span]
        sig = jax.nn.sigmoid(g)
        act = g * sig
        normed = (act * u - mean) * inv
        m_ref[:, span] = (normed * gain).astype(BF)
        dgain_ref[:, span] = jnp.sum(dm * normed, axis=0, keepdims=True)
        dz = inv * (dm * gain - first - normed * second)
        dg_ref[:, span] = (dz * u * sig * (1.0 + g * (1.0 - sig))).astype(BF)
        du_ref[:, span] = (dz * act).astype(BF)
    loads[0].wait()
    loads[1].wait()
    dg = dg_ref[...]
    du = du_ref[...]
    for at, size in tiles(width):
        dh_ref[:, at : at + size] = (
            dot_nt(dg, gw_s[at : at + size, :]) + dot_nt(du, uw_s[at : at + size, :])
        ).astype(BF)
    loads[2].wait()
    m = m_ref[...]
    for at, size in tiles(width):
        out_ref[:, at : at + size] = dot_nt(m, dw_s[at : at + size, :]).astype(BF)


def attn_norm_back_kernel(
    sc_ref, dha_ref, dhb_ref, x1_ref, cot_ref, ln2_ref, own_ref, other_ref, again_ref, w_ref,
    dx_ref, dab_ref, do_ref, dln2_ref, dgain_ref,
    pj_s, o_s, e_s, f_s, sem, *, image,
):
    width = x1_ref.shape[2]
    half = own_ref.shape[1]
    load = pltpu.make_async_copy(w_ref.at[:, pl.ds(0, width)], pj_s, sem.at[0])
    load.start()
    tp = sc_ref[3]
    dh = dha_ref[...].astype(F32) + dhb_ref[...].astype(F32)
    normed, inv = row_norm(x1_ref[0], width)
    dln2_ref[...] = jnp.sum(dh * normed, axis=0, keepdims=True)
    dy = valid_rows(cot_ref[0].astype(F32), sc_ref[image])
    dx = dy + row_norm_back(dh * ln2_ref[...], normed, inv, width)
    dx_ref[...] = dx
    dab_ref[...] = dx.astype(BF)
    merge_heads(o_s, own_ref, other_ref, tp, half)
    normed, inv = row_norm(o_s[...].astype(F32), width)
    load.wait()
    dab = dab_ref[...]
    for at, size in tiles(width):
        da = dot_nn(dab, pj_s[:, at : at + size])
        e_s[:, at : at + size] = da
    da = e_s[...]
    f_s[...] = jnp.broadcast_to(jnp.sum(da * normed, axis=0, keepdims=True), f_s.shape)
    dgain_ref[...] = f_s[0:1, pl.ds(pl.multiple_of(tp * half, half), half)]
    e_s[...] = row_norm_back(da * again_ref[...], normed, inv, width)
    do_ref[...] = e_s[:, pl.ds(pl.multiple_of(tp * half, half), half)].astype(BF)


def qkv_back_kernel(keep_ref, recv_ref, far_ref, dq_ref, rope_ref, w_ref, dkv_ref, dh_ref):
    rows, half = dq_ref.shape
    total = keep_ref[0].astype(F32) + recv_ref[0].astype(F32) + far_ref[...].astype(F32)
    for at in range(0, half, LANES):
        pair = total[:, 2 * at : 2 * at + 2 * LANES]
        dkv_ref[:, at : at + LANES] = turn(pair[:, :LANES], rope_ref, -1.0).astype(BF)
        dkv_ref[:, half + at : half + at + LANES] = pair[:, LANES:].astype(BF)
    dq = dq_ref[...]
    dk = dkv_ref[:, :half]
    dv = dkv_ref[:, half:]
    for at, size in tiles(w_ref.shape[1]):
        span = slice(at, at + size)
        dh_ref[:, span] = (
            dot_nt(dq, w_ref[0, span, :]) + dot_nt(dk, w_ref[1, span, :]) + dot_nt(dv, w_ref[2, span, :])
        ).astype(BF)


def tokens_back_kernel(da_ref, db_ref, x_ref, gain_ref, dx_ref, *rest):
    out_ref, dgain_ref = rest[-2:]
    width = dx_ref.shape[1]
    dh = da_ref[...].astype(F32) + db_ref[...].astype(F32)
    normed, inv = row_norm(x_ref[0].astype(F32), width)
    dgain_ref[...] = jnp.sum(dh * normed, axis=0, keepdims=True)
    out_ref[0] = (dx_ref[...] + row_norm_back(dh * gain_ref[...], normed, inv, width)).astype(BF)


def mixed_kernel(x1_ref, pa_ref, pb_ref, *rest):
    out_ref = rest[-1]
    out_ref[0] = (x1_ref[0] + (pa_ref[...].astype(F32) + pb_ref[...].astype(F32))).astype(BF)


def finish_kernel(sum_ref, pairs_ref, down_ref):
    ff = down_ref.shape[0]
    ffp = sum_ref.shape[1] // 3
    for at in range(0, ff, LANES):
        size = min(LANES, ff - at)
        for slot in range(3):
            cols = slice(slot * ffp + at, slot * ffp + at + LANES)
            flipped = sum_ref[:, cols].astype(F32).T[:size]
            if slot < 2:
                pairs_ref[at : at + size, slot, :] = flipped
            else:
                down_ref[at : at + size, :] = flipped


def grads_kernel(n_ref, *refs, plan, split=None):
    outs = 1 if split is None else 2
    refs = list(refs)
    *out_refs, flip_s, out_s, sem = refs[-outs - 3 :]
    refs = refs[: -outs - 3]

    def take(count):
        mine = refs[:count]
        del refs[:count]
        return mine

    def joined(mine, cols):
        if len(mine) == 1:
            block = mine[0][:, :, cols]
            return block.reshape(block.shape[0] * block.shape[1], block.shape[2])
        return jnp.concatenate([ref[:, cols] for ref in mine], axis=0)

    copies = []
    column = 0
    for group, (masked, left, rights) in enumerate(plan):
        mine = take(left)
        if masked:
            parts = [valid_rows(mine[0][i], n_ref[i]) for i in range(mine[0].shape[0])]
            flip_s[...] = jnp.concatenate(parts, axis=0).T
        else:
            flip_s[...] = joined(mine, slice(None)).T
        flipped = flip_s[...]
        start = column
        for right in rights:
            mine = take(right)
            span = mine[0].shape[-1]
            for at, size in tiles(span):
                out_s[:, column + at : column + at + size] = dot_nn(
                    flipped, joined(mine, slice(at, at + size))
                ).astype(BF)
            column += span
        if split is None:
            copies.append(
                pltpu.make_async_copy(
                    out_s.at[:, pl.ds(start, column - start)],
                    out_refs[0].at[:, pl.ds(start, column - start)],
                    sem.at[group],
                )
            )
            copies[-1].start()
    if split is not None:
        shards, part = split
        low = n_ref[n_ref.shape[0] - 1]
        for block in range(2 * shards):
            for slot, parity in enumerate((1 - low, low)):
                row = pl.multiple_of((2 * block + parity) * part, part)
                copies.append(
                    pltpu.make_async_copy(
                        out_s.at[pl.ds(row, part), :],
                        out_refs[slot].at[pl.ds(block * part, part), :],
                        sem.at[2 * block + slot],
                    )
                )
                copies[-1].start()
    for copy in copies:
        copy.wait()


VMEM = pl.BlockSpec(memory_space=pltpu.VMEM)
SMEM = pl.BlockSpec(memory_space=pltpu.SMEM)
ANY = pl.BlockSpec(memory_space=pl.ANY)
HBM = pl.BlockSpec(memory_space=pltpu.HBM)


def shape(*dims, dtype=BF):
    return jax.ShapeDtypeStruct(dims, dtype)


def call(kernel, out_shape, in_specs, out_specs, scratch=(), name=None, flops=0, moved=0, aliases=None, mib=48, grid=1):
    return pl.pallas_call(
        kernel,
        out_shape=out_shape,
        in_specs=in_specs,
        out_specs=out_specs,
        grid=(grid,),
        scratch_shapes=list(scratch),
        input_output_aliases=aliases or {},
        name=name,
        cost_estimate=pl.CostEstimate(flops=flops // 16, bytes_accessed=moved // 16, transcendentals=0),
        compiler_params=pltpu.CompilerParams(vmem_limit_bytes=mib << 20),
    )


def whole(*dims):
    return pl.BlockSpec(dims, lambda i: (0,) * len(dims))


def image_of(index, rows, width):
    return pl.BlockSpec((1, rows, width), lambda i: (index, 0, 0))


def in_hbm(value):
    return pltpu.with_memory_space_constraint(value, pltpu.HBM)


def local(
    tokens, cotangent, lengths, ln1_gain, qkv_weight, attn_gain, proj_weight, ln2_gain, gate_up, ffn_gain, down_weight
):
    images, rows, width = tokens.shape
    half = attn_gain.shape[0]
    ff = ffn_gain.shape[0]
    ffp = -(-ff // LANES) * LANES
    pad = ffp - ff
    tp_size = lax.axis_size("tp")
    pairs_of = ("far", "near")
    ctx_size = lax.axis_size(pairs_of)
    ctx = lax.axis_index(pairs_of)
    tp = lax.axis_index("tp")
    ff_total = ff * tp_size
    both = ("shard", *pairs_of)
    swap_tp = pair_perm(tp_size, 1)
    swap_pair = pair_perm(2, 1)

    def swap(value):
        return lax.ppermute(value, "tp", swap_tp)

    def near(value):
        return lax.ppermute(value, "near", swap_pair)

    def far(value):
        return lax.ppermute(value, "far", swap_pair)

    def ordered(own, axis):
        other = swap(own)
        low = jnp.where(tp == 0, own, other)
        high = jnp.where(tp == 0, other, own)
        return jnp.concatenate([low, high], axis=axis)

    depth = qkv_weight.shape[1]
    part = depth // ctx_size
    first = ctx * part
    qkv_part = lax.dynamic_slice_in_dim(qkv_weight, first, part, axis=1)
    full_qkv = lax.all_gather(qkv_part, both, axis=1, tiled=True)
    proj_part = lax.dynamic_slice_in_dim(proj_weight, first, part, axis=1).T
    down_part = lax.dynamic_slice_in_dim(down_weight, first, part, axis=1).T
    pairs_part = lax.dynamic_slice_in_dim(gate_up, first, part, axis=1)
    shards = lax.axis_size("shard")
    rest_part = jnp.concatenate(
        [
            ordered(proj_part, 1),
            jnp.pad(down_part, ((0, 0), (0, pad))),
            jnp.pad(pairs_part[0], ((0, 0), (0, pad))),
            jnp.pad(pairs_part[1], ((0, 0), (0, pad))),
        ],
        axis=1,
    )
    rest = lax.all_gather(rest_part, both, axis=0, tiled=True)
    rest = pltpu.with_memory_space_constraint(rest, pltpu.HBM)

    ln1 = ln1_gain[None, :]
    ln2 = ln2_gain[None, :]
    again = ordered(attn_gain[None, :], 1)
    fgain = jnp.pad(ffn_gain, (0, pad))[None, :]
    tables = rope_tables(ctx * rows + jnp.arange(rows, dtype=jnp.int32))
    order = ctx ^ jnp.arange(4, dtype=jnp.int32)
    counts = jnp.clip(lengths[:, None] - rows * order[None, :], 0, rows)
    valid = jnp.concatenate([counts[:, 0], tp.astype(jnp.int32)[None]])
    all_counts = counts.reshape(images * 4)

    act = whole(rows, width)
    act_half = whole(rows, half)
    act_ff = whole(rows, ffp)
    line = whole(1, width)
    line_ff = whole(1, ffp)
    rope_spec = whole(3, rows, LANES)
    qkv_spec = whole(3, width, half)
    pair_half = pl.BlockSpec((rows, LANES), lambda i: (0, i))
    pair_kv = pl.BlockSpec((rows, 2 * LANES), lambda i: (0, i))
    pair_kv2 = pl.BlockSpec((2, rows, 2 * LANES), lambda i: (0, 0, i))
    pair_line = pl.BlockSpec((1, 1, 2 * rows), lambda i: (i, 0, 0))
    block_mb = rows * width

    st = [dict() for _ in range(images)]
    for i in range(images):
        s = st[i]
        s["h1"], s["q"], s["kv"] = call(
            qkv_kernel,
            (shape(rows, width), shape(rows, half), shape(rows, 2 * half)),
            [image_of(i, rows, width), line, qkv_spec, rope_spec],
            [act, act_half, whole(rows, 2 * half)],
            name="qkv",
            mib=14,
            flops=2 * rows * width * 3 * half,
            moved=6 * width * half + 8 * block_mb,
        )(tokens, ln1, full_qkv, tables)
        s["kvc"] = in_hbm(near(s["kv"]))
        s["kvf"] = far(s["kv"])
        s["q"] = in_hbm(s["q"])
    for i in range(images):
        s = st[i]
        if i == images - 1:
            s["kvf"], st[0]["o"] = lax.optimization_barrier((s["kvf"], st[0]["o"]))
        s["kvx"] = in_hbm(near(s["kvf"]))
        s["kvf"], s["kv"] = in_hbm(s["kvf"]), in_hbm(s["kv"])
        s["o"], s["lse"] = call(
            functools.partial(attend_kernel, image=i),
            (shape(rows, half), shape(half // LANES, 1, 2 * rows, dtype=F32)),
            [SMEM, pair_half] + [pair_kv] * 4,
            [pair_half, pair_line],
            [
                pltpu.VMEM((1, 2 * rows), F32),
                pltpu.VMEM((1, 2 * rows), F32),
                pltpu.VMEM((LANES, 2 * rows), F32),
            ],
            name="attend",
            mib=8,
            grid=half // LANES,
            flops=16 * rows * 4 * rows * half,
            moved=12 * block_mb,
        )(all_counts, s["q"], s["kv"], s["kvc"], s["kvf"], s["kvx"])
        s["o"] = in_hbm(s["o"])
        s["ox"] = in_hbm(swap(s["o"]))

    def each(*dims):
        return pl.BlockSpec((1,) + dims, lambda i: (i,) + (0,) * len(dims))

    x1, h2, gate, up, dm, attn_in, stats = call(
        middle_kernel,
        (
            shape(images, rows, width, dtype=F32),
            shape(images, rows, width),
            shape(images, rows, ffp),
            shape(images, rows, ffp),
            shape(images, rows, ffp),
            shape(images, rows, half),
            shape(images, 8, 384, dtype=F32),
        ),
        [SMEM, each(rows, width), each(rows, width)] + [act_half] * 6 + [line, line, line_ff, HBM],
        [
            each(rows, width), each(rows, width), each(rows, ffp), each(rows, ffp), each(rows, ffp),
            each(rows, half), each(8, 384),
        ],
        [
            pltpu.VMEM((width, width), BF),
            pltpu.VMEM((width, ffp), BF),
            pltpu.VMEM((width, ffp), BF),
            pltpu.VMEM((width, ffp), BF),
            pltpu.VMEM((rows, width), BF),
            pltpu.VMEM((rows, width), BF),
            pltpu.VMEM((384, LANES), F32),
            pltpu.SemaphoreType.DMA((4,)),
        ],
        name="middle",
        mib=36,
        grid=images,
        flops=2 * images * rows * width * (width + 3 * ffp),
        moved=2 * width * (width + 3 * ffp) + images * (12 * block_mb + 6 * rows * ffp),
    )(valid, tokens, cotangent, *[s["o"] for s in st], *[s["ox"] for s in st], again, ln2, fgain, rest)
    stats_x = swap(stats)
    for i in range(images):
        s = st[i]
        s["m"], s["dg"], s["du"], s["out"], s["dh2"], s["dffn"] = call(
            functools.partial(ffn_kernel, total=ff_total),
            (
                shape(rows, ffp),
                shape(rows, ffp),
                shape(rows, ffp),
                shape(rows, width),
                shape(rows, width),
                shape(1, ffp, dtype=F32),
            ),
            [image_of(i, 8, 384)] * 2 + [image_of(i, rows, ffp)] * 3 + [line_ff, HBM],
            [act_ff, act_ff, act_ff, act, act, line_ff],
            [
                pltpu.VMEM((width, ffp), BF),
                pltpu.VMEM((width, ffp), BF),
                pltpu.VMEM((width, ffp), BF),
                pltpu.VMEM((LANES, 384), F32),
                pltpu.SemaphoreType.DMA((3,)),
            ],
            name="ffn",
            mib=26,
            flops=2 * rows * width * 3 * ffp,
            moved=6 * width * ffp + 12 * rows * ffp + 4 * block_mb,
        )(stats, stats_x, gate, up, dm, fgain, rest)
        s["dh2x"] = swap(s["dh2"])
    def weight_grads(groups, tag, split=None):
        plan = [(masked, len(left), [len(right) for right in rights]) for masked, left, rights in groups]
        flat = [v for _, left, rights in groups for v in left + [w for right in rights for w in right]]
        columns = sum(right[0].shape[-1] for _, _, rights in groups for right in rights)
        return call(
            functools.partial(grads_kernel, plan=plan, split=split),
            shape(width, columns) if split is None else (shape(width // 2, columns),) * 2,
            [SMEM] + [whole(*v.shape) for v in flat],
            ANY if split is None else (ANY, ANY),
            [
                pltpu.VMEM((width, images * rows), BF),
                pltpu.VMEM((width, columns), BF),
                pltpu.SemaphoreType.DMA((len(groups) if split is None else 4 * split[0],)),
            ],
            name=tag,
            flops=2 * images * rows * width * columns,
            moved=4 * width * columns,
            mib=40 if columns > 2 * width else 26,
        )(jnp.concatenate([counts[:, 0], (ctx % 2).astype(jnp.int32)[None]]), *flat)

    def of(key):
        return [s[key] for s in st]

    grads_ffn = weight_grads(
        [(False, [h2], [of("dg"), of("du")]), (True, [cotangent], [of("m")])], "grads_ffn"
    )
    def norm_back(i):
        s = st[i]
        s["dx"], s["dab"], s["do"], s["dln2"], s["dattn"] = call(
            functools.partial(attn_norm_back_kernel, image=i),
            (
                shape(rows, width, dtype=F32),
                shape(rows, width),
                shape(rows, half),
                shape(1, width, dtype=F32),
                shape(1, half, dtype=F32),
            ),
            [SMEM, act, act, image_of(i, rows, width), image_of(i, rows, width), line, act_half, act_half, line, HBM],
            [act, act, act_half, line, whole(1, half)],
            [
                pltpu.VMEM((width, width), BF),
                pltpu.VMEM((rows, width), BF),
                pltpu.VMEM((rows, width), F32),
                pltpu.VMEM((8, width), F32),
                pltpu.SemaphoreType.DMA((1,)),
            ],
            name="attn_norm_back",
            mib=18,
            flops=2 * rows * width * width,
            moved=2 * width * width + 16 * block_mb,
        )(valid, s["dh2"], s["dh2x"], x1, cotangent, ln2, s["o"], s["ox"], again, rest)

    def attention_back(i):
        s = st[i]
        s["dq"], s["keep"], s["send"] = call(
            functools.partial(attend_back_kernel, image=i),
            (shape(rows, half), shape(2, rows, 2 * half), shape(2, rows, 2 * half)),
            [SMEM, pair_half] + [pair_kv] * 4 + [pair_half, pair_half, pair_line, rope_spec],
            [pair_half, pair_kv2, pair_kv2],
            [pltpu.VMEM((LANES, 2 * rows), F32)],
            grid=half // LANES,
            name="attend_back",
            mib=12,
            flops=40 * rows * 4 * rows * half,
            moved=20 * block_mb,
        )(all_counts, s["q"], s["kv"], s["kvc"], s["kvf"], s["kvx"], s["o"], s["do"], s["lse"], tables)
        s["recv"] = near(s["send"])
        s["mid"] = (s["keep"][1].astype(F32) + s["recv"][1].astype(F32)).astype(BF)

    def qkv_back(i):
        s = st[i]
        s["dkv"], s["dh1"] = call(
            qkv_back_kernel,
            (shape(rows, 2 * half), shape(rows, width)),
            [
                pl.BlockSpec((1, rows, 2 * half), lambda i: (0, 0, 0)),
                pl.BlockSpec((1, rows, 2 * half), lambda i: (0, 0, 0)),
                whole(rows, 2 * half),
                act_half,
                rope_spec,
                qkv_spec,
            ],
            [whole(rows, 2 * half), act],
            name="qkv_back",
            mib=14,
            flops=2 * rows * width * 3 * half,
            moved=6 * width * half + 10 * block_mb,
        )(s["keep"], s["recv"], s["far"], s["dq"], tables, full_qkv)
        s["dh1x"] = swap(s["dh1"])

    def mixed_part(i, mixed):
        s = st[i]
        again_buf = [] if mixed is None else [mixed]
        mixed = call(
            mixed_kernel,
            shape(images, rows, width),
            [image_of(i, rows, width), act, act] + [ANY] * len(again_buf),
            image_of(i, rows, width),
            name="mixed",
            mib=12,
            moved=10 * block_mb,
            aliases={3: 0} if again_buf else None,
        )(x1, s["out"], s["outx"], *again_buf)
        return mixed

    def tokens_part(i, grad_tokens):
        s = st[i]
        again_buf = [] if grad_tokens is None else [grad_tokens]
        grad_tokens, s["dln1"] = call(
            tokens_back_kernel,
            (shape(images, rows, width), shape(1, width, dtype=F32)),
            [act, act, image_of(i, rows, width), line, act] + [ANY] * len(again_buf),
            [image_of(i, rows, width), line],
            name="tokens_back",
            mib=16,
            moved=12 * block_mb,
            aliases={5: 0} if again_buf else None,
        )(s["dh1"], s["dh1x"], tokens, ln1, s["dx"], *again_buf)
        return grad_tokens

    def tie(*values):
        return lax.optimization_barrier(values)

    mixed = grad_tokens = None
    norm_back(0)
    late = [st[1], st[2]]
    tied = tie(st[0]["do"], *[s["out"] for s in st], *[s["dh2x"] for s in late], grads_ffn)
    st[0]["do"], grads_ffn = tied[0], tied[-1]
    for i, s in enumerate(st):
        s["out"] = tied[1 + i]
        s["outx"] = swap(s["out"])
    for i, s in enumerate(late):
        s["dh2x"] = tied[1 + images + i]
    attention_back(0)
    norm_back(1)
    st[1]["do"], st[0]["mid"] = tie(st[1]["do"], st[0]["mid"])
    st[0]["far"] = far(st[0]["mid"])
    attention_back(1)
    norm_back(2)
    st[2]["do"], st[0]["far"] = tie(st[2]["do"], st[0]["far"])
    st[1]["far"] = far(st[1]["mid"])
    qkv_back(0)
    attention_back(2)
    st[2]["far"] = far(st[2]["mid"])
    qkv_back(1)
    st[2]["far"], st[1]["dkv"], st[0]["outx"], st[0]["dh1x"] = tie(
        st[2]["far"], st[1]["dkv"], st[0]["outx"], st[0]["dh1x"]
    )
    qkv_back(2)
    for i in range(images):
        mixed = mixed_part(i, mixed)
    for i in range(images):
        grad_tokens = tokens_part(i, grad_tokens)
    own_ffn = lax.psum_scatter(grads_ffn, both, scatter_dimension=0, tiled=True)

    def around(own):
        beyond = far(own)
        held = [own, near(own), beyond, near(beyond)]
        return jnp.concatenate([lax.select_n(ctx ^ at, *held) for at in range(4)], axis=0)

    send, keep = weight_grads(
        [(False, of("h1"), [of("dq"), of("dkv")]), (False, of("dab"), [[attn_in]])], "grads_qkv", split=(shards, part)
    )
    grads_qkv = (keep.astype(F32) + near(send).astype(F32)).astype(BF)
    grads_qkv, own_ffn = tie(grads_qkv, own_ffn)
    own_qkv = lax.psum_scatter(grads_qkv, ("shard", "far"), scatter_dimension=0, tiled=True)
    grad_pairs, grad_down = call(
        finish_kernel,
        (shape(ff, 2, depth, dtype=F32), shape(ff, depth, dtype=F32)),
        [whole(depth, 3 * ffp)],
        [whole(ff, 2, depth), whole(ff, depth)],
        name="finish",
        mib=20,
        moved=18 * ff * depth,
    )(around(own_ffn))

    def everywhere(value):
        value = value + near(value)
        value = value + far(value)
        step = 1
        while step < shards:
            value = value + lax.ppermute(value, "shard", pair_perm(shards, step))
            step *= 2
        return value

    def gain(name):
        return sum(s[name] for s in st)[0]

    packed = everywhere(jnp.concatenate([gain("dffn"), gain("dln2"), gain("dattn")]))
    gain_ffn = packed[:ff]
    gain_ln2 = packed[ffp : ffp + width]
    gain_attn = packed[ffp + width :]
    gain_ln1 = everywhere(gain("dln1"))
    own_qkv, grad_tokens, mixed, gain_ln1, gain_ffn, grad_pairs, grad_down = tie(
        own_qkv, grad_tokens, mixed, gain_ln1, gain_ffn, grad_pairs, grad_down
    )
    grad_pairs = jnp.transpose(grad_pairs, (1, 2, 0))
    sum_qkv = lax.all_gather(own_qkv[:, : 3 * half], pairs_of, axis=0, tiled=True).astype(F32)
    grad_proj = around(own_qkv[:, 3 * half :]).astype(F32).T
    grad_qkv = jnp.stack([sum_qkv[:, j * half : (j + 1) * half] for j in range(3)])

    return (
        mixed,
        grad_tokens,
        gain_ln1,
        grad_qkv,
        gain_attn,
        grad_proj,
        gain_ln2,
        grad_pairs,
        gain_ffn,
        grad_down,
    )


def solution(mesh):
    size = dict(mesh.shape)
    mesh = Mesh(
        mesh.devices.reshape(size["shard"], size["ctx"] // 2, 2, size["tp"]), ("shard", "far", "near", "tp")
    )
    tokens = P("shard", ("far", "near"), None)
    matrix = P(None, "shard", "tp")
    flipped = P("tp", "shard")
    return jax.shard_map(
        local,
        mesh=mesh,
        in_specs=(
            tokens, tokens, P("shard"), P(), matrix, P("tp"), flipped, P(), matrix, P("tp"), flipped,
        ),
        out_specs=(tokens, tokens, P(), matrix, P("tp"), flipped, P(), matrix, P("tp"), flipped),
        check_vma=False,
    )
```

```python
import functools
import math

import jax
import jax.numpy as jnp
from jax import lax
from jax.experimental import pallas as pl
from jax.experimental.pallas import tpu as pltpu
from jax.sharding import Mesh, PartitionSpec as P

HEAD = 64
GRID = 32
LANES = 128
EPS = 1e-06
BF = jnp.bfloat16
F32 = jnp.float32
TAIL = 80


def dot_nn(a, b):
    return lax.dot_general(a, b, (((1,), (0,)), ((), ())), preferred_element_type=F32)


def dot_nt(a, b):
    return lax.dot_general(a, b, (((1,), (1,)), ((), ())), preferred_element_type=F32)


def dot_tn(a, b):
    return lax.dot_general(a, b, (((0,), (0,)), ((), ())), preferred_element_type=F32)


def tiles(width, step=256):
    return [(at, min(step, width - at)) for at in range(0, width, step)]


def pair_perm(size, flip):
    return [(at, at ^ flip) for at in range(size)]


def rope_tables(positions):
    quarter = HEAD // 4
    place = jnp.maximum(positions - 1, 0)
    row_pos = (place // GRID).astype(F32)
    col_pos = (place % GRID).astype(F32)
    frequency = jnp.exp(jnp.arange(quarter).astype(F32) * (-math.log(10000.0) / quarter))
    row_angle = row_pos[:, None] * frequency[None, :]
    col_angle = col_pos[:, None] * frequency[None, :]
    cr, sr, cc, sc = jnp.cos(row_angle), jnp.sin(row_angle), jnp.cos(col_angle), jnp.sin(col_angle)
    zero = jnp.zeros_like(sr)
    cos = jnp.concatenate([cr, cr, cc, cc], axis=1)
    up = jnp.concatenate([-sr, zero, -sc, zero], axis=1)
    down = jnp.concatenate([zero, sr, zero, sc], axis=1)
    return jnp.stack([jnp.concatenate([t, t], axis=1) for t in (cos, up, down)])


def turn(values, tables_ref, sign):
    shift = HEAD // 4
    return values * tables_ref[0] + sign * (
        pltpu.roll(values, LANES - shift, 1) * tables_ref[1]
        + pltpu.roll(values, shift, 1) * tables_ref[2]
    )


def row_norm(values, width):
    mean = jnp.sum(values, axis=1, keepdims=True) * (1.0 / width)
    centred = values - mean
    inv = lax.rsqrt(jnp.sum(centred * centred, axis=1, keepdims=True) * (1.0 / width) + EPS)
    return centred * inv, inv


def row_norm_back(scaled, normed, inv, width):
    first = jnp.sum(scaled, axis=1, keepdims=True) * (1.0 / width)
    second = jnp.sum(scaled * normed, axis=1, keepdims=True) * (1.0 / width)
    return inv * (scaled - first - normed * second)


def valid_rows(values, count):
    rows = lax.broadcasted_iota(jnp.int32, values.shape, 0)
    return jnp.where(rows < count, values, jnp.zeros_like(values))


def qkv_kernel(x_ref, gain_ref, w_ref, rope_ref, h_ref, q_ref, kv_ref):
    x = x_ref[0].astype(F32)
    normed, _ = row_norm(x, x.shape[1])
    h_ref[...] = (normed * gain_ref[...]).astype(BF)
    width = w_ref.shape[2]
    h = h_ref[...]
    for at, size in tiles(width):
        q = dot_nn(h, w_ref[0, :, at : at + size])
        k = dot_nn(h, w_ref[1, :, at : at + size])
        v = dot_nn(h, w_ref[2, :, at : at + size])
        for off in range(0, size, LANES):
            cols = slice(off, off + LANES)
            q_ref[:, at + off : at + off + LANES] = (
                turn(q[:, cols], rope_ref, 1.0) * HEAD ** (-0.5)
            ).astype(BF)
            pair = 2 * (at + off)
            kv_ref[:, pair : pair + LANES] = turn(k[:, cols], rope_ref, 1.0).astype(BF)
            kv_ref[:, pair + LANES : pair + 2 * LANES] = v[:, cols].astype(BF)


def split_pair(values):
    lane = lax.broadcasted_iota(jnp.int32, values.shape, 1)
    zero = jnp.zeros_like(values)
    return jnp.concatenate(
        [jnp.where(lane < HEAD, values, zero), jnp.where(lane >= HEAD, values, zero)], axis=0
    )


def join_pair(values):
    rows = values.shape[0] // 2
    lane = lax.broadcasted_iota(jnp.int32, (rows, values.shape[1]), 1)
    return jnp.where(lane < HEAD, values[:rows], values[rows:])


def attend_kernel(n_ref, q_ref, kv0, kv1, kv2, kv3, o_ref, lse_ref, m_s, l_s, acc_s, *, image):
    qb = split_pair(q_ref[...])
    m_s[...] = jnp.full(m_s.shape, -1e30, F32)
    l_s[...] = jnp.zeros(l_s.shape, F32)
    acc_s[...] = jnp.zeros(acc_s.shape, F32)

    def step(kv_ref, count, size):
        s = dot_nt(kv_ref[:size, :LANES], qb)
        if count is not None:
            key = lax.broadcasted_iota(jnp.int32, s.shape, 0)
            s = jnp.where(key < count, s, -1e30)
        m_old = m_s[...]
        m_new = jnp.maximum(m_old, jnp.max(s, axis=0, keepdims=True))
        scale = jnp.exp(m_old - m_new)
        e = jnp.exp(s - m_new)
        m_s[...] = m_new
        l_s[...] = l_s[...] * scale + jnp.sum(e, axis=0, keepdims=True)
        acc_s[...] = acc_s[...] * scale + dot_tn(kv_ref[:size, LANES:], e.astype(BF))

    for at, kv_ref in enumerate((kv0, kv1, kv2, kv3)):
        count = n_ref[4 * image + at]

        @pl.when(count >= kv_ref.shape[0])
        def _():
            step(kv_ref, None, kv_ref.shape[0])

        @pl.when((count > TAIL) & (count < kv_ref.shape[0]))
        def _():
            step(kv_ref, count, kv_ref.shape[0])

        @pl.when((count > 0) & (count <= TAIL))
        def _():
            step(kv_ref, count, TAIL)

    total = l_s[...]
    out = acc_s[...] * (1.0 / total)
    o_ref[...] = join_pair(out.T).astype(BF)
    lse_ref[0] = m_s[...] + jnp.log(total)


def attend_back_kernel(
    n_ref, q_ref, kv0, kv1, kv2, kv3, o_ref, do_ref, lse_ref, rope_ref, dq_ref, keep_ref, send_ref, dq_s, *, image
):
    rows = q_ref.shape[0]
    qb = split_pair(q_ref[...])
    do = do_ref[...]
    dob = split_pair(do)
    prod = split_pair(do.astype(F32) * o_ref[...].astype(F32))
    delta = jnp.sum(prod.T, axis=0, keepdims=True)
    lse = lse_ref[0]
    dq_s[...] = jnp.zeros(dq_s.shape, F32)

    def step(kv_ref, out_ref, slot, count, size):
        k = kv_ref[:size, :LANES]
        s = dot_nt(k, qb)
        p = jnp.exp(s - lse)
        if count is not None:
            key = lax.broadcasted_iota(jnp.int32, s.shape, 0)
            p = jnp.where(key < count, p, 0.0)
        dp = dot_nt(kv_ref[:size, LANES:], dob)
        ds = (p * (dp - delta)).astype(BF)
        out_ref[slot, :size, LANES:] = dot_nn(p.astype(BF), dob).astype(BF)
        out_ref[slot, :size, :LANES] = dot_nn(ds, qb).astype(BF)
        dq_s[...] += dot_tn(k, ds)
        if size < rows:
            out_ref[slot, size:, :] = jnp.zeros((rows - size, 2 * LANES), BF)

    for at, kv_ref in enumerate((kv0, kv1, kv2, kv3)):
        count = n_ref[4 * image + at]
        out_ref = (keep_ref, send_ref)[at % 2]
        slot = at // 2

        @pl.when(count >= kv_ref.shape[0])
        def _():
            step(kv_ref, out_ref, slot, None, kv_ref.shape[0])

        @pl.when((count > TAIL) & (count < kv_ref.shape[0]))
        def _():
            step(kv_ref, out_ref, slot, count, kv_ref.shape[0])

        @pl.when((count > 0) & (count <= TAIL))
        def _():
            step(kv_ref, out_ref, slot, count, TAIL)

        @pl.when(count <= 0)
        def _():
            out_ref[slot] = jnp.zeros((rows, 2 * LANES), BF)

    dq = join_pair(dq_s[...].T) * HEAD ** (-0.5)
    dq_ref[...] = turn(dq, rope_ref, -1.0).astype(BF)


def merge_heads(dst, own_ref, other_ref, tp, half):
    dst[:, pl.ds(pl.multiple_of(tp * half, half), half)] = own_ref[...]
    dst[:, pl.ds(pl.multiple_of((1 - tp) * half, half), half)] = other_ref[...]


def middle_kernel(
    sc_ref, x_ref, cot_ref, own_ref0, own_ref1, own_ref2, other_ref0, other_ref1, other_ref2,
    again_ref, ln2_ref, fgain_ref, w_ref,
    x1_ref, h2_ref, g_ref, u_ref, dm_ref, a_ref, st_ref,
    pj_s, gw_s, uw_s, dw_s, o_s, a_s, st_s, sem,
):
    image = pl.program_id(0)
    width = x_ref.shape[2]
    half = own_ref0.shape[1]
    rows = own_ref0.shape[0]
    ff = g_ref.shape[2]
    loads = [
        pltpu.make_async_copy(w_ref.at[:, pl.ds(0, width)], pj_s, sem.at[0]),
        pltpu.make_async_copy(w_ref.at[:, pl.ds(width + ff, ff)], gw_s, sem.at[1]),
        pltpu.make_async_copy(w_ref.at[:, pl.ds(width + 2 * ff, ff)], uw_s, sem.at[2]),
        pltpu.make_async_copy(w_ref.at[:, pl.ds(width, ff)], dw_s, sem.at[3]),
    ]

    @pl.when(image == 0)
    def _():
        for load in loads:
            load.start()

    tp = sc_ref[3]
    for at, (own_ref, other_ref) in enumerate(
        ((own_ref0, other_ref0), (own_ref1, other_ref1), (own_ref2, other_ref2))
    ):

        @pl.when(image == at)
        def _():
            merge_heads(o_s, own_ref, other_ref, tp, half)

    normed, _ = row_norm(o_s[...].astype(F32), width)
    a_s[...] = (normed * again_ref[...]).astype(BF)
    a_ref[0] = a_s[:, pl.ds(pl.multiple_of(tp * half, half), half)]

    @pl.when(image == 0)
    def _():
        loads[0].wait()

    a = a_s[...]
    for at, size in tiles(width):
        x1_ref[0, :, at : at + size] = x_ref[0, :, at : at + size].astype(F32) + dot_nt(
            a, pj_s[at : at + size, :]
        )
    normed, _ = row_norm(x1_ref[0], width)
    h2_ref[0] = (normed * ln2_ref[...]).astype(BF)
    h2 = h2_ref[0]
    dyb = valid_rows(cot_ref[0], sc_ref[image])

    @pl.when(image == 0)
    def _():
        for load in loads[1:]:
            load.wait()

    sums = [jnp.zeros((rows, LANES), F32) for _ in range(4)]
    for at, size in tiles(ff):
        span = slice(at, at + size)
        g = dot_nn(h2, gw_s[:, span]).astype(BF)
        u = dot_nn(h2, uw_s[:, span]).astype(BF)
        dm = dot_nn(dyb, dw_s[:, span]).astype(BF)
        g_ref[0, :, span] = g
        u_ref[0, :, span] = u
        dm_ref[0, :, span] = dm
        gf = g.astype(F32)
        z = gf * jax.nn.sigmoid(gf) * u.astype(F32)
        e = dm.astype(F32) * fgain_ref[:, span]
        for off in range(0, size, LANES):
            zo = z[:, off : off + LANES]
            eo = e[:, off : off + LANES]
            sums = [sums[0] + zo, sums[1] + zo * zo, sums[2] + eo, sums[3] + eo * zo]
    lane = lax.broadcasted_iota(jnp.int32, (rows, LANES), 1)
    packed = jnp.zeros((rows, LANES), F32)
    for slot, part in enumerate(sums):
        packed = jnp.where(lane == slot, jnp.sum(part, axis=1, keepdims=True), packed)
    st_s[...] = jnp.zeros(st_s.shape, F32)
    st_s[:rows, :] = packed
    st_ref[0] = st_s[...].T[:8, :]


def ffn_kernel(
    sa_ref, sb_ref, g_ref, u_ref, dm_ref, fgain_ref, w_ref,
    m_ref, dg_ref, du_ref, out_ref, dh_ref, dgain_ref,
    gw_s, uw_s, dw_s, st_s, sem, *, total,
):
    _, rows, ff = g_ref.shape
    width = w_ref.shape[0]
    loads = [
        pltpu.make_async_copy(w_ref.at[:, pl.ds(width + ff, ff)], gw_s, sem.at[0]),
        pltpu.make_async_copy(w_ref.at[:, pl.ds(width + 2 * ff, ff)], uw_s, sem.at[1]),
        pltpu.make_async_copy(w_ref.at[:, pl.ds(width, ff)], dw_s, sem.at[2]),
    ]
    for load in loads:
        load.start()
    st_s[...] = jnp.zeros(st_s.shape, F32)
    st_s[:8, :] = sa_ref[0] + sb_ref[0]
    st = st_s[...].T[:rows, :]
    lane = lax.broadcasted_iota(jnp.int32, st.shape, 1)

    def column(slot):
        return jnp.sum(jnp.where(lane == slot, st, 0.0), axis=1, keepdims=True) * (1.0 / total)

    mean = column(0)
    inv = lax.rsqrt(jnp.maximum(column(1) - mean * mean, 0.0) + EPS)
    first = column(2)
    second = inv * (column(3) - mean * first)
    for at, size in tiles(ff):
        span = slice(at, at + size)
        g = g_ref[0, :, span].astype(F32)
        u = u_ref[0, :, span].astype(F32)
        dm = dm_ref[0, :, span].astype(F32)
        gain = fgain_ref[:, span]
        sig = jax.nn.sigmoid(g)
        act = g * sig
        normed = (act * u - mean) * inv
        m_ref[:, span] = (normed * gain).astype(BF)
        dgain_ref[:, span] = jnp.sum(dm * normed, axis=0, keepdims=True)
        dz = inv * (dm * gain - first - normed * second)
        dg_ref[:, span] = (dz * u * sig * (1.0 + g * (1.0 - sig))).astype(BF)
        du_ref[:, span] = (dz * act).astype(BF)
    loads[0].wait()
    loads[1].wait()
    dg = dg_ref[...]
    du = du_ref[...]
    for at, size in tiles(width):
        dh_ref[:, at : at + size] = (
            dot_nt(dg, gw_s[at : at + size, :]) + dot_nt(du, uw_s[at : at + size, :])
        ).astype(BF)
    loads[2].wait()
    m = m_ref[...]
    for at, size in tiles(width):
        out_ref[:, at : at + size] = dot_nt(m, dw_s[at : at + size, :]).astype(BF)


def attn_norm_back_kernel(
    sc_ref, dha_ref, dhb_ref, x1_ref, cot_ref, ln2_ref, own_ref, other_ref, again_ref, w_ref,
    dx_ref, dab_ref, do_ref, dln2_ref, dgain_ref,
    pj_s, o_s, e_s, f_s, sem, *, image,
):
    width = x1_ref.shape[2]
    half = own_ref.shape[1]
    load = pltpu.make_async_copy(w_ref.at[:, pl.ds(0, width)], pj_s, sem.at[0])
    load.start()
    tp = sc_ref[3]
    dh = dha_ref[...].astype(F32) + dhb_ref[...].astype(F32)
    normed, inv = row_norm(x1_ref[0], width)
    dln2_ref[...] = jnp.sum(dh * normed, axis=0, keepdims=True)
    dy = valid_rows(cot_ref[0].astype(F32), sc_ref[image])
    dx = dy + row_norm_back(dh * ln2_ref[...], normed, inv, width)
    dx_ref[...] = dx
    dab_ref[...] = dx.astype(BF)
    merge_heads(o_s, own_ref, other_ref, tp, half)
    normed, inv = row_norm(o_s[...].astype(F32), width)
    load.wait()
    dab = dab_ref[...]
    for at, size in tiles(width):
        da = dot_nn(dab, pj_s[:, at : at + size])
        e_s[:, at : at + size] = da
    da = e_s[...]
    f_s[...] = jnp.broadcast_to(jnp.sum(da * normed, axis=0, keepdims=True), f_s.shape)
    dgain_ref[...] = f_s[0:1, pl.ds(pl.multiple_of(tp * half, half), half)]
    e_s[...] = row_norm_back(da * again_ref[...], normed, inv, width)
    do_ref[...] = e_s[:, pl.ds(pl.multiple_of(tp * half, half), half)].astype(BF)


def qkv_back_kernel(keep_ref, recv_ref, far_ref, dq_ref, rope_ref, w_ref, dkv_ref, dh_ref):
    rows, half = dq_ref.shape
    total = keep_ref[0].astype(F32) + recv_ref[0].astype(F32) + far_ref[...].astype(F32)
    for at in range(0, half, LANES):
        pair = total[:, 2 * at : 2 * at + 2 * LANES]
        dkv_ref[:, at : at + LANES] = turn(pair[:, :LANES], rope_ref, -1.0).astype(BF)
        dkv_ref[:, half + at : half + at + LANES] = pair[:, LANES:].astype(BF)
    dq = dq_ref[...]
    dk = dkv_ref[:, :half]
    dv = dkv_ref[:, half:]
    for at, size in tiles(w_ref.shape[1]):
        span = slice(at, at + size)
        dh_ref[:, span] = (
            dot_nt(dq, w_ref[0, span, :]) + dot_nt(dk, w_ref[1, span, :]) + dot_nt(dv, w_ref[2, span, :])
        ).astype(BF)


def tokens_back_kernel(da_ref, db_ref, x_ref, gain_ref, dx_ref, *rest):
    out_ref, dgain_ref = rest[-2:]
    width = dx_ref.shape[1]
    dh = da_ref[...].astype(F32) + db_ref[...].astype(F32)
    normed, inv = row_norm(x_ref[0].astype(F32), width)
    dgain_ref[...] = jnp.sum(dh * normed, axis=0, keepdims=True)
    out_ref[0] = (dx_ref[...] + row_norm_back(dh * gain_ref[...], normed, inv, width)).astype(BF)


def mixed_kernel(x1_ref, pa_ref, pb_ref, *rest):
    out_ref = rest[-1]
    out_ref[0] = (x1_ref[0] + (pa_ref[...].astype(F32) + pb_ref[...].astype(F32))).astype(BF)


def finish_kernel(sum_ref, pairs_ref, down_ref):
    ff = down_ref.shape[0]
    ffp = sum_ref.shape[1] // 3
    for at in range(0, ff, LANES):
        size = min(LANES, ff - at)
        for slot in range(3):
            cols = slice(slot * ffp + at, slot * ffp + at + LANES)
            flipped = sum_ref[:, cols].astype(F32).T[:size]
            if slot < 2:
                pairs_ref[at : at + size, slot, :] = flipped
            else:
                down_ref[at : at + size, :] = flipped


def grads_kernel(n_ref, *refs, plan, split=None):
    outs = 1 if split is None else 2
    refs = list(refs)
    *out_refs, flip_s, out_s, sem = refs[-outs - 3 :]
    refs = refs[: -outs - 3]

    def take(count):
        mine = refs[:count]
        del refs[:count]
        return mine

    def joined(mine, cols):
        if len(mine) == 1:
            block = mine[0][:, :, cols]
            return block.reshape(block.shape[0] * block.shape[1], block.shape[2])
        return jnp.concatenate([ref[:, cols] for ref in mine], axis=0)

    copies = []
    column = 0
    for group, (masked, left, rights) in enumerate(plan):
        mine = take(left)
        if masked:
            parts = [valid_rows(mine[0][i], n_ref[i]) for i in range(mine[0].shape[0])]
            flip_s[...] = jnp.concatenate(parts, axis=0).T
        else:
            flip_s[...] = joined(mine, slice(None)).T
        flipped = flip_s[...]
        start = column
        for right in rights:
            mine = take(right)
            span = mine[0].shape[-1]
            for at, size in tiles(span):
                out_s[:, column + at : column + at + size] = dot_nn(
                    flipped, joined(mine, slice(at, at + size))
                ).astype(BF)
            column += span
        if split is None:
            copies.append(
                pltpu.make_async_copy(
                    out_s.at[:, pl.ds(start, column - start)],
                    out_refs[0].at[:, pl.ds(start, column - start)],
                    sem.at[group],
                )
            )
            copies[-1].start()
    if split is not None:
        shards, part = split
        low = n_ref[n_ref.shape[0] - 1]
        for block in range(2 * shards):
            for slot, parity in enumerate((1 - low, low)):
                row = pl.multiple_of((2 * block + parity) * part, part)
                copies.append(
                    pltpu.make_async_copy(
                        out_s.at[pl.ds(row, part), :],
                        out_refs[slot].at[pl.ds(block * part, part), :],
                        sem.at[2 * block + slot],
                    )
                )
                copies[-1].start()
    for copy in copies:
        copy.wait()


VMEM = pl.BlockSpec(memory_space=pltpu.VMEM)
SMEM = pl.BlockSpec(memory_space=pltpu.SMEM)
ANY = pl.BlockSpec(memory_space=pl.ANY)
HBM = pl.BlockSpec(memory_space=pltpu.HBM)


def shape(*dims, dtype=BF):
    return jax.ShapeDtypeStruct(dims, dtype)


def call(kernel, out_shape, in_specs, out_specs, scratch=(), name=None, flops=0, moved=0, aliases=None, mib=48, grid=1):
    return pl.pallas_call(
        kernel,
        out_shape=out_shape,
        in_specs=in_specs,
        out_specs=out_specs,
        grid=(grid,),
        scratch_shapes=list(scratch),
        input_output_aliases=aliases or {},
        name=name,
        cost_estimate=pl.CostEstimate(flops=flops // 16, bytes_accessed=moved // 16, transcendentals=0),
        compiler_params=pltpu.CompilerParams(vmem_limit_bytes=mib << 20),
    )


def whole(*dims):
    return pl.BlockSpec(dims, lambda i: (0,) * len(dims))


def image_of(index, rows, width):
    return pl.BlockSpec((1, rows, width), lambda i: (index, 0, 0))


def in_hbm(value):
    return pltpu.with_memory_space_constraint(value, pltpu.HBM)


def local(
    tokens, cotangent, lengths, ln1_gain, qkv_weight, attn_gain, proj_weight, ln2_gain, gate_up, ffn_gain, down_weight
):
    images, rows, width = tokens.shape
    half = attn_gain.shape[0]
    ff = ffn_gain.shape[0]
    ffp = -(-ff // LANES) * LANES
    pad = ffp - ff
    tp_size = lax.axis_size("tp")
    pairs_of = ("far", "near")
    ctx_size = lax.axis_size(pairs_of)
    ctx = lax.axis_index(pairs_of)
    tp = lax.axis_index("tp")
    ff_total = ff * tp_size
    both = ("shard", *pairs_of)
    swap_tp = pair_perm(tp_size, 1)
    swap_pair = pair_perm(2, 1)

    def swap(value):
        return lax.ppermute(value, "tp", swap_tp)

    def near(value):
        return lax.ppermute(value, "near", swap_pair)

    def far(value):
        return lax.ppermute(value, "far", swap_pair)

    def ordered(own, axis):
        other = swap(own)
        low = jnp.where(tp == 0, own, other)
        high = jnp.where(tp == 0, other, own)
        return jnp.concatenate([low, high], axis=axis)

    depth = qkv_weight.shape[1]
    part = depth // ctx_size
    first = ctx * part
    qkv_part = lax.dynamic_slice_in_dim(qkv_weight, first, part, axis=1)
    full_qkv = lax.all_gather(qkv_part, both, axis=1, tiled=True)
    proj_part = lax.dynamic_slice_in_dim(proj_weight, first, part, axis=1).T
    down_part = lax.dynamic_slice_in_dim(down_weight, first, part, axis=1).T
    pairs_part = lax.dynamic_slice_in_dim(gate_up, first, part, axis=1)
    shards = lax.axis_size("shard")
    rest_part = jnp.concatenate(
        [
            ordered(proj_part, 1),
            jnp.pad(down_part, ((0, 0), (0, pad))),
            jnp.pad(pairs_part[0], ((0, 0), (0, pad))),
            jnp.pad(pairs_part[1], ((0, 0), (0, pad))),
        ],
        axis=1,
    )
    rest = lax.all_gather(rest_part, both, axis=0, tiled=True)
    rest = pltpu.with_memory_space_constraint(rest, pltpu.HBM)

    ln1 = ln1_gain[None, :]
    ln2 = ln2_gain[None, :]
    again = ordered(attn_gain[None, :], 1)
    fgain = jnp.pad(ffn_gain, (0, pad))[None, :]
    tables = rope_tables(ctx * rows + jnp.arange(rows, dtype=jnp.int32))
    order = ctx ^ jnp.arange(4, dtype=jnp.int32)
    counts = jnp.clip(lengths[:, None] - rows * order[None, :], 0, rows)
    valid = jnp.concatenate([counts[:, 0], tp.astype(jnp.int32)[None]])
    all_counts = counts.reshape(images * 4)

    act = whole(rows, width)
    act_half = whole(rows, half)
    act_ff = whole(rows, ffp)
    line = whole(1, width)
    line_ff = whole(1, ffp)
    rope_spec = whole(3, rows, LANES)
    qkv_spec = whole(3, width, half)
    pair_half = pl.BlockSpec((rows, LANES), lambda i: (0, i))
    pair_kv = pl.BlockSpec((rows, 2 * LANES), lambda i: (0, i))
    pair_kv2 = pl.BlockSpec((2, rows, 2 * LANES), lambda i: (0, 0, i))
    pair_line = pl.BlockSpec((1, 1, 2 * rows), lambda i: (i, 0, 0))
    block_mb = rows * width

    st = [dict() for _ in range(images)]
    for i in range(images):
        s = st[i]
        s["h1"], s["q"], s["kv"] = call(
            qkv_kernel,
            (shape(rows, width), shape(rows, half), shape(rows, 2 * half)),
            [image_of(i, rows, width), line, qkv_spec, rope_spec],
            [act, act_half, whole(rows, 2 * half)],
            name="qkv",
            mib=10,
            flops=2 * rows * width * 3 * half,
            moved=6 * width * half + 8 * block_mb,
        )(tokens, ln1, full_qkv, tables)
        s["kvc"] = in_hbm(near(s["kv"]))
        s["kvf"] = far(s["kv"])
        s["q"] = in_hbm(s["q"])
    for i in range(images):
        s = st[i]
        if i == images - 1:
            s["kvf"], st[0]["o"] = lax.optimization_barrier((s["kvf"], st[0]["o"]))
        s["kvx"] = in_hbm(near(s["kvf"]))
        s["kvf"], s["kv"] = in_hbm(s["kvf"]), in_hbm(s["kv"])
        s["o"], s["lse"] = call(
            functools.partial(attend_kernel, image=i),
            (shape(rows, half), shape(half // LANES, 1, 2 * rows, dtype=F32)),
            [SMEM, pair_half] + [pair_kv] * 4,
            [pair_half, pair_line],
            [
                pltpu.VMEM((1, 2 * rows), F32),
                pltpu.VMEM((1, 2 * rows), F32),
                pltpu.VMEM((LANES, 2 * rows), F32),
            ],
            name="attend",
            mib=6,
            grid=half // LANES,
            flops=16 * rows * 4 * rows * half,
            moved=12 * block_mb,
        )(all_counts, s["q"], s["kv"], s["kvc"], s["kvf"], s["kvx"])
        s["o"] = in_hbm(s["o"])
        s["ox"] = in_hbm(swap(s["o"]))

    def each(*dims):
        return pl.BlockSpec((1,) + dims, lambda i: (i,) + (0,) * len(dims))

    x1, h2, gate, up, dm, attn_in, stats = call(
        middle_kernel,
        (
            shape(images, rows, width, dtype=F32),
            shape(images, rows, width),
            shape(images, rows, ffp),
            shape(images, rows, ffp),
            shape(images, rows, ffp),
            shape(images, rows, half),
            shape(images, 8, 384, dtype=F32),
        ),
        [SMEM, each(rows, width), each(rows, width)] + [act_half] * 6 + [line, line, line_ff, HBM],
        [
            each(rows, width), each(rows, width), each(rows, ffp), each(rows, ffp), each(rows, ffp),
            each(rows, half), each(8, 384),
        ],
        [
            pltpu.VMEM((width, width), BF),
            pltpu.VMEM((width, ffp), BF),
            pltpu.VMEM((width, ffp), BF),
            pltpu.VMEM((width, ffp), BF),
            pltpu.VMEM((rows, width), BF),
            pltpu.VMEM((rows, width), BF),
            pltpu.VMEM((384, LANES), F32),
            pltpu.SemaphoreType.DMA((4,)),
        ],
        name="middle",
        mib=30,
        grid=images,
        flops=2 * images * rows * width * (width + 3 * ffp),
        moved=2 * width * (width + 3 * ffp) + images * (12 * block_mb + 6 * rows * ffp),
    )(valid, tokens, cotangent, *[s["o"] for s in st], *[s["ox"] for s in st], again, ln2, fgain, rest)
    stats_x = swap(stats)
    for i in range(images):
        s = st[i]
        s["m"], s["dg"], s["du"], s["out"], s["dh2"], s["dffn"] = call(
            functools.partial(ffn_kernel, total=ff_total),
            (
                shape(rows, ffp),
                shape(rows, ffp),
                shape(rows, ffp),
                shape(rows, width),
                shape(rows, width),
                shape(1, ffp, dtype=F32),
            ),
            [image_of(i, 8, 384)] * 2 + [image_of(i, rows, ffp)] * 3 + [line_ff, HBM],
            [act_ff, act_ff, act_ff, act, act, line_ff],
            [
                pltpu.VMEM((width, ffp), BF),
                pltpu.VMEM((width, ffp), BF),
                pltpu.VMEM((width, ffp), BF),
                pltpu.VMEM((LANES, 384), F32),
                pltpu.SemaphoreType.DMA((3,)),
            ],
            name="ffn",
            mib=20,
            flops=2 * rows * width * 3 * ffp,
            moved=6 * width * ffp + 12 * rows * ffp + 4 * block_mb,
        )(stats, stats_x, gate, up, dm, fgain, rest)
        s["dh2x"] = swap(s["dh2"])
    def weight_grads(groups, tag, split=None):
        plan = [(masked, len(left), [len(right) for right in rights]) for masked, left, rights in groups]
        flat = [v for _, left, rights in groups for v in left + [w for right in rights for w in right]]
        columns = sum(right[0].shape[-1] for _, _, rights in groups for right in rights)
        return call(
            functools.partial(grads_kernel, plan=plan, split=split),
            shape(width, columns) if split is None else (shape(width // 2, columns),) * 2,
            [SMEM] + [whole(*v.shape) for v in flat],
            ANY if split is None else (ANY, ANY),
            [
                pltpu.VMEM((width, images * rows), BF),
                pltpu.VMEM((width, columns), BF),
                pltpu.SemaphoreType.DMA((len(groups) if split is None else 4 * split[0],)),
            ],
            name=tag,
            flops=2 * images * rows * width * columns,
            moved=4 * width * columns,
            mib=40 if columns > 2 * width else 26,
        )(jnp.concatenate([counts[:, 0], (ctx % 2).astype(jnp.int32)[None]]), *flat)

    def of(key):
        return [s[key] for s in st]

    grads_ffn = weight_grads(
        [(False, [h2], [of("dg"), of("du")]), (True, [cotangent], [of("m")])], "grads_ffn"
    )
    def norm_back(i):
        s = st[i]
        s["dx"], s["dab"], s["do"], s["dln2"], s["dattn"] = call(
            functools.partial(attn_norm_back_kernel, image=i),
            (
                shape(rows, width, dtype=F32),
                shape(rows, width),
                shape(rows, half),
                shape(1, width, dtype=F32),
                shape(1, half, dtype=F32),
            ),
            [SMEM, act, act, image_of(i, rows, width), image_of(i, rows, width), line, act_half, act_half, line, HBM],
            [act, act, act_half, line, whole(1, half)],
            [
                pltpu.VMEM((width, width), BF),
                pltpu.VMEM((rows, width), BF),
                pltpu.VMEM((rows, width), F32),
                pltpu.VMEM((8, width), F32),
                pltpu.SemaphoreType.DMA((1,)),
            ],
            name="attn_norm_back",
            mib=14,
            flops=2 * rows * width * width,
            moved=2 * width * width + 16 * block_mb,
        )(valid, s["dh2"], s["dh2x"], x1, cotangent, ln2, s["o"], s["ox"], again, rest)

    def attention_back(i):
        s = st[i]
        s["dq"], s["keep"], s["send"] = call(
            functools.partial(attend_back_kernel, image=i),
            (shape(rows, half), shape(2, rows, 2 * half), shape(2, rows, 2 * half)),
            [SMEM, pair_half] + [pair_kv] * 4 + [pair_half, pair_half, pair_line, rope_spec],
            [pair_half, pair_kv2, pair_kv2],
            [pltpu.VMEM((LANES, 2 * rows), F32)],
            grid=half // LANES,
            name="attend_back",
            mib=9,
            flops=40 * rows * 4 * rows * half,
            moved=20 * block_mb,
        )(all_counts, s["q"], s["kv"], s["kvc"], s["kvf"], s["kvx"], s["o"], s["do"], s["lse"], tables)
        s["recv"] = near(s["send"])
        s["mid"] = (s["keep"][1].astype(F32) + s["recv"][1].astype(F32)).astype(BF)

    def qkv_back(i):
        s = st[i]
        s["dkv"], s["dh1"] = call(
            qkv_back_kernel,
            (shape(rows, 2 * half), shape(rows, width)),
            [
                pl.BlockSpec((1, rows, 2 * half), lambda i: (0, 0, 0)),
                pl.BlockSpec((1, rows, 2 * half), lambda i: (0, 0, 0)),
                whole(rows, 2 * half),
                act_half,
                rope_spec,
                qkv_spec,
            ],
            [whole(rows, 2 * half), act],
            name="qkv_back",
            mib=10,
            flops=2 * rows * width * 3 * half,
            moved=6 * width * half + 10 * block_mb,
        )(s["keep"], s["recv"], s["far"], s["dq"], tables, full_qkv)
        s["dh1x"] = swap(s["dh1"])

    def mixed_part(i, mixed):
        s = st[i]
        again_buf = [] if mixed is None else [mixed]
        mixed = call(
            mixed_kernel,
            shape(images, rows, width),
            [image_of(i, rows, width), act, act] + [ANY] * len(again_buf),
            image_of(i, rows, width),
            name="mixed",
            mib=12,
            moved=10 * block_mb,
            aliases={3: 0} if again_buf else None,
        )(x1, s["out"], s["outx"], *again_buf)
        return mixed

    def tokens_part(i, grad_tokens):
        s = st[i]
        again_buf = [] if grad_tokens is None else [grad_tokens]
        grad_tokens, s["dln1"] = call(
            tokens_back_kernel,
            (shape(images, rows, width), shape(1, width, dtype=F32)),
            [act, act, image_of(i, rows, width), line, act] + [ANY] * len(again_buf),
            [image_of(i, rows, width), line],
            name="tokens_back",
            mib=16,
            moved=12 * block_mb,
            aliases={5: 0} if again_buf else None,
        )(s["dh1"], s["dh1x"], tokens, ln1, s["dx"], *again_buf)
        return grad_tokens

    def tie(*values):
        return lax.optimization_barrier(values)

    mixed = grad_tokens = None
    norm_back(0)
    late = [st[1], st[2]]
    tied = tie(st[0]["do"], *[s["out"] for s in st], *[s["dh2x"] for s in late], grads_ffn)
    st[0]["do"], grads_ffn = tied[0], tied[-1]
    for i, s in enumerate(st):
        s["out"] = tied[1 + i]
        s["outx"] = swap(s["out"])
    for i, s in enumerate(late):
        s["dh2x"] = tied[1 + images + i]
    attention_back(0)
    norm_back(1)
    st[1]["do"], st[0]["mid"] = tie(st[1]["do"], st[0]["mid"])
    st[0]["far"] = far(st[0]["mid"])
    attention_back(1)
    norm_back(2)
    st[2]["do"], st[0]["far"] = tie(st[2]["do"], st[0]["far"])
    st[1]["far"] = far(st[1]["mid"])
    qkv_back(0)
    attention_back(2)
    st[2]["far"] = far(st[2]["mid"])
    qkv_back(1)
    st[2]["far"], st[1]["dkv"], st[0]["outx"], st[0]["dh1x"] = tie(
        st[2]["far"], st[1]["dkv"], st[0]["outx"], st[0]["dh1x"]
    )
    qkv_back(2)
    for i in range(images):
        mixed = mixed_part(i, mixed)
    for i in range(images):
        grad_tokens = tokens_part(i, grad_tokens)
    own_ffn = lax.psum_scatter(grads_ffn, both, scatter_dimension=0, tiled=True)

    def around(own):
        beyond = far(own)
        held = [own, near(own), beyond, near(beyond)]
        return jnp.concatenate([lax.select_n(ctx ^ at, *held) for at in range(4)], axis=0)

    send, keep = weight_grads(
        [(False, of("h1"), [of("dq"), of("dkv")]), (False, of("dab"), [[attn_in]])], "grads_qkv", split=(shards, part)
    )
    grads_qkv = (keep.astype(F32) + near(send).astype(F32)).astype(BF)
    grads_qkv, own_ffn = tie(grads_qkv, own_ffn)
    own_qkv = lax.psum_scatter(grads_qkv, ("shard", "far"), scatter_dimension=0, tiled=True)
    grad_pairs, grad_down = call(
        finish_kernel,
        (shape(ff, 2, depth, dtype=F32), shape(ff, depth, dtype=F32)),
        [whole(depth, 3 * ffp)],
        [whole(ff, 2, depth), whole(ff, depth)],
        name="finish",
        mib=20,
        moved=18 * ff * depth,
    )(around(own_ffn))

    def everywhere(value):
        value = value + near(value)
        value = value + far(value)
        step = 1
        while step < shards:
            value = value + lax.ppermute(value, "shard", pair_perm(shards, step))
            step *= 2
        return value

    def gain(name):
        return sum(s[name] for s in st)[0]

    packed = everywhere(jnp.concatenate([gain("dffn"), gain("dln2"), gain("dattn")]))
    gain_ffn = packed[:ff]
    gain_ln2 = packed[ffp : ffp + width]
    gain_attn = packed[ffp + width :]
    gain_ln1 = everywhere(gain("dln1"))
    own_qkv, grad_tokens, mixed, gain_ln1, gain_ffn, grad_pairs, grad_down = tie(
        own_qkv, grad_tokens, mixed, gain_ln1, gain_ffn, grad_pairs, grad_down
    )
    grad_pairs = jnp.transpose(grad_pairs, (1, 2, 0))
    sum_qkv = lax.all_gather(own_qkv[:, : 3 * half], pairs_of, axis=0, tiled=True).astype(F32)
    grad_proj = around(own_qkv[:, 3 * half :]).astype(F32).T
    grad_qkv = jnp.stack([sum_qkv[:, j * half : (j + 1) * half] for j in range(3)])

    return (
        mixed,
        grad_tokens,
        gain_ln1,
        grad_qkv,
        gain_attn,
        grad_proj,
        gain_ln2,
        grad_pairs,
        gain_ffn,
        grad_down,
    )


def solution(mesh):
    size = dict(mesh.shape)
    mesh = Mesh(
        mesh.devices.reshape(size["shard"], size["ctx"] // 2, 2, size["tp"]), ("shard", "far", "near", "tp")
    )
    tokens = P("shard", ("far", "near"), None)
    matrix = P(None, "shard", "tp")
    flipped = P("tp", "shard")
    return jax.shard_map(
        local,
        mesh=mesh,
        in_specs=(
            tokens, tokens, P("shard"), P(), matrix, P("tp"), flipped, P(), matrix, P("tp"), flipped,
        ),
        out_specs=(tokens, tokens, P(), matrix, P("tp"), flipped, P(), matrix, P("tp"), flipped),
        check_vma=False,
    )
```
